256 devices in a mesh: ha: 8 (over x, core), wa: 32 (over z, y).
Axes of the slice: x: 4, y: 4, z: 8, core: 2. Of those that a mesh axis runs over, the one named last changes fastest.
Arguments:
- features: bfloat16 [2, 64, 512, 320], P(None, 'ha', 'wa'), may hold values from -30 to 30
- target: bfloat16 [2, 64, 512, 320], P(None, 'ha', 'wa'), may hold values from -6 to 6
- norm1_gain: float32 [320], replicated, may hold values from 0.1 to 1.9
- norm1_shift: float32 [320], replicated, may hold values from -2 to 2
- kernel1: bfloat16 [3, 3, 320, 320], replicated, may hold values from -0.109375 to 0.109375
- bias1: float32 [320], replicated, may hold values from -2 to 2
- time_weight: bfloat16 [1280, 320], replicated, may hold values from -0.3125 to 0.3125
- time_bias: float32 [320], replicated, may hold values from -2 to 2
- norm2_gain: float32 [320], replicated, may hold values from 0.1 to 1.9
- norm2_shift: float32 [320], replicated, may hold values from -2 to 2
- kernel2: bfloat16 [3, 3, 320, 320], replicated, may hold values from -0.109375 to 0.109375
- bias2: float32 [320], replicated, may hold values from -2 to 2
- ref_error: float32 [1, 2], replicated, may hold values from 2 to 6
- preference: int32 [1], replicated, may hold values from 0 to 1
- timestep: int32 [1], replicated, may hold values from 0 to 999
Outputs:
- block_out: bfloat16 [2, 64, 512, 320], P(None, 'ha', 'wa')
- feature_grad: bfloat16 [2, 64, 512, 320], P(None, 'ha', 'wa')
- kernel1_grad: float32 [3, 3, 320, 320], P(None, None, None, 'wa')
- kernel2_grad: float32 [3, 3, 320, 320], P(None, None, None, 'wa')
- loss: float32 [], replicated
The draws below stay inside these ranges and needn't reach their ends.
All inputs are finite; a program needn't handle non-finite values.
Results may differ from the reference program's by a relative error of at most 0.015.
Values may be sent and summed in bfloat16 or wider, within the bound.
No kernel may reach another device: no remote copies, remote signals or barrier semaphores. Data moves between devices by JAX's collectives and lax.ppermute only.
A program may use at most 128 MiB of HBM per device.

```python
import jax
import jax.numpy as jnp
from jax import lax

C = 320
GROUPS = 32
TEMB = 1280
P_SIZE = 1
B = 2
HH = 64
WW = 512


def draw_features(key, part):
    key = jax.random.fold_in(key, 11)
    first = jax.random.fold_in(key, 0)
    rows = jnp.arange(HH, dtype=jnp.float32) / max(HH - 1, 1)
    cols = jnp.arange(WW, dtype=jnp.float32) / max(WW - 1, 1)
    scale = 0.4 * jnp.power(10.0, 0.5 * (rows[:, None] + cols[None, :]))
    base = jax.random.truncated_normal(first, -6.0, 6.0, (B, HH, WW, C), jnp.float32)
    return (base * scale[None, :, :, None]).astype(jnp.bfloat16)


def block_levels(key, extent, cuts, least, largest):
    level, own = 1.0, jax.random.fold_in(key, 6)
    for axis_at, shards_of in cuts:
        draws = jnp.exp(jax.random.uniform(jax.random.fold_in(own, axis_at), (shards_of,), jnp.float32, least / len(cuts), largest / len(cuts)))
        level = level * jnp.repeat(draws, extent[axis_at] // shards_of).reshape([-1 if axis == axis_at else 1 for axis in range(len(extent))])
    return level


def bell_draw(own_key, dims, width, reach, pieces=(), held_as=jnp.bfloat16):
    level = block_levels(own_key, dims, pieces, -0.22, 0.18) if pieces else 1.0
    drawn = jax.random.normal(own_key, dims, jnp.float32) * width * level
    return jnp.minimum(jnp.maximum(drawn, -reach), reach).astype(held_as)


def setup_inputs(seed: int = 0) -> dict:
    streams_of = jax.random.split(jax.random.key(seed), 16)
    return {
        "features": draw_features(jax.random.fold_in(streams_of[15], 71), 0),
        "target": bell_draw(streams_of[1], (B, HH, WW, C), 1.0, 6.0, ((1, 8), (2, 32))),
        "norm1_gain": jnp.clip(1.0 + 0.18 * jax.random.normal(streams_of[2], (C,), jnp.float32), 0.1, 1.9),
        "norm1_shift": bell_draw(streams_of[3], (C,), 0.4, 2.0, (), jnp.float32),
        "kernel1": bell_draw(streams_of[4], (3, 3, C, C), (9 * C) ** -0.5, 0.109375),
        "bias1": bell_draw(streams_of[5], (C,), 0.4, 2.0, (), jnp.float32),
        "time_weight": bell_draw(streams_of[6], (TEMB, C), (TEMB // 4) ** -0.5, 0.3125),
        "time_bias": bell_draw(streams_of[7], (C,), 0.4, 2.0, (), jnp.float32),
        "norm2_gain": jnp.clip(1.0 + 0.18 * jax.random.normal(streams_of[8], (C,), jnp.float32), 0.1, 1.9),
        "norm2_shift": bell_draw(streams_of[9], (C,), 0.4, 2.0, (), jnp.float32),
        "kernel2": bell_draw(streams_of[10], (3, 3, C, C), (9 * C) ** -0.5, 0.109375),
        "bias2": bell_draw(streams_of[11], (C,), 0.4, 2.0, (), jnp.float32),
        "ref_error": jnp.clip(jax.random.uniform(streams_of[12], (P_SIZE, 2), jnp.float32, 2.0, 6.0), 2.0, 6.0),
        "preference": jax.random.randint(streams_of[13], (P_SIZE,), 0, 2).astype(jnp.int32),
        "timestep": jax.random.randint(streams_of[14], (P_SIZE,), 0, 1000).astype(jnp.int32),
    }


def pad_band(a):
    return jnp.pad(a.astype(jnp.float32), ((0, 0), (1, 1), (1, 1), (0, 0)))

def convolve(padded, kernel):
    rows = padded.shape[1] - 2
    cols = padded.shape[2] - 2
    kern = kernel.astype(jnp.float32)
    total = jnp.zeros(padded.shape[:1] + (rows, cols, kern.shape[3]), jnp.float32)
    for ky in range(3):
        for kx in range(3):
            total = total + jnp.einsum('bhwi,io->bhwo', padded[:, ky:ky + rows, kx:kx + cols], kern[ky, kx], precision=lax.Precision.HIGHEST)
    return total

def convolve_back(padded, kernel):
    rows = padded.shape[1] - 2
    cols = padded.shape[2] - 2
    kern = kernel.astype(jnp.float32)
    total = jnp.zeros(padded.shape[:1] + (rows, cols, kern.shape[2]), jnp.float32)
    for ky in range(3):
        for kx in range(3):
            total = total + jnp.einsum('bhwo,io->bhwi', padded[:, 2 - ky:2 - ky + rows, 2 - kx:2 - kx + cols], kern[ky, kx], precision=lax.Precision.HIGHEST)
    return total

def kernel_sum(padded, grads):
    rows = grads.shape[1]
    cols = grads.shape[2]
    gfl = grads.astype(jnp.float32)
    blocks = []
    for ky in range(3):
        line = []
        for kx in range(3):
            line.append(jnp.einsum('bhwi,bhwo->io', padded[:, ky:ky + rows, kx:kx + cols], gfl, precision=lax.Precision.HIGHEST))
        blocks.append(jnp.stack(line))
    return jnp.stack(blocks)

def group_norm(values, gain, shift):
    nb, rows, cols, chans = values.shape
    grouped = values.reshape(nb, rows, cols, GROUPS, chans // GROUPS)
    mean = lax.optimization_barrier(jnp.mean(grouped, axis=(1, 2, 4), keepdims=True))
    var = lax.optimization_barrier(jnp.mean((grouped - mean) ** 2, axis=(1, 2, 4), keepdims=True))
    rstd = 1.0 / jnp.sqrt(var + 1e-05)
    nhat = ((grouped - mean) * rstd).reshape(values.shape)
    return (nhat * gain + shift, nhat, rstd)

def group_back(grad, nhat, rstd, gain):
    nb, rows, cols, chans = grad.shape
    scaled = (grad * gain).reshape(nb, rows, cols, GROUPS, chans // GROUPS)
    normed = nhat.reshape(scaled.shape)
    first = lax.optimization_barrier(jnp.mean(scaled, axis=(1, 2, 4), keepdims=True))
    second = lax.optimization_barrier(jnp.mean(scaled * normed, axis=(1, 2, 4), keepdims=True))
    return (rstd * (scaled - first - normed * second)).reshape(grad.shape)

def silu_slope(v):
    sig = jax.nn.sigmoid(v)
    return sig * (1.0 + v * (1.0 - sig))

def time_embed(timestep, time_weight, time_bias):
    half = TEMB // 2
    freqs = jnp.exp(-jnp.log(10000.0) * jnp.arange(half, dtype=jnp.float32) / half)
    angles = timestep.astype(jnp.float32)[:, None] * freqs[None, :]
    emb = jnp.concatenate([jnp.cos(angles), jnp.sin(angles)], axis=1)
    proj = jnp.dot(jax.nn.silu(emb), time_weight.astype(jnp.float32), precision=lax.Precision.HIGHEST) + time_bias
    return jnp.repeat(proj, 2, axis=0)

def reference(features, target, norm1_gain, norm1_shift, kernel1, bias1, time_weight, time_bias, norm2_gain, norm2_shift, kernel2, bias2, ref_error, preference, timestep):
    inputs = features.astype(jnp.float32)
    temb = time_embed(timestep, time_weight, time_bias)
    n1, nhat1, rstd1 = group_norm(inputs, norm1_gain, norm1_shift)
    a1 = jax.nn.silu(n1).astype(jnp.bfloat16)
    pad1 = pad_band(a1)
    h1 = convolve(pad1, kernel1) + bias1 + temb[:, None, None, :]
    n2, nhat2, rstd2 = group_norm(h1, norm2_gain, norm2_shift)
    a2 = jax.nn.silu(n2).astype(jnp.bfloat16)
    pad2 = pad_band(a2)
    out = inputs + convolve(pad2, kernel2) + bias2
    block_out = out.astype(jnp.bfloat16)
    diff = out - target.astype(jnp.float32)
    err = lax.optimization_barrier(jnp.sum(diff * diff, axis=(1, 2, 3))) / (HH * WW * C)
    pairs = err.reshape(P_SIZE, 2)
    chosen = preference == 0
    gap = jnp.where(chosen, pairs[:, 0], pairs[:, 1]) - jnp.where(chosen, ref_error[:, 0], ref_error[:, 1]) - (jnp.where(chosen, pairs[:, 1], pairs[:, 0]) - jnp.where(chosen, ref_error[:, 1], ref_error[:, 0]))
    loss = jnp.mean(jax.nn.softplus(gap))
    weight = jax.nn.sigmoid(gap) / P_SIZE
    signs = jnp.where(jnp.arange(2)[None, :] == preference[:, None], 1.0, -1.0).astype(jnp.float32)
    coef = (weight[:, None] * signs).reshape(B)
    g_out = (2.0 * coef[:, None, None, None] * diff).astype(jnp.bfloat16)
    scale = 1.0 / jnp.sqrt(jnp.float32(B * HH * WW))
    grad2 = kernel_sum(pad2, g_out) * scale
    da2 = convolve_back(pad_band(g_out), kernel2)
    dh1 = group_back(da2 * silu_slope(n2), nhat2, rstd2, norm2_gain).astype(jnp.bfloat16)
    grad1 = kernel_sum(pad1, dh1) * scale
    da1 = convolve_back(pad_band(dh1), kernel1)
    dx = group_back(da1 * silu_slope(n1), nhat1, rstd1, norm1_gain)
    feature_grad = (g_out.astype(jnp.float32) + dx).astype(jnp.bfloat16)
    return (block_out, feature_grad, grad1, grad2, loss)
```

```python
import functools

import jax
import jax.numpy as jnp
import numpy as np
from jax import lax
from jax.experimental import pallas as pl
from jax.experimental.pallas import tpu as pltpu
from jax.sharding import Mesh
from jax.sharding import PartitionSpec as P

GROUPS = 32
TEMB = 1280
C = 320
WIDTH = C // GROUPS
ROWS, COLS = 8, 16
BAND_ROWS, BAND_COLS = 64, 512
RIM = 4
GH, GW = ROWS + 2 * RIM, COLS + 2 * RIM
LINE = 2 * GW
DEVICES = 256
LOCAL = ROWS * COLS * WIDTH
TOTAL = LOCAL * DEVICES
TAPS = 9 * C
LANES = 3072
EPS = 1e-05
F32, BF16 = jnp.float32, jnp.bfloat16
HIGH = lax.Precision.HIGHEST


def dot(a, b):
    return jnp.dot(a, b, preferred_element_type=F32)


def group_to_lanes(rows, slot):
    chan = lax.broadcasted_iota(jnp.int32, (C, 128), 0)
    low = (lax.broadcasted_iota(jnp.int32, (C, 128), 1) - slot * GROUPS) * WIDTH
    hot = ((chan >= low) & (chan < low + WIDTH)).astype(F32)
    return jnp.dot(rows, hot, precision=HIGH, preferred_element_type=F32)


def lanes_to_chans(row, slot):
    low = (lax.broadcasted_iota(jnp.int32, (128, C), 0) - slot * GROUPS) * WIDTH
    chan = lax.broadcasted_iota(jnp.int32, (128, C), 1)
    hot = ((chan >= low) & (chan < low + WIDTH)).astype(F32)
    return jnp.dot(row, hot, precision=HIGH, preferred_element_type=F32)


def per_line(first, second):
    return jnp.concatenate(
        [jnp.broadcast_to(first, (GW, C)), jnp.broadcast_to(second, (GW, C))], axis=0
    )


def tile_lines(line, count):
    return jnp.broadcast_to(line[None], (count, LINE, C)).reshape(count * LINE, C)


def grid_masks(pos_ref, top, count):
    shape = (count, LINE, C)
    y = lax.broadcasted_iota(jnp.int32, shape, 0) + top
    col = lax.broadcasted_iota(jnp.int32, shape, 1)
    x = jnp.where(col >= GW, col - GW, col)
    gy = y + (pos_ref[0] * ROWS - RIM)
    gx = x + (pos_ref[1] * COLS - RIM)
    band = (gy >= 0) & (gy < BAND_ROWS) & (gx >= 0) & (gx < BAND_COLS)
    return band.reshape(count * LINE, C)


def center_masks():
    shape = (ROWS, LINE, C)
    col = lax.broadcasted_iota(jnp.int32, shape, 1)
    one = (col >= RIM) & (col < RIM + COLS)
    two = (col >= GW + RIM) & (col < GW + RIM + COLS)
    return one.reshape(ROWS * LINE, C), two.reshape(ROWS * LINE, C)


def norm_lines(stats_ref):
    stats = stats_ref[...]
    sums = jnp.sum(stats, axis=0, keepdims=True)
    mean = sums * (1.0 / DEVICES)
    off = stats - mean
    spread = jnp.sum(off * off, axis=0, keepdims=True)
    means, rstds = [], []
    for b in range(2):
        means.append(lanes_to_chans(mean, b))
        var = (lanes_to_chans(sums, 2 + b) + LOCAL * lanes_to_chans(spread, b)) * (1.0 / TOTAL)
        rstds.append(1.0 / jnp.sqrt(var + EPS))
    return per_line(*means), per_line(*rstds)


def moments(values, masks):
    out = jnp.zeros((1, 128), F32)
    for b in range(2):
        kept = jnp.where(masks[b], values, 0.0)
        total = jnp.sum(kept, axis=0, keepdims=True)
        mean = group_to_lanes(total, b) * (1.0 / LOCAL)
        out = out + mean
        off = jnp.where(masks[b], values - lanes_to_chans(mean, b), 0.0)
        out = out + group_to_lanes(jnp.sum(off * off, axis=0, keepdims=True), 2 + b)
    return out


def pair_sums(scaled, normed, masks):
    out = jnp.zeros((1, 128), F32)
    prod = scaled * normed
    for b in range(2):
        first = jnp.sum(jnp.where(masks[b], scaled, 0.0), axis=0, keepdims=True)
        second = jnp.sum(jnp.where(masks[b], prod, 0.0), axis=0, keepdims=True)
        out = out + group_to_lanes(first, b) + group_to_lanes(second, 2 + b)
    return out


def sigmoid(v):
    return 0.5 + 0.5 * jnp.tanh(0.5 * v)


def silu_slope(v):
    sig = sigmoid(v)
    return sig * (1.0 + v * (1.0 - sig))


def spread_taps(ref, values):
    count = values.shape[0]
    ref[:, 0:C] = pltpu.roll(values, 1, 0).astype(BF16)
    ref[:, C : 2 * C] = values.astype(BF16)
    ref[:, 2 * C : 3 * C] = pltpu.roll(values, count - 1, 0).astype(BF16)


def conv_lines(ref, weights_ref, count):
    total = dot(ref[0 : count * LINE, :], weights_ref[0])
    for ky in range(1, 3):
        total = total + dot(ref[ky * LINE : (ky + count) * LINE, :], weights_ref[ky])
    return total


def kernel_grad(out_ref, taps_ref, top, grads, order_ref):
    ordered = dot(grads, order_ref[...])
    left = ordered.T.astype(BF16)
    parts = []
    for ky in range(3):
        lines = taps_ref[(top + ky) * LINE : (top + ky + ROWS) * LINE, :]
        parts.append(dot(left, lines).astype(BF16))
    parts.append(jnp.zeros((C, LANES - TAPS), BF16))
    whole = jnp.concatenate(parts, axis=1)
    out_ref[0] = whole[:, : LANES // 2]
    out_ref[1] = whole[:, LANES // 2 :]


def moments_kernel(x_ref, out_ref):
    out = jnp.zeros((1, 128), F32)
    half = ROWS * COLS
    for b in range(2):
        v = x_ref[b * half : (b + 1) * half, :].astype(F32)
        mean = group_to_lanes(jnp.sum(v, axis=0, keepdims=True), b) * (1.0 / LOCAL)
        off = v - lanes_to_chans(mean, b)
        out = out + mean + group_to_lanes(jnp.sum(off * off, axis=0, keepdims=True), 2 + b)
    out_ref[...] = out


def first_kernel(pos_ref, x_ref, stats_ref, gain_ref, shift_ref, w_ref, add_ref, h_ref, taps_ref, out_ref, scr):
    mean, rstd = norm_lines(stats_ref)
    scale = tile_lines(rstd * gain_ref[...], GH)
    n1 = (x_ref[...].astype(F32) - tile_lines(mean, GH)) * scale + shift_ref[...]
    a1 = jnp.where(grid_masks(pos_ref, 0, GH), n1 * sigmoid(n1), 0.0)
    spread_taps(scr, a1)
    taps_ref[...] = scr[3 * LINE : 13 * LINE, :]
    h1 = conv_lines(scr, w_ref, GH - 2) + add_ref[...]
    h_ref[...] = h1
    out_ref[...] = moments(h1[3 * LINE : 11 * LINE], center_masks())


def second_kernel(
    pos_ref, h_ref, stats_ref, gain_ref, shift_ref, w_ref, wt_ref, bias_ref, x_ref, t_ref, sign_ref, order_ref,
    bout_ref, u_ref, e_ref, grad_ref, out_ref, err_ref, scr_a, scr_u,
):
    mean, rstd = norm_lines(stats_ref)
    nhat = (h_ref[...] - tile_lines(mean, GH - 2)) * tile_lines(rstd, GH - 2)
    n2 = nhat * gain_ref[...] + shift_ref[...]
    a2 = jnp.where(grid_masks(pos_ref, 1, GH - 2), n2 * sigmoid(n2), 0.0)
    spread_taps(scr_a, a2)
    out = x_ref[2 * LINE : 14 * LINE, :].astype(F32) + conv_lines(scr_a, w_ref, 12) + bias_ref[...]
    bout_ref[...] = out[2 * LINE : 10 * LINE].astype(BF16)
    diff = out - t_ref[...].astype(F32)
    masks = center_masks()
    mid = diff[2 * LINE : 10 * LINE]
    square = mid * mid
    lane = lax.broadcasted_iota(jnp.int32, (1, 128), 1)
    errs = jnp.zeros((1, 128), F32)
    for b in range(2):
        part = jnp.sum(jnp.where(masks[b], square, 0.0), axis=0, keepdims=True)
        errs = errs + jnp.where(lane == b, jnp.sum(part, axis=1, keepdims=True), 0.0)
    err_ref[...] = errs
    sign = tile_lines(per_line(sign_ref[0:1, :], sign_ref[1:2, :]), 12)
    u = jnp.where(grid_masks(pos_ref, 2, 12), diff * sign, 0.0)
    spread_taps(scr_u, u)
    center = u[2 * LINE : 10 * LINE]
    u_ref[...] = center.astype(BF16)
    kept = jnp.where(masks[0] | masks[1], center, 0.0).astype(BF16)
    kernel_grad(grad_ref, scr_a, 2, kept, order_ref)
    da2 = conv_lines(scr_u, wt_ref, 10)
    e = da2 * silu_slope(n2[2 * LINE : 12 * LINE]) * gain_ref[...]
    e_ref[...] = e
    out_ref[...] = pair_sums(e[LINE : 9 * LINE], nhat[3 * LINE : 11 * LINE], masks)


def back_line(sums_ref):
    sums = jnp.sum(sums_ref[...], axis=0, keepdims=True) * (1.0 / TOTAL)
    first = per_line(lanes_to_chans(sums, 0), lanes_to_chans(sums, 1))
    second = per_line(lanes_to_chans(sums, 2), lanes_to_chans(sums, 3))
    return first, second


def third_kernel(pos_ref, e_ref, h_ref, stats_ref, sums_ref, taps_ref, order_ref, d_ref, grad_ref):
    mean, rstd = norm_lines(stats_ref)
    first, second = back_line(sums_ref)
    scale = tile_lines(rstd, 10)
    nhat = (h_ref[2 * LINE : 12 * LINE, :] - tile_lines(mean, 10)) * scale
    dh = scale * (e_ref[...] - tile_lines(first, 10) - nhat * tile_lines(second, 10))
    dh = jnp.where(grid_masks(pos_ref, 3, 10), dh, 0.0)
    d_ref[...] = dh.astype(BF16)
    masks = center_masks()
    kept = jnp.where(masks[0] | masks[1], dh[LINE : 9 * LINE], 0.0).astype(BF16)
    kernel_grad(grad_ref, taps_ref, 0, kept, order_ref)


def fourth_kernel(d_ref, x_ref, stats_ref, gain_ref, shift_ref, wt_ref, e_ref, out_ref, scr):
    spread_taps(scr, d_ref[...].astype(F32))
    da1 = conv_lines(scr, wt_ref, ROWS)
    mean, rstd = norm_lines(stats_ref)
    nhat = (x_ref[4 * LINE : 12 * LINE, :].astype(F32) - tile_lines(mean, ROWS)) * tile_lines(rstd, ROWS)
    n1 = nhat * gain_ref[...] + shift_ref[...]
    e1 = da1 * silu_slope(n1) * gain_ref[...]
    e_ref[...] = e1
    out_ref[...] = pair_sums(e1, nhat, center_masks())


def last_kernel(e_ref, x_ref, stats_ref, sums_ref, u_ref, weight_ref, out_ref):
    mean, rstd = norm_lines(stats_ref)
    first, second = back_line(sums_ref)
    scale = tile_lines(rstd, ROWS)
    nhat = (x_ref[4 * LINE : 12 * LINE, :].astype(F32) - tile_lines(mean, ROWS)) * scale
    dx = scale * (e_ref[...] - tile_lines(first, ROWS) - nhat * tile_lines(second, ROWS))
    out_ref[...] = ((u_ref[...].astype(F32) + dx) * weight_ref[...]).astype(BF16)


def core_sum_kernel(a_ref, out_ref):
    for i in range(4):
        for j in range(4):
            rows, lanes = slice(j * 80, (j + 1) * 80), slice(i * 384, (i + 1) * 384)
            out_ref[i * 4 + j] = (a_ref[0, rows, lanes].astype(F32) + a_ref[1, rows, lanes].astype(F32)).astype(BF16)


VM = pl.BlockSpec(memory_space=pltpu.VMEM)
SM = pl.BlockSpec(memory_space=pltpu.SMEM)


def call(kernel, shapes, args, scratch=(), scalars=0, flops=0):
    size = sum(int(np.prod(s.shape)) * s.dtype.itemsize for s in shapes) + sum(a.size * a.dtype.itemsize for a in args)
    many = len(shapes) > 1
    return pl.pallas_call(
        kernel,
        out_shape=tuple(shapes) if many else shapes[0],
        in_specs=[SM] * scalars + [VM] * (len(args) - scalars),
        out_specs=tuple([VM] * len(shapes)) if many else VM,
        scratch_shapes=list(scratch),
        compiler_params=pltpu.CompilerParams(vmem_limit_bytes=40 * 2**20),
        cost_estimate=pl.CostEstimate(flops=flops, bytes_accessed=size, transcendentals=0),
    )(*args)


def sds(shape, dtype=F32):
    return jax.ShapeDtypeStruct(shape, dtype)


AXES = ("x", "c", "z", "y")


def share(row):
    flat = row.reshape(128)
    return lax.all_to_all(jnp.broadcast_to(flat[None], (DEVICES, 128)), AXES, 0, 0, tiled=True)


def widen(features, target):
    up = [(i, i + 1) for i in range(7)]
    down = [(i + 1, i) for i in range(7)]
    low = jnp.concatenate([features[:, ROWS - 4 :], target[:, ROWS - 2 :]], axis=1)
    high = jnp.concatenate([features[:, :4], target[:, :2]], axis=1)
    low = lax.ppermute(low, ("x", "c"), up)
    high = lax.ppermute(high, ("x", "c"), down)
    f = jnp.concatenate([low[:, :4], features, high[:, :4]], axis=1)
    t = jnp.concatenate([low[:, 4:], target, high[:, 4:]], axis=1)
    right = [(i, i + 1) for i in range(31)]
    left = [(i + 1, i) for i in range(31)]

    def pack(a, b):
        return jnp.concatenate([a.reshape(2, GH * 4, C), b.reshape(2, 12 * 4, C)], axis=1)

    first = lax.ppermute(pack(f[:, :, COLS - 4 :], t[:, :, COLS - 4 :]), ("z", "y"), right)
    last = lax.ppermute(pack(f[:, :, :4], t[:, :, :4]), ("z", "y"), left)

    def unpack(v):
        return v[:, : GH * 4].reshape(2, GH, 4, C), v[:, GH * 4 :].reshape(2, 12, 4, C)

    fl, tl = unpack(first)
    fr, tr = unpack(last)
    f = jnp.concatenate([fl, f, fr], axis=2).transpose(1, 0, 2, 3).reshape(GH * LINE, C)
    t = jnp.concatenate([tl, t, tr], axis=2).transpose(1, 0, 2, 3).reshape(12 * LINE, C)
    return f, t


def center(values):
    return values.reshape(ROWS, 2, GW, C)[:, :, RIM : RIM + COLS].transpose(1, 0, 2, 3)


def turned(kernel):
    return kernel[::-1, ::-1].transpose(0, 1, 3, 2).reshape(3, 3 * C, C)


def time_embed(timestep, time_weight, time_bias):
    half = TEMB // 2
    freqs = jnp.exp(-jnp.log(10000.0) * jnp.arange(half, dtype=F32) / half)
    angles = timestep.astype(F32)[:, None] * freqs[None, :]
    emb = jnp.concatenate([jnp.cos(angles), jnp.sin(angles)], axis=1)
    return jnp.dot(jax.nn.silu(emb), time_weight.astype(F32), precision=HIGH) + time_bias


def order_matrix():
    out = np.zeros((C, C), np.float32)
    for z in range(8):
        for y in range(4):
            for j in range(10):
                out[z * 40 + y * 10 + j, y * 80 + z * 10 + j] = 1.0
    return jnp.asarray(out, BF16)


def core_swap(partial):
    both = lax.all_to_all(partial, ("c",), 0, 0, tiled=True)
    return call(core_sum_kernel, [sds((16, 80, 384), BF16)], [both])


def body(
    features, target, norm1_gain, norm1_shift, kernel1, bias1, time_weight, time_bias,
    norm2_gain, norm2_shift, kernel2, bias2, ref_error, preference, timestep,
):
    h = lax.axis_index("x") * 2 + lax.axis_index("c")
    w = lax.axis_index("z") * 4 + lax.axis_index("y")
    pos = jnp.stack([h, w]).astype(jnp.int32)
    gain1, shift1 = norm1_gain.reshape(1, C), norm1_shift.reshape(1, C)
    gain2, shift2 = norm2_gain.reshape(1, C), norm2_shift.reshape(1, C)
    stats1 = share(call(moments_kernel, [sds((1, 128))], [features.reshape(2 * ROWS * COLS, C)]))
    fx, tx = widen(features, target)
    add1 = bias1.reshape(1, C) + time_embed(timestep, time_weight, time_bias)
    order = order_matrix()
    signs = jnp.where(jnp.arange(2) == preference[0], 2.0, -2.0).astype(F32)
    sign_rows = jnp.broadcast_to(signs[:, None], (2, C))
    w1, w2 = kernel1.reshape(3, 3 * C, C), kernel2.reshape(3, 3 * C, C)
    w1t, w2t = turned(kernel1), turned(kernel2)
    conv_flops = 2 * 9 * C * C * LINE
    h1, taps1, part = call(
        first_kernel,
        [sds((14 * LINE, C)), sds((10 * LINE, 3 * C), BF16), sds((1, 128))],
        [pos, fx, stats1, gain1, shift1, w1, add1],
        [pltpu.VMEM((GH * LINE, 3 * C), BF16)],
        1,
        14 * conv_flops,
    )
    stats2 = share(part)
    bout, u, e2, grad2, part, errs = call(
        second_kernel,
        [
            sds((ROWS * LINE, C), BF16), sds((ROWS * LINE, C), BF16), sds((10 * LINE, C)),
            sds((2, C, LANES // 2), BF16), sds((1, 128)), sds((1, 128)),
        ],
        [pos, h1, stats2, gain2, shift2, w2, w2t, bias2.reshape(1, C), fx, tx, sign_rows, order],
        [pltpu.VMEM((14 * LINE, 3 * C), BF16), pltpu.VMEM((12 * LINE, 3 * C), BF16)],
        1,
        30 * conv_flops,
    )
    sums2 = share(part)
    block_out = center(bout)
    half2 = core_swap(grad2)
    d1, grad1 = call(
        third_kernel,
        [sds((10 * LINE, C), BF16), sds((2, C, LANES // 2), BF16)],
        [pos, e2, h1, stats2, sums2, taps1, order],
        (),
        1,
        8 * conv_flops,
    )
    half1 = core_swap(grad1)
    plane = lax.all_to_all(jnp.concatenate([half2, half1], axis=1), ("x", "y"), 0, 0, tiled=True)
    e1, part = call(
        fourth_kernel,
        [sds((ROWS * LINE, C)), sds((1, 128))],
        [d1, fx, stats1, gain1, shift1, w1t],
        [pltpu.VMEM((10 * LINE, 3 * C), BF16)],
        0,
        8 * conv_flops,
    )
    tail = jnp.concatenate([part, errs], axis=1).reshape(256)
    tail = lax.all_to_all(jnp.broadcast_to(tail[None], (DEVICES, 256)), AXES, 0, 0, tiled=True)
    sums1, errs = tail[:, :128], tail[:, 128:]
    err = jnp.sum(errs, axis=0)[:2] / (BAND_ROWS * BAND_COLS * C)
    excess = err - ref_error[0]
    gap = jnp.where(preference[0] == 0, excess[0] - excess[1], excess[1] - excess[0])
    loss = jax.nn.softplus(gap)
    weight = jax.nn.sigmoid(gap)
    grad = call(
        last_kernel,
        [sds((ROWS * LINE, C), BF16)],
        [e1, fx, stats1, sums1, u, jnp.broadcast_to(weight, (1, C))],
    )
    feature_grad = center(grad)
    depth = jnp.sum(plane.astype(F32), axis=0).astype(BF16)
    depth = depth.reshape(2, 8, 10, 384).transpose(1, 0, 2, 3).reshape(8, 20, 384)
    depth = lax.all_to_all(depth, ("z",), 0, 0, tiled=True)
    mine = jnp.sum(depth.astype(F32), axis=0)
    whole = lax.all_gather(mine, ("x", "c"), axis=0, tiled=False)
    whole = whole.reshape(4, 2, 2, 10, 384).transpose(2, 3, 1, 0, 4).reshape(2, 10, LANES)[:, :, :TAPS]
    scale = weight / jnp.sqrt(F32(2 * BAND_ROWS * BAND_COLS))
    whole = (whole * scale).reshape(2, 10, 3, 3, C).transpose(0, 2, 3, 4, 1)
    return (block_out, feature_grad, whole[1], whole[0], loss)


def solution(mesh):
    fine = Mesh(mesh.devices.reshape(4, 2, 8, 4), AXES)
    cells = P(None, ("x", "c"), ("z", "y"), None)
    kernels = P(None, None, None, ("z", "y"))
    return jax.shard_map(
        body,
        mesh=fine,
        in_specs=(cells, cells) + (P(),) * 13,
        out_specs=(cells, cells, kernels, kernels, P()),
        check_vma=False,
    )
```

```python
import functools

import jax
import jax.numpy as jnp
import numpy as np
from jax import lax
from jax.experimental import pallas as pl
from jax.experimental.pallas import tpu as pltpu
from jax.sharding import Mesh
from jax.sharding import PartitionSpec as P

GROUPS = 32
TEMB = 1280
C = 320
WIDTH = C // GROUPS
ROWS, COLS = 8, 16
BAND_ROWS, BAND_COLS = 64, 512
RIM = 4
GH, GW = ROWS + 2 * RIM, COLS + 2 * RIM
LINE = 2 * GW
DEVICES = 256
LOCAL = ROWS * COLS * WIDTH
TOTAL = LOCAL * DEVICES
TAPS = 9 * C
LANES = 3072
EPS = 1e-05
F32, BF16 = jnp.float32, jnp.bfloat16
HIGH = lax.Precision.HIGHEST


def dot(a, b):
    return jnp.dot(a, b, preferred_element_type=F32)


def group_to_lanes(rows, slot):
    chan = lax.broadcasted_iota(jnp.int32, (C, 128), 0)
    low = (lax.broadcasted_iota(jnp.int32, (C, 128), 1) - slot * GROUPS) * WIDTH
    hot = ((chan >= low) & (chan < low + WIDTH)).astype(F32)
    return jnp.dot(rows, hot, precision=HIGH, preferred_element_type=F32)


def lanes_to_chans(row, slot):
    low = (lax.broadcasted_iota(jnp.int32, (128, C), 0) - slot * GROUPS) * WIDTH
    chan = lax.broadcasted_iota(jnp.int32, (128, C), 1)
    hot = ((chan >= low) & (chan < low + WIDTH)).astype(F32)
    return jnp.dot(row, hot, precision=HIGH, preferred_element_type=F32)


def per_line(first, second):
    return jnp.concatenate(
        [jnp.broadcast_to(first, (GW, C)), jnp.broadcast_to(second, (GW, C))], axis=0
    )


def tile_lines(line, count):
    return jnp.broadcast_to(line[None], (count, LINE, C)).reshape(count * LINE, C)


def grid_masks(pos_ref, top, count):
    shape = (count, LINE, C)
    y = lax.broadcasted_iota(jnp.int32, shape, 0) + top
    col = lax.broadcasted_iota(jnp.int32, shape, 1)
    x = jnp.where(col >= GW, col - GW, col)
    gy = y + (pos_ref[0] * ROWS - RIM)
    gx = x + (pos_ref[1] * COLS - RIM)
    band = (gy >= 0) & (gy < BAND_ROWS) & (gx >= 0) & (gx < BAND_COLS)
    return band.reshape(count * LINE, C)


def center_masks():
    shape = (ROWS, LINE, C)
    col = lax.broadcasted_iota(jnp.int32, shape, 1)
    one = (col >= RIM) & (col < RIM + COLS)
    two = (col >= GW + RIM) & (col < GW + RIM + COLS)
    return one.reshape(ROWS * LINE, C), two.reshape(ROWS * LINE, C)


def norm_lines(stats_ref):
    stats = stats_ref[...]
    count = stats.shape[0]
    sums = jnp.sum(stats, axis=0, keepdims=True)
    mean = sums * (1.0 / count)
    off = stats - mean
    spread = jnp.sum(off * off, axis=0, keepdims=True) * (TOTAL / count)
    means, rstds = [], []
    for b in range(2):
        means.append(lanes_to_chans(mean, b))
        var = (lanes_to_chans(sums, 2 + b) + lanes_to_chans(spread, b)) * (1.0 / TOTAL)
        rstds.append(1.0 / jnp.sqrt(var + EPS))
    return per_line(*means), per_line(*rstds)


def merge_kernel(share_of, stats_ref, out_ref):
    stats = stats_ref[...]
    count = stats.shape[0]
    sums = jnp.sum(stats, axis=0, keepdims=True)
    mean = sums * (1.0 / count)
    off = stats - mean
    spread = jnp.sum(off * off, axis=0, keepdims=True) * share_of
    lane = lax.broadcasted_iota(jnp.int32, (1, 128), 1)
    row = jnp.where(lane < 64, mean, sums + pltpu.roll(spread, 64, 1))
    out_ref[...] = jnp.broadcast_to(row, out_ref.shape)


def moments(values, masks):
    out = jnp.zeros((1, 128), F32)
    for b in range(2):
        kept = jnp.where(masks[b], values, 0.0)
        total = jnp.sum(kept, axis=0, keepdims=True)
        mean = group_to_lanes(total, b) * (1.0 / LOCAL)
        out = out + mean
        off = jnp.where(masks[b], values - lanes_to_chans(mean, b), 0.0)
        out = out + group_to_lanes(jnp.sum(off * off, axis=0, keepdims=True), 2 + b)
    return out


def pair_sums(scaled, normed, masks):
    out = jnp.zeros((1, 128), F32)
    prod = scaled * normed
    for b in range(2):
        first = jnp.sum(jnp.where(masks[b], scaled, 0.0), axis=0, keepdims=True)
        second = jnp.sum(jnp.where(masks[b], prod, 0.0), axis=0, keepdims=True)
        out = out + group_to_lanes(first, b) + group_to_lanes(second, 2 + b)
    return out


def sigmoid(v):
    return 0.5 + 0.5 * jnp.tanh(0.5 * v)


def silu_slope(v):
    sig = sigmoid(v)
    return sig * (1.0 + v * (1.0 - sig))


def spread_taps(ref, values):
    count = values.shape[0]
    ref[:, 0:C] = pltpu.roll(values, 1, 0).astype(BF16)
    ref[:, C : 2 * C] = values.astype(BF16)
    ref[:, 2 * C : 3 * C] = pltpu.roll(values, count - 1, 0).astype(BF16)


def spread_wide(ref, values):
    count = values.shape[0]
    ref[:, 0:C] = pltpu.roll(values, 1, 0).astype(BF16)
    ref[:, 384 : 384 + C] = values.astype(BF16)
    ref[:, 768 : 768 + C] = pltpu.roll(values, count - 1, 0).astype(BF16)


def conv_lines(ref, weights_ref, count):
    total = dot(ref[0 : count * LINE, :], weights_ref[0])
    for ky in range(1, 3):
        total = total + dot(ref[ky * LINE : (ky + count) * LINE, :], weights_ref[ky])
    return total


def conv_turned(ref, weights_ref, count):
    total = None
    for ky in range(3):
        for kx in range(3):
            part = lax.dot_general(
                ref[ky * LINE : (ky + count) * LINE, kx * 384 : kx * 384 + C],
                weights_ref[2 - ky, 2 - kx],
                (((1,), (1,)), ((), ())),
                preferred_element_type=F32,
            )
            total = part if total is None else total + part
    return total


def kernel_grad(mine_ref, theirs_ref, core, taps_ref, top, grads, order_ref):
    ordered = dot(grads, order_ref[...])
    left = ordered.T.astype(BF16)
    parts = []
    for ky in range(3):
        lines = taps_ref[(top + ky) * LINE : (top + ky + ROWS) * LINE, :]
        parts.append(dot(left, lines).astype(BF16))
    parts.append(jnp.zeros((C, LANES - TAPS), BF16))
    whole = jnp.concatenate(parts, axis=1)
    low, high = whole[:, : LANES // 2], whole[:, LANES // 2 :]

    @pl.when(core == 0)
    def _():
        mine_ref[...] = low
        theirs_ref[...] = high

    @pl.when(core == 1)
    def _():
        mine_ref[...] = high
        theirs_ref[...] = low


def fetch(sems, index, src, dst):
    copy = pltpu.make_async_copy(src, dst, sems.at[index])
    copy.start()
    return copy


def moments_kernel(x_ref, out_ref):
    out = jnp.zeros((1, 128), F32)
    half = ROWS * COLS
    for b in range(2):
        v = x_ref[b * half : (b + 1) * half, :].astype(F32)
        mean = group_to_lanes(jnp.sum(v, axis=0, keepdims=True), b) * (1.0 / LOCAL)
        off = v - lanes_to_chans(mean, b)
        out = out + mean + group_to_lanes(jnp.sum(off * off, axis=0, keepdims=True), 2 + b)
    out_ref[...] = out


def first_kernel(
    pos_ref, x_ref, stats_ref, gain_ref, shift_ref, add_ref, w_hbm,
    h_ref, out_ref, taps_hbm, scr, w_ref, sems,
):
    weights = fetch(sems, 0, w_hbm, w_ref)
    mean, rstd = norm_lines(stats_ref)
    scale = tile_lines(rstd * gain_ref[...], GH)
    n1 = (x_ref[...].astype(F32) - tile_lines(mean, GH)) * scale + shift_ref[...]
    a1 = jnp.where(grid_masks(pos_ref, 0, GH), n1 * sigmoid(n1), 0.0)
    spread_taps(scr, a1)
    taps = fetch(sems, 1, scr.at[3 * LINE : 13 * LINE, :], taps_hbm)
    weights.wait()
    h1 = conv_lines(scr, w_ref, GH - 2) + add_ref[...]
    h_ref[...] = h1
    out_ref[...] = moments(h1[3 * LINE : 11 * LINE], center_masks())
    taps.wait()


def second_kernel(
    pos_ref, h_ref, stats_ref, gain_ref, shift_ref, bias_ref, sign_ref, w_hbm, wt_hbm, x_hbm, t_hbm, order_hbm,
    e_ref, out_ref, err_ref, bout_hbm, u_hbm, mine_hbm, theirs_hbm,
    scr_a, scr_u, w_ref, wt_ref, x_ref, t_ref, order_ref, bout_ref, u_ref, mine_ref, theirs_ref, sems,
):
    weights = fetch(sems, 0, w_hbm, w_ref)
    xs = fetch(sems, 1, x_hbm.at[2 * LINE : 14 * LINE, :], x_ref)
    ts = fetch(sems, 2, t_hbm, t_ref)
    turned = fetch(sems, 3, wt_hbm, wt_ref)
    orders = fetch(sems, 4, order_hbm, order_ref)
    mean, rstd = norm_lines(stats_ref)
    nhat = (h_ref[...] - tile_lines(mean, GH - 2)) * tile_lines(rstd, GH - 2)
    n2 = nhat * gain_ref[...] + shift_ref[...]
    a2 = jnp.where(grid_masks(pos_ref, 1, GH - 2), n2 * sigmoid(n2), 0.0)
    spread_taps(scr_a, a2)
    weights.wait()
    conv = conv_lines(scr_a, w_ref, 12) + bias_ref[...]
    xs.wait()
    out = x_ref[...].astype(F32) + conv
    bout_ref[...] = out[2 * LINE : 10 * LINE].astype(BF16)
    bouts = fetch(sems, 5, bout_ref, bout_hbm)
    ts.wait()
    diff = out - t_ref[...].astype(F32)
    masks = center_masks()
    mid = diff[2 * LINE : 10 * LINE]
    square = mid * mid
    lane = lax.broadcasted_iota(jnp.int32, (1, 128), 1)
    errs = jnp.zeros((1, 128), F32)
    for b in range(2):
        part = jnp.sum(jnp.where(masks[b], square, 0.0), axis=0, keepdims=True)
        errs = errs + jnp.where(lane == b, jnp.sum(part, axis=1, keepdims=True), 0.0)
    err_ref[...] = errs
    sign = tile_lines(per_line(sign_ref[0:1, :], sign_ref[1:2, :]), 12)
    u = jnp.where(grid_masks(pos_ref, 2, 12), diff * sign, 0.0)
    spread_wide(scr_u, u)
    center = u[2 * LINE : 10 * LINE]
    u_ref[...] = center.astype(BF16)
    us = fetch(sems, 6, u_ref, u_hbm)
    kept = jnp.where(masks[0] | masks[1], center, 0.0).astype(BF16)
    orders.wait()
    kernel_grad(mine_ref, theirs_ref, pos_ref[2], scr_a, 2, kept, order_ref)
    mines = fetch(sems, 7, mine_ref, mine_hbm)
    others = fetch(sems, 8, theirs_ref, theirs_hbm)
    turned.wait()
    da2 = conv_turned(scr_u, wt_ref, 10)
    e = da2 * silu_slope(n2[2 * LINE : 12 * LINE]) * gain_ref[...]
    e_ref[...] = e
    out_ref[...] = pair_sums(e[LINE : 9 * LINE], nhat[3 * LINE : 11 * LINE], masks)
    for copy in (bouts, us, mines, others):
        copy.wait()


def back_line(sums_ref):
    sums = jnp.sum(sums_ref[...], axis=0, keepdims=True) * (1.0 / TOTAL)
    first = per_line(lanes_to_chans(sums, 0), lanes_to_chans(sums, 1))
    second = per_line(lanes_to_chans(sums, 2), lanes_to_chans(sums, 3))
    return first, second


def third_kernel(
    pos_ref, e_ref, stats_ref, sums_ref, h_hbm, taps_hbm, order_hbm,
    d_ref, mine_ref, theirs_ref, h_ref, taps_ref, order_ref, sems,
):
    hs = fetch(sems, 0, h_hbm.at[2 * LINE : 12 * LINE, :], h_ref)
    orders = fetch(sems, 1, order_hbm, order_ref)
    taps = fetch(sems, 2, taps_hbm, taps_ref)
    mean, rstd = norm_lines(stats_ref)
    first, second = back_line(sums_ref)
    scale = tile_lines(rstd, 10)
    hs.wait()
    nhat = (h_ref[...] - tile_lines(mean, 10)) * scale
    dh = scale * (e_ref[...] - tile_lines(first, 10) - nhat * tile_lines(second, 10))
    dh = jnp.where(grid_masks(pos_ref, 3, 10), dh, 0.0)
    d_ref[...] = dh.astype(BF16)
    masks = center_masks()
    kept = jnp.where(masks[0] | masks[1], dh[LINE : 9 * LINE], 0.0).astype(BF16)
    orders.wait()
    taps.wait()
    kernel_grad(mine_ref, theirs_ref, pos_ref[2], taps_ref, 0, kept, order_ref)


def fourth_kernel(
    d_ref, stats_ref, gain_ref, shift_ref, x_hbm, wt_hbm, e_ref, out_ref, scr, x_ref, wt_ref, sems
):
    turned = fetch(sems, 0, wt_hbm, wt_ref)
    xs = fetch(sems, 1, x_hbm.at[4 * LINE : 12 * LINE, :], x_ref)
    spread_wide(scr, d_ref[...].astype(F32))
    mean, rstd = norm_lines(stats_ref)
    xs.wait()
    nhat = (x_ref[...].astype(F32) - tile_lines(mean, ROWS)) * tile_lines(rstd, ROWS)
    n1 = nhat * gain_ref[...] + shift_ref[...]
    slope = silu_slope(n1) * gain_ref[...]
    turned.wait()
    e1 = conv_turned(scr, wt_ref, ROWS) * slope
    e_ref[...] = e1
    out_ref[...] = pair_sums(e1, nhat, center_masks())


def last_kernel(e_ref, x_ref, stats_ref, sums_ref, u_ref, weight_ref, out_ref):
    mean, rstd = norm_lines(stats_ref)
    first, second = back_line(sums_ref)
    scale = tile_lines(rstd, ROWS)
    nhat = (x_ref[4 * LINE : 12 * LINE, :].astype(F32) - tile_lines(mean, ROWS)) * scale
    dx = scale * (e_ref[...] - tile_lines(first, ROWS) - nhat * tile_lines(second, ROWS))
    out_ref[...] = ((u_ref[...].astype(F32) + dx) * weight_ref[...]).astype(BF16)


def pieces(row):
    high = row.astype(BF16).astype(F32)
    rest = row - high
    mid = rest.astype(BF16).astype(F32)
    return high, mid, (rest - mid).astype(BF16).astype(F32)


def piece_rows(count, at, sums, errs):
    index = lax.broadcasted_iota(jnp.int32, (count, 128), 0)
    out = jnp.zeros((count, 128), F32)
    for i, piece in enumerate(pieces(sums) + pieces(errs)):
        out = out + jnp.where(index == at + i, piece, 0.0)
    return out


def chunks(out_ref, mine_ref, got_ref):
    for j in range(4):
        for i in range(4):
            for k in range(3):
                rows = slice(j * 80, (j + 1) * 80)
                lanes = slice(i * 384 + k * 128, i * 384 + (k + 1) * 128)
                both = mine_ref[rows, lanes].astype(F32) + got_ref[rows, lanes].astype(F32)
                out_ref[i * 4 + j, k * 80 : (k + 1) * 80, :] = both.astype(BF16)


def early_kernel(mine_ref, got_ref, out_hbm, scr, sems):
    chunks(scr, mine_ref, got_ref)
    fetch(sems, 0, scr, out_hbm.at[:, 0:240, :]).wait()


def late_kernel(mine_ref, got_ref, tails_ref, in_hbm, out_hbm, scr, sems):
    del in_hbm
    chunks(scr, mine_ref, got_ref)
    tails = jnp.sum(tails_ref[...], axis=0)
    rows = piece_rows(16, 0, tails[0:1], tails[1:2]).astype(BF16)
    for i in range(16):
        scr[i, 240:256, :] = rows
    fetch(sems, 0, scr, out_hbm.at[:, 240:496, :]).wait()


def plane_kernel(in_ref, move_ref, out_ref):
    total = in_ref[0].astype(F32)
    for i in range(1, 16):
        total = total + in_ref[i].astype(F32)
    tail = total[480:496]
    sums = tail[0:1] + tail[1:2] + tail[2:3]
    errs = tail[3:4] + tail[4:5] + tail[5:6]
    rows = piece_rows(80, 60, sums, errs)
    moved = dot(move_ref[...], total[0:480].astype(BF16))
    for z in range(8):
        out_ref[z] = (moved[z * 80 : (z + 1) * 80] + rows).astype(BF16)


def depth_kernel(in_ref, out_ref, sums_ref, errs_ref):
    total = in_ref[0].astype(F32)
    for i in range(1, 8):
        total = total + in_ref[i].astype(F32)
    grads = total[0:64].astype(BF16)
    for i in range(8):
        out_ref[i] = grads
    sums_ref[...] = total[60:61] + total[61:62] + total[62:63]
    errs_ref[...] = total[63:64] + total[64:65] + total[65:66]


VM = pl.BlockSpec(memory_space=pltpu.VMEM)
SM = pl.BlockSpec(memory_space=pltpu.SMEM)
HB = pl.BlockSpec(memory_space=pltpu.HBM)
DMA = pltpu.SemaphoreType.DMA


def call(kernel, outs, ins, scratch=(), flops=0, aliases=None):
    size = sum(int(np.prod(s.shape)) * s.dtype.itemsize for _, s in outs)
    size += sum(a.size * a.dtype.itemsize for _, a in ins)
    many = len(outs) > 1
    shapes, spaces = [s for _, s in outs], [p for p, _ in outs]
    return pl.pallas_call(
        kernel,
        out_shape=tuple(shapes) if many else shapes[0],
        in_specs=[p for p, _ in ins],
        out_specs=tuple(spaces) if many else spaces[0],
        scratch_shapes=list(scratch),
        input_output_aliases=aliases or {},
        compiler_params=pltpu.CompilerParams(vmem_limit_bytes=40 * 2**20),
        cost_estimate=pl.CostEstimate(flops=flops, bytes_accessed=size, transcendentals=0),
    )(*[a for _, a in ins])


def sds(shape, dtype=F32):
    return jax.ShapeDtypeStruct(shape, dtype)


AXES = ("x", "c", "z", "y")


def share(row):
    flat = row.reshape(128)
    return lax.all_to_all(jnp.broadcast_to(flat[None], (DEVICES, 128)), AXES, 0, 0, tiled=True)


def widen(features, target):
    up = [(i, i + 1) for i in range(7)]
    down = [(i + 1, i) for i in range(7)]
    low = jnp.concatenate([features[:, ROWS - 4 :], target[:, ROWS - 2 :]], axis=1)
    high = jnp.concatenate([features[:, :4], target[:, :2]], axis=1)
    low = lax.ppermute(low, ("x", "c"), up)
    high = lax.ppermute(high, ("x", "c"), down)
    f = jnp.concatenate([low[:, :4], features, high[:, :4]], axis=1)
    t = jnp.concatenate([low[:, 4:], target, high[:, 4:]], axis=1)
    right = [(i, i + 1) for i in range(31)]
    left = [(i + 1, i) for i in range(31)]

    def pack(a, b):
        return jnp.concatenate([a.reshape(2, GH * 4, C), b.reshape(2, 12 * 4, C)], axis=1)

    first = lax.ppermute(pack(f[:, :, COLS - 4 :], t[:, :, COLS - 4 :]), ("z", "y"), right)
    last = lax.ppermute(pack(f[:, :, :4], t[:, :, :4]), ("z", "y"), left)

    def unpack(v):
        return v[:, : GH * 4].reshape(2, GH, 4, C), v[:, GH * 4 :].reshape(2, 12, 4, C)

    fl, tl = unpack(first)
    fr, tr = unpack(last)
    f = jnp.concatenate([fl, f, fr], axis=2).transpose(1, 0, 2, 3).reshape(GH * LINE, C)
    t = jnp.concatenate([tl, t, tr], axis=2).transpose(1, 0, 2, 3).reshape(12 * LINE, C)
    return f, t


def center(values):
    return values.reshape(ROWS, 2, GW, C)[:, :, RIM : RIM + COLS].transpose(1, 0, 2, 3)


def time_embed(timestep, time_weight, time_bias):
    half = TEMB // 2
    freqs = jnp.exp(-jnp.log(10000.0) * jnp.arange(half, dtype=F32) / half)
    angles = timestep.astype(F32)[:, None] * freqs[None, :]
    emb = jnp.concatenate([jnp.cos(angles), jnp.sin(angles)], axis=1)
    return jnp.dot(jax.nn.silu(emb), time_weight.astype(F32), precision=HIGH) + time_bias


def order_matrix():
    out = np.zeros((C, C), np.float32)
    for z in range(8):
        for y in range(4):
            for j in range(10):
                out[z * 40 + y * 10 + j, y * 80 + z * 10 + j] = 1.0
    return jnp.asarray(out, BF16)


def move_matrix():
    out = np.zeros((640, 480), np.float32)
    for grad in range(2):
        for k in range(3):
            for z in range(8):
                for j in range(10):
                    out[z * 80 + grad * 30 + k * 10 + j, grad * 240 + k * 80 + z * 10 + j] = 1.0
    return jnp.asarray(out, BF16)


def swap(theirs):
    return lax.ppermute(theirs, "c", [(0, 1), (1, 0)])


def first_stats(features):
    row = call(moments_kernel, [(VM, sds((1, 128)))], [(VM, features.reshape(2 * ROWS * COLS, C))])
    pair = lax.all_gather(row.reshape(128), "c")
    plane = call(functools.partial(merge_kernel, float(LOCAL)), [(VM, sds((16, 128)))], [(VM, pair)])
    plane = lax.all_to_all(plane, ("x", "y"), 0, 0, tiled=True)
    depth = call(functools.partial(merge_kernel, float(2 * LOCAL)), [(VM, sds((8, 128)))], [(VM, plane)])
    return lax.all_to_all(depth, ("z",), 0, 0, tiled=True)


def body(
    features, target, norm1_gain, norm1_shift, kernel1, bias1, time_weight, time_bias,
    norm2_gain, norm2_shift, kernel2, bias2, ref_error, preference, timestep,
):
    h = lax.axis_index("x") * 2 + lax.axis_index("c")
    w = lax.axis_index("z") * 4 + lax.axis_index("y")
    pos = jnp.stack([h, w, lax.axis_index("c")]).astype(jnp.int32)
    gain1, shift1 = norm1_gain.reshape(1, C), norm1_shift.reshape(1, C)
    gain2, shift2 = norm2_gain.reshape(1, C), norm2_shift.reshape(1, C)
    stats1 = first_stats(features)
    fx, tx = widen(features, target)
    add1 = bias1.reshape(1, C) + time_embed(timestep, time_weight, time_bias)
    order, move = order_matrix(), move_matrix()
    signs = jnp.where(jnp.arange(2) == preference[0], 2.0, -2.0).astype(F32)
    sign_rows = jnp.broadcast_to(signs[:, None], (2, C))
    w1, w2 = kernel1.reshape(3, 3 * C, C), kernel2.reshape(3, 3 * C, C)
    conv_flops = 2 * 9 * C * C * LINE
    half = sds((C, LANES // 2), BF16)
    row, lines = sds((1, 128)), sds((ROWS * LINE, C), BF16)
    h1, part, taps1 = call(
        first_kernel,
        [(VM, sds((14 * LINE, C))), (VM, row), (HB, sds((10 * LINE, 3 * C), BF16))],
        [(SM, pos), (VM, fx), (VM, stats1), (VM, gain1), (VM, shift1), (VM, add1), (HB, w1)],
        [pltpu.VMEM((GH * LINE, 3 * C), BF16), pltpu.VMEM((3, 3 * C, C), BF16), DMA((2,))],
        14 * conv_flops,
    )
    stats2 = share(part)
    e2, part, errs, bout, u, mine2, theirs2 = call(
        second_kernel,
        [
            (VM, sds((10 * LINE, C))), (VM, row), (VM, row), (HB, lines), (HB, lines), (HB, half), (HB, half),
        ],
        [
            (SM, pos), (VM, h1), (VM, stats2), (VM, gain2), (VM, shift2), (VM, bias2.reshape(1, C)),
            (VM, sign_rows), (HB, w2), (HB, kernel2), (HB, fx), (HB, tx), (HB, order),
        ],
        [
            pltpu.VMEM((14 * LINE, 3 * C), BF16), pltpu.VMEM((12 * LINE, 1152), BF16),
            pltpu.VMEM((3, 3 * C, C), BF16), pltpu.VMEM((3, 3, C, C), BF16),
            pltpu.VMEM((12 * LINE, C), BF16), pltpu.VMEM((12 * LINE, C), BF16), pltpu.VMEM((C, C), BF16),
            pltpu.VMEM((ROWS * LINE, C), BF16), pltpu.VMEM((ROWS * LINE, C), BF16),
            pltpu.VMEM((C, LANES // 2), BF16), pltpu.VMEM((C, LANES // 2), BF16), DMA((9,)),
        ],
        30 * conv_flops,
    )
    sums2 = share(part)
    got2 = swap(theirs2)
    block_out = center(bout)
    plane = call(
        early_kernel,
        [(HB, sds((16, 496, 128), BF16))],
        [(VM, mine2), (VM, got2)],
        [pltpu.VMEM((16, 240, 128), BF16), DMA((1,))],
    )
    d1, mine1, theirs1 = call(
        third_kernel,
        [(VM, sds((10 * LINE, C), BF16)), (VM, half), (VM, half)],
        [(SM, pos), (VM, e2), (VM, stats2), (VM, sums2), (HB, h1), (HB, taps1), (HB, order)],
        [
            pltpu.VMEM((10 * LINE, C), F32), pltpu.VMEM((10 * LINE, 3 * C), BF16),
            pltpu.VMEM((C, C), BF16), DMA((3,)),
        ],
        8 * conv_flops,
    )
    got1 = swap(theirs1)
    e1, part = call(
        fourth_kernel,
        [(VM, sds((ROWS * LINE, C))), (VM, row)],
        [(VM, d1), (VM, stats1), (VM, gain1), (VM, shift1), (HB, fx), (HB, kernel1)],
        [
            pltpu.VMEM((10 * LINE, 1152), BF16), pltpu.VMEM((ROWS * LINE, C), BF16),
            pltpu.VMEM((3, 3, C, C), BF16), DMA((2,)),
        ],
        8 * conv_flops,
    )
    tails = lax.all_gather(jnp.concatenate([part, errs], axis=0), "c")
    plane = call(
        late_kernel,
        [(HB, sds((16, 496, 128), BF16))],
        [(VM, mine1), (VM, got1), (VM, tails), (HB, plane)],
        [pltpu.VMEM((16, 256, 128), BF16), DMA((1,))],
        0,
        {3: 0},
    )
    plane = lax.all_to_all(plane, ("x", "y"), 0, 0, tiled=True)
    depth = call(plane_kernel, [(VM, sds((8, 80, 128), BF16))], [(VM, plane), (VM, move)])
    depth = lax.all_to_all(depth, ("z",), 0, 0, tiled=True)
    copies, sums1, errs = call(
        depth_kernel, [(VM, sds((8, 64, 128), BF16)), (VM, row), (VM, row)], [(VM, depth)]
    )
    whole = lax.all_to_all(copies, ("x", "c"), 0, 0, tiled=True)
    err = errs[0, :2] / (BAND_ROWS * BAND_COLS * C)
    excess = err - ref_error[0]
    gap = jnp.where(preference[0] == 0, excess[0] - excess[1], excess[1] - excess[0])
    loss = jax.nn.softplus(gap)
    weight = jax.nn.sigmoid(gap)
    grad = call(
        last_kernel,
        [(VM, lines)],
        [(VM, e1), (VM, fx), (VM, stats1), (VM, sums1), (VM, u), (VM, jnp.broadcast_to(weight, (1, C)))],
    )
    feature_grad = center(grad)
    scale = weight / jnp.sqrt(F32(2 * BAND_ROWS * BAND_COLS))
    whole = whole[:, :60].reshape(4, 2, 2, 3, 10, 128).transpose(2, 1, 0, 3, 5, 4).reshape(2, LANES, 10)
    whole = (whole[:, :TAPS].astype(F32) * scale).reshape(2, 3, 3, C, 10)
    return (block_out, feature_grad, whole[1], whole[0], loss)


def solution(mesh):
    fine = Mesh(mesh.devices.reshape(4, 2, 8, 4), AXES)
    cells = P(None, ("x", "c"), ("z", "y"), None)
    kernels = P(None, None, None, ("z", "y"))
    return jax.shard_map(
        body,
        mesh=fine,
        in_specs=(cells, cells) + (P(),) * 13,
        out_specs=(cells, cells, kernels, kernels, P()),
        check_vma=False,
    )
```

```python
import functools

import jax
import jax.numpy as jnp
import numpy as np
from jax import lax
from jax.experimental import pallas as pl
from jax.experimental.pallas import tpu as pltpu
from jax.sharding import Mesh
from jax.sharding import PartitionSpec as P

GROUPS = 32
TEMB = 1280
C = 320
WIDTH = C // GROUPS
ROWS, COLS = 8, 16
BAND_ROWS, BAND_COLS = 64, 512
RIM = 4
GH, GW = ROWS + 2 * RIM, COLS + 2 * RIM
LINE = 2 * GW
DEVICES = 256
LOCAL = ROWS * COLS * WIDTH
TOTAL = LOCAL * DEVICES
TAPS = 9 * C
LANES = 3072
EPS = 1e-05
F32, BF16 = jnp.float32, jnp.bfloat16
HIGH = lax.Precision.HIGHEST
VMEM_LIMIT = 63 * 2**20


def dot(a, b):
    return jnp.dot(a, b, preferred_element_type=F32)


def pieces(row):
    high = row.astype(BF16).astype(F32)
    rest = row - high
    mid = rest.astype(BF16).astype(F32)
    return high, mid, rest - mid


def hot():
    blocks = []
    for slot in range(4):
        low = (lax.broadcasted_iota(jnp.int32, (128, 384), 0) - slot * GROUPS) * WIDTH
        chan = lax.broadcasted_iota(jnp.int32, (128, 384), 1)
        blocks.append(((chan >= low) & (chan < low + WIDTH) & (chan < C)).astype(F32).astype(BF16))
    return jnp.concatenate(blocks, axis=1)


def stacked(row):
    index = lax.broadcasted_iota(jnp.int32, (16, row.shape[1]), 0)
    out = jnp.zeros((16, row.shape[1]), F32)
    for i, piece in enumerate(pieces(row)):
        out = jnp.where(index == i, piece, out)
    return out.astype(BF16)


def expand(row, table):
    wide = jnp.sum(dot(stacked(row), table), axis=0, keepdims=True)
    return [wide[:, i * 384 : i * 384 + C] for i in range(4)]


def collapse(rows, table):
    gap, empty = jnp.zeros((1, 384 - C), F32), jnp.zeros((1, C), F32)
    wide = jnp.concatenate([v for row in rows for v in (empty if row is None else row, gap)], axis=1)
    small = lax.dot_general(stacked(wide), table, (((1,), (1,)), ((), ())), preferred_element_type=F32)
    return jnp.sum(small, axis=0, keepdims=True)


def per_line(first, second):
    return jnp.concatenate(
        [jnp.broadcast_to(first, (GW, C)), jnp.broadcast_to(second, (GW, C))], axis=0
    )


def tile_lines(line, count):
    return jnp.broadcast_to(line[None], (count, LINE, C)).reshape(count * LINE, C)


def masked(values, top, count):
    high = lax.axis_index("x") * 2 + lax.axis_index("c")
    wide = lax.axis_index("z") * 4 + lax.axis_index("y")
    col = lax.broadcasted_iota(jnp.int32, (LINE, C), 0)
    gx = jnp.where(col >= GW, col - GW, col) + (wide * COLS - RIM)
    line = ((gx >= 0) & (gx < BAND_COLS)).astype(F32)
    upper = line * jnp.where(high > 0, 1.0, 0.0)
    lower = line * jnp.where(high < BAND_ROWS // ROWS - 1, 1.0, 0.0)
    parts = [(upper, RIM - top), (line, ROWS), (lower, top + count - RIM - ROWS)]
    mask = jnp.concatenate([jnp.broadcast_to(v[None], (n, LINE, C)) for v, n in parts], axis=0)
    return values * mask.reshape(count * LINE, C)


def center_line():
    col = lax.broadcasted_iota(jnp.int32, (LINE, C), 0)
    one = (col >= RIM) & (col < RIM + COLS)
    two = (col >= GW + RIM) & (col < GW + RIM + COLS)
    return one.astype(F32), two.astype(F32)


def line_sums(values):
    total = jnp.sum(values.reshape(ROWS, LINE, C), axis=0)
    return [jnp.sum(total * line, axis=0, keepdims=True) for line in center_line()]


def norm_lines(stats_ref, table):
    stats = stats_ref[...]
    sums = jnp.sum(stats, axis=0, keepdims=True)
    mean = sums * (1.0 / DEVICES)
    off = stats - mean
    spread = jnp.sum(off * off, axis=0, keepdims=True) * LOCAL
    var = (sums + pltpu.roll(spread, 64, 1)) * (1.0 / TOTAL)
    lane = lax.broadcasted_iota(jnp.int32, (1, 128), 1)
    row = jnp.where(lane < 64, mean, 1.0 / jnp.sqrt(jnp.maximum(var, 0.0) + EPS))
    one, two, three, four = expand(row, table)
    return per_line(one, two), per_line(three, four)


def moments(values, table):
    first, second = line_sums(values)
    means = collapse([first, second, None, None], table) * (1.0 / LOCAL)
    one, two, _, _ = expand(means, table)
    off = values - tile_lines(per_line(one, two), ROWS)
    first, second = line_sums(off * off)
    return means + collapse([None, None, first, second], table)


def pair_sums(scaled, normed, table):
    return collapse(line_sums(scaled) + line_sums(scaled * normed), table)


def sigmoid(v):
    return 0.5 + 0.5 * jnp.tanh(0.5 * v)


def silu_slope(v):
    sig = sigmoid(v)
    return sig * (1.0 + v * (1.0 - sig))


def spread_taps(ref, values):
    count = values.shape[0]
    ref[:, 0:C] = pltpu.roll(values, 1, 0).astype(BF16)
    ref[:, C : 2 * C] = values.astype(BF16)
    ref[:, 2 * C : 3 * C] = pltpu.roll(values, count - 1, 0).astype(BF16)


def spread_wide(ref, values):
    count = values.shape[0]
    ref[:, 0:C] = pltpu.roll(values, 1, 0).astype(BF16)
    ref[:, 384 : 384 + C] = values.astype(BF16)
    ref[:, 768 : 768 + C] = pltpu.roll(values, count - 1, 0).astype(BF16)


def conv_lines(ref, weights_ref, count):
    total = dot(ref[0 : count * LINE, :], weights_ref[0])
    for ky in range(1, 3):
        total = total + dot(ref[ky * LINE : (ky + count) * LINE, :], weights_ref[ky])
    return total


def conv_turned(ref, weights_ref, count):
    total = None
    for ky in range(3):
        for kx in range(3):
            part = lax.dot_general(
                ref[ky * LINE : (ky + count) * LINE, kx * 384 : kx * 384 + C],
                weights_ref[2 - ky, 2 - kx],
                (((1,), (1,)), ((), ())),
                preferred_element_type=F32,
            )
            total = part if total is None else total + part
    return total


def kernel_grad(mine_ref, theirs_ref, taps_ref, top, grads, order_ref):
    core = lax.axis_index("c")
    ordered = dot(grads.astype(BF16), order_ref[...])
    left = ordered.T.astype(BF16)
    parts = []
    for ky in range(3):
        lines = taps_ref[(top + ky) * LINE : (top + ky + ROWS) * LINE, :]
        parts.append(dot(left, lines).astype(BF16))
    parts.append(jnp.zeros((C, LANES - TAPS), BF16))
    whole = jnp.concatenate(parts, axis=1)
    low, high = whole[:, : LANES // 2], whole[:, LANES // 2 :]

    @pl.when(core == 0)
    def _():
        mine_ref[...] = low
        theirs_ref[...] = high

    @pl.when(core == 1)
    def _():
        mine_ref[...] = high
        theirs_ref[...] = low


def fetch(sems, index, src, dst):
    copy = pltpu.make_async_copy(src, dst, sems.at[index])
    copy.start()
    return copy


def fetch_all(sems, first, pairs):
    return [fetch(sems, first + i, src, dst) for i, (src, dst) in enumerate(pairs)]


def wait_all(copies):
    for copy in copies:
        copy.wait()


def flat(ref):
    return ref[...].reshape(1, C)


def moments_kernel(x_ref, t_ref, out_ref, low_ref, high_ref):
    half = ROWS * COLS
    for b in range(2):
        at, to = b * half, b * 6 * COLS
        low_ref[to : to + 4 * COLS] = x_ref[at + 4 * COLS : at + 8 * COLS, :]
        low_ref[to + 4 * COLS : to + 6 * COLS] = t_ref[at + 6 * COLS : at + 8 * COLS, :]
        high_ref[to : to + 4 * COLS] = x_ref[at : at + 4 * COLS, :]
        high_ref[to + 4 * COLS : to + 6 * COLS] = t_ref[at : at + 2 * COLS, :]
    table = hot()
    values = [x_ref[b * half : (b + 1) * half, :].astype(F32) for b in range(2)]
    sums = [jnp.sum(v, axis=0, keepdims=True) for v in values]
    means = collapse(sums + [None, None], table) * (1.0 / LOCAL)
    offs = [v - m for v, m in zip(values, expand(means, table))]
    sums = [jnp.sum(v * v, axis=0, keepdims=True) for v in offs]
    out = means + collapse([None, None] + sums, table)
    out_ref[...] = jnp.broadcast_to(out, (DEVICES, 128))


def first_kernel(
    stats_hbm, gain_hbm, shift_hbm, bias_hbm, temb_hbm, x_hbm, w_hbm,
    out_ref, h_hbm, taps_hbm, scr, w_ref, x_ref, h_ref, stats_ref, gain_ref, shift_ref, bias_ref, temb_ref, sems,
):
    small = fetch_all(
        sems, 4,
        [
            (stats_hbm, stats_ref), (gain_hbm, gain_ref), (shift_hbm, shift_ref),
            (bias_hbm, bias_ref), (temb_hbm, temb_ref),
        ],
    )
    xs = fetch(sems, 2, x_hbm, x_ref)
    weights = fetch(sems, 0, w_hbm, w_ref)
    table = hot()
    wait_all(small)
    mean, rstd = norm_lines(stats_ref, table)
    scale = tile_lines(rstd * flat(gain_ref), GH)
    xs.wait()
    n1 = (x_ref[...].astype(F32) - tile_lines(mean, GH)) * scale + flat(shift_ref)
    spread_taps(scr, masked(n1 * sigmoid(n1), 0, GH))
    taps = fetch(sems, 1, scr.at[3 * LINE : 13 * LINE, :], taps_hbm)
    weights.wait()
    h1 = conv_lines(scr, w_ref, GH - 2) + (flat(bias_ref) + flat(temb_ref))
    h_ref[...] = h1
    hs = fetch(sems, 3, h_ref, h_hbm)
    out_ref[...] = jnp.broadcast_to(moments(h1[3 * LINE : 11 * LINE], table), (DEVICES, 128))
    taps.wait()
    hs.wait()


def second_kernel(
    stats_hbm, gain_hbm, shift_hbm, bias_hbm, sign_hbm, h_hbm, w_hbm, wt_hbm, x_hbm, t_hbm, order_hbm,
    out_ref, err_ref, e_hbm, bout_hbm, u_hbm, mine_hbm, theirs_hbm,
    scr_a, scr_u, w_ref, wt_ref, x_ref, t_ref, order_ref, bout_ref, u_ref, mine_ref, theirs_ref, h_ref, e_ref,
    stats_ref, gain_ref, shift_ref, bias_ref, sign_ref, sems,
):
    small = fetch_all(
        sems, 11,
        [
            (stats_hbm, stats_ref), (gain_hbm, gain_ref), (shift_hbm, shift_ref),
            (bias_hbm, bias_ref), (sign_hbm, sign_ref),
        ],
    )
    hs = fetch(sems, 9, h_hbm, h_ref)
    weights = fetch(sems, 0, w_hbm, w_ref)
    xs = fetch(sems, 1, x_hbm.at[2 * LINE : 14 * LINE, :], x_ref)
    ts = fetch(sems, 2, t_hbm, t_ref)
    orders = fetch(sems, 4, order_hbm, order_ref)
    turned = fetch(sems, 3, wt_hbm, wt_ref)
    table = hot()
    wait_all(small)
    mean, rstd = norm_lines(stats_ref, table)
    hs.wait()
    nhat = (h_ref[...] - tile_lines(mean, GH - 2)) * tile_lines(rstd, GH - 2)
    n2 = nhat * flat(gain_ref) + flat(shift_ref)
    spread_taps(scr_a, masked(n2 * sigmoid(n2), 1, GH - 2))
    weights.wait()
    conv = conv_lines(scr_a, w_ref, 12) + flat(bias_ref)
    xs.wait()
    out = x_ref[...].astype(F32) + conv
    bout_ref[...] = out[2 * LINE : 10 * LINE].astype(BF16)
    bouts = fetch(sems, 5, bout_ref, bout_hbm)
    ts.wait()
    diff = out - t_ref[...].astype(F32)
    mid = diff[2 * LINE : 10 * LINE]
    lane = lax.broadcasted_iota(jnp.int32, (1, 128), 1)
    errs = jnp.zeros((1, 128), F32)
    for b, part in enumerate(line_sums(mid * mid)):
        errs = errs + jnp.where(lane == b, jnp.sum(part, axis=1, keepdims=True), 0.0)
    err_ref[...] = errs
    sign = tile_lines(per_line(flat(sign_ref), -flat(sign_ref)), 12)
    u = masked(diff * sign, 2, 12)
    spread_wide(scr_u, u)
    center = u[2 * LINE : 10 * LINE]
    u_ref[...] = center.astype(BF16)
    us = fetch(sems, 6, u_ref, u_hbm)
    one, two = center_line()
    orders.wait()
    kernel_grad(mine_ref, theirs_ref, scr_a, 2, center * tile_lines(one + two, ROWS), order_ref)
    mines = fetch(sems, 7, mine_ref, mine_hbm)
    others = fetch(sems, 8, theirs_ref, theirs_hbm)
    turned.wait()
    da2 = conv_turned(scr_u, wt_ref, 10)
    e = da2 * silu_slope(n2[2 * LINE : 12 * LINE]) * flat(gain_ref)
    e_ref[...] = e
    es = fetch(sems, 10, e_ref, e_hbm)
    sums = pair_sums(e[LINE : 9 * LINE], nhat[3 * LINE : 11 * LINE], table)
    out_ref[...] = jnp.broadcast_to(sums, (DEVICES, 128))
    for copy in (bouts, us, mines, others, es):
        copy.wait()


def back_line(sums_ref, table):
    sums = jnp.sum(sums_ref[...], axis=0, keepdims=True) * (1.0 / TOTAL)
    one, two, three, four = expand(sums, table)
    return per_line(one, two), per_line(three, four)


def third_kernel(
    stats_hbm, sums_hbm, e_hbm, h_hbm, taps_hbm, order_hbm,
    d_hbm, mine_ref, theirs_ref, e_ref, h_ref, taps_ref, order_ref, d_ref, stats_ref, sums_ref, sems,
):
    small = fetch_all(sems, 5, [(stats_hbm, stats_ref), (sums_hbm, sums_ref)])
    hs = fetch(sems, 0, h_hbm.at[2 * LINE : 12 * LINE, :], h_ref)
    es = fetch(sems, 3, e_hbm, e_ref)
    orders = fetch(sems, 1, order_hbm, order_ref)
    taps = fetch(sems, 2, taps_hbm, taps_ref)
    table = hot()
    wait_all(small)
    mean, rstd = norm_lines(stats_ref, table)
    first, second = back_line(sums_ref, table)
    scale = tile_lines(rstd, 10)
    hs.wait()
    es.wait()
    nhat = (h_ref[...] - tile_lines(mean, 10)) * scale
    dh = scale * (e_ref[...] - tile_lines(first, 10) - nhat * tile_lines(second, 10))
    dh = masked(dh, 3, 10)
    d_ref[...] = dh.astype(BF16)
    ds = fetch(sems, 4, d_ref, d_hbm)
    one, two = center_line()
    orders.wait()
    taps.wait()
    kernel_grad(mine_ref, theirs_ref, taps_ref, 0, dh[LINE : 9 * LINE] * tile_lines(one + two, ROWS), order_ref)
    ds.wait()


def fourth_kernel(
    stats_hbm, gain_hbm, shift_hbm, d_hbm, x_hbm, wt_hbm,
    out_ref, e_hbm, scr, x_ref, wt_ref, d_ref, e_ref, stats_ref, gain_ref, shift_ref, sems,
):
    ds = fetch(sems, 2, d_hbm, d_ref)
    small = fetch_all(sems, 4, [(stats_hbm, stats_ref), (gain_hbm, gain_ref), (shift_hbm, shift_ref)])
    xs = fetch(sems, 1, x_hbm.at[4 * LINE : 12 * LINE, :], x_ref)
    turned = fetch(sems, 0, wt_hbm, wt_ref)
    table = hot()
    wait_all(small)
    mean, rstd = norm_lines(stats_ref, table)
    ds.wait()
    spread_wide(scr, d_ref[...].astype(F32))
    xs.wait()
    nhat = (x_ref[...].astype(F32) - tile_lines(mean, ROWS)) * tile_lines(rstd, ROWS)
    n1 = nhat * flat(gain_ref) + flat(shift_ref)
    slope = silu_slope(n1) * flat(gain_ref)
    turned.wait()
    e1 = conv_turned(scr, wt_ref, ROWS) * slope
    e_ref[...] = e1
    es = fetch(sems, 3, e_ref, e_hbm)
    out_ref[...] = pair_sums(e1, nhat, table)
    es.wait()


def last_kernel(sums_ref, errs_ref, stats_ref, sign_ref, ref_ref, e_ref, x_ref, u_ref, out_ref, info_ref):
    excess = errs_ref[:, 0:2] * (1.0 / (BAND_ROWS * BAND_COLS * C)) - ref_ref[...]
    gap = 0.5 * flat(sign_ref)[:, 0:1] * (excess[:, 0:1] - excess[:, 1:2])
    weight = 1.0 / (1.0 + jnp.exp(-gap))
    lane = lax.broadcasted_iota(jnp.int32, (1, 128), 1)
    info_ref[...] = jnp.where(lane == 0, weight, gap)
    table = hot()
    mean, rstd = norm_lines(stats_ref, table)
    first, second = back_line(sums_ref, table)
    scale = tile_lines(rstd, ROWS)
    nhat = (x_ref[4 * LINE : 12 * LINE, :].astype(F32) - tile_lines(mean, ROWS)) * scale
    dx = scale * (e_ref[...] - tile_lines(first, ROWS) - nhat * tile_lines(second, ROWS))
    out_ref[...] = ((u_ref[...].astype(F32) + dx) * weight).astype(BF16)


def piece_rows(count, at, sums, errs):
    index = lax.broadcasted_iota(jnp.int32, (count, 128), 0)
    out = jnp.zeros((count, 128), F32)
    for i, piece in enumerate(pieces(sums) + pieces(errs)):
        out = out + jnp.where(index == at + i, piece, 0.0)
    return out


def chunks(out_ref, mine_ref, got_ref):
    for j in range(4):
        for i in range(4):
            for k in range(3):
                rows = slice(j * 80, (j + 1) * 80)
                lanes = slice(i * 384 + k * 128, i * 384 + (k + 1) * 128)
                both = mine_ref[rows, lanes].astype(F32) + got_ref[rows, lanes].astype(F32)
                out_ref[i * 4 + j, k * 80 : (k + 1) * 80, :] = both.astype(BF16)


def early_kernel(mine_ref, got_ref, out_hbm, scr, sems):
    chunks(scr, mine_ref, got_ref)
    fetch(sems, 0, scr, out_hbm.at[:, 0:240, :]).wait()


def late_kernel(mine_ref, got_ref, tails_ref, in_hbm, out_hbm, scr, sems):
    del in_hbm
    chunks(scr, mine_ref, got_ref)
    tails = jnp.sum(tails_ref[...], axis=0)
    rows = piece_rows(16, 0, tails[0:1], tails[1:2]).astype(BF16)
    for i in range(16):
        scr[i, 240:256, :] = rows
    fetch(sems, 0, scr, out_hbm.at[:, 240:496, :]).wait()


def plane_kernel(in_ref, move_ref, out_ref):
    total = in_ref[0].astype(F32)
    for i in range(1, 16):
        total = total + in_ref[i].astype(F32)
    tail = total[480:496]
    sums = tail[0:1] + tail[1:2] + tail[2:3]
    errs = tail[3:4] + tail[4:5] + tail[5:6]
    rows = piece_rows(80, 60, sums, errs)
    moved = dot(move_ref[...], total[0:480].astype(BF16))
    for z in range(8):
        out_ref[z] = (moved[z * 80 : (z + 1) * 80] + rows).astype(BF16)


def depth_kernel(in_ref, out_ref, sums_ref, errs_ref):
    total = in_ref[0].astype(F32)
    for i in range(1, 8):
        total = total + in_ref[i].astype(F32)
    grads = total[0:64].astype(BF16)
    for i in range(8):
        out_ref[i] = grads
    sums_ref[...] = total[60:61] + total[61:62] + total[62:63]
    errs_ref[...] = total[63:64] + total[64:65] + total[65:66]


VM = pl.BlockSpec(memory_space=pltpu.VMEM)
HB = pl.BlockSpec(memory_space=pltpu.HBM)
DMA = pltpu.SemaphoreType.DMA


def call(kernel, outs, ins, scratch=(), flops=0, aliases=None):
    size = sum(int(np.prod(s.shape)) * s.dtype.itemsize for _, s in outs)
    size += sum(a.size * a.dtype.itemsize for _, a in ins)
    many = len(outs) > 1
    shapes, spaces = [s for _, s in outs], [p for p, _ in outs]
    return pl.pallas_call(
        kernel,
        out_shape=tuple(shapes) if many else shapes[0],
        in_specs=[p for p, _ in ins],
        out_specs=tuple(spaces) if many else spaces[0],
        scratch_shapes=list(scratch),
        input_output_aliases=aliases or {},
        compiler_params=pltpu.CompilerParams(vmem_limit_bytes=VMEM_LIMIT),
        cost_estimate=pl.CostEstimate(flops=flops, bytes_accessed=size, transcendentals=0),
    )(*[a for _, a in ins])


def sds(shape, dtype=F32):
    return jax.ShapeDtypeStruct(shape, dtype)


AXES = ("x", "c", "z", "y")


def share(rows):
    return lax.all_to_all(rows, AXES, 0, 0, tiled=True)


def widen(features, target, low, high, part):
    up = [(i, i + 1) for i in range(7)]
    down = [(i + 1, i) for i in range(7)]
    low = lax.ppermute(low, ("x", "c"), up).reshape(2, 6, COLS, C)
    high = lax.ppermute(high, ("x", "c"), down).reshape(2, 6, COLS, C)
    f = jnp.concatenate([low[:, :4], features, high[:, :4]], axis=1)
    t = jnp.concatenate([low[:, 4:], target, high[:, 4:]], axis=1)
    right = [(i, i + 1) for i in range(31)]
    left = [(i + 1, i) for i in range(31)]

    def pack(a, b):
        return jnp.concatenate([a.reshape(2, GH * 4, C), b.reshape(2, 12 * 4, C)], axis=1)

    first = lax.ppermute(pack(f[:, :, COLS - 4 :], t[:, :, COLS - 4 :]), ("z", "y"), right)
    last = lax.ppermute(pack(f[:, :, :4], t[:, :, :4]), ("z", "y"), left)

    def unpack(v):
        return v[:, : GH * 4].reshape(2, GH, 4, C), v[:, GH * 4 :].reshape(2, 12, 4, C)

    first, last, part = lax.optimization_barrier((first, last, part))
    fl, tl = unpack(first)
    fr, tr = unpack(last)
    f = jnp.concatenate([fl, f, fr], axis=2).transpose(1, 0, 2, 3).reshape(GH * LINE, C)
    t = jnp.concatenate([tl, t, tr], axis=2).transpose(1, 0, 2, 3).reshape(12 * LINE, C)
    return f, t, part


def center(values):
    return values.reshape(ROWS, 2, GW, C)[:, :, RIM : RIM + COLS].transpose(1, 0, 2, 3)


def time_embed(timestep, time_weight, time_bias):
    half = TEMB // 2
    freqs = jnp.exp(-jnp.log(10000.0) * jnp.arange(half, dtype=F32) / half)
    angles = timestep.astype(F32)[:, None] * freqs[None, :]
    emb = jnp.concatenate([jnp.cos(angles), jnp.sin(angles)], axis=1)
    return jnp.dot(jax.nn.silu(emb), time_weight.astype(F32), precision=HIGH) + time_bias


def order_matrix():
    out = np.zeros((C, C), np.float32)
    for z in range(8):
        for y in range(4):
            for j in range(10):
                out[z * 40 + y * 10 + j, y * 80 + z * 10 + j] = 1.0
    return jnp.asarray(out, BF16)


def move_matrix():
    out = np.zeros((640, 480), np.float32)
    for grad in range(2):
        for k in range(3):
            for z in range(8):
                for j in range(10):
                    out[z * 80 + grad * 30 + k * 10 + j, grad * 240 + k * 80 + z * 10 + j] = 1.0
    return jnp.asarray(out, BF16)


def swap(theirs):
    return lax.ppermute(theirs, "c", [(0, 1), (1, 0)])


def body(
    features, target, norm1_gain, norm1_shift, kernel1, bias1, time_weight, time_bias,
    norm2_gain, norm2_shift, kernel2, bias2, ref_error, preference, timestep,
):
    sign = jnp.broadcast_to(jnp.where(preference == 0, 2.0, -2.0).astype(F32), (C,))
    strip, cells = sds((2 * 6 * COLS, C), BF16), 2 * ROWS * COLS
    part, low, high = call(
        moments_kernel,
        [(VM, sds((DEVICES, 128))), (VM, strip), (VM, strip)],
        [(VM, features.reshape(cells, C)), (VM, target.reshape(cells, C))],
    )
    fx, tx, part = widen(features, target, low, high, part)
    stats1 = share(part)
    temb = time_embed(timestep, time_weight, time_bias).reshape(C)
    order, move = order_matrix(), move_matrix()
    w1, w2 = kernel1.reshape(3, 3 * C, C), kernel2.reshape(3, 3 * C, C)
    conv_flops = 2 * 9 * C * C * LINE
    half = sds((C, LANES // 2), BF16)
    row, table, lines = sds((1, 128)), sds((DEVICES, 128)), sds((ROWS * LINE, C), BF16)
    full = sds((3, 3, C, C), BF16)
    part, h1, taps1 = call(
        first_kernel,
        [(VM, table), (HB, sds((14 * LINE, C))), (HB, sds((10 * LINE, 3 * C), BF16))],
        [(HB, v) for v in (stats1, norm1_gain, norm1_shift, bias1, temb, fx, w1)],
        [
            pltpu.VMEM((GH * LINE, 3 * C), BF16), pltpu.VMEM((3, 3 * C, C), BF16),
            pltpu.VMEM((GH * LINE, C), BF16), pltpu.VMEM((14 * LINE, C), F32),
            pltpu.VMEM((DEVICES, 128), F32), *[pltpu.VMEM((C,), F32)] * 4, DMA((9,)),
        ],
        14 * conv_flops,
    )
    stats2 = share(part)
    part, errs, e2, bout, u, mine2, theirs2 = call(
        second_kernel,
        [
            (VM, table), (VM, row), (HB, sds((10 * LINE, C))), (HB, lines), (HB, lines), (HB, half), (HB, half),
        ],
        [
            (HB, v)
            for v in (stats2, norm2_gain, norm2_shift, bias2, sign, h1, w2, kernel2, fx, tx, order)
        ],
        [
            pltpu.VMEM((14 * LINE, 3 * C), BF16), pltpu.VMEM((12 * LINE, 1152), BF16),
            pltpu.VMEM((3, 3 * C, C), BF16), pltpu.VMEM(full.shape, BF16),
            pltpu.VMEM((12 * LINE, C), BF16), pltpu.VMEM((12 * LINE, C), BF16), pltpu.VMEM((C, C), BF16),
            pltpu.VMEM((ROWS * LINE, C), BF16), pltpu.VMEM((ROWS * LINE, C), BF16),
            pltpu.VMEM((C, LANES // 2), BF16), pltpu.VMEM((C, LANES // 2), BF16),
            pltpu.VMEM((14 * LINE, C), F32), pltpu.VMEM((10 * LINE, C), F32),
            pltpu.VMEM((DEVICES, 128), F32), *[pltpu.VMEM((C,), F32)] * 4, DMA((16,)),
        ],
        30 * conv_flops,
    )
    sums2 = share(part)
    got2 = swap(theirs2)
    block_out = center(bout)
    plane = call(
        early_kernel,
        [(HB, sds((16, 496, 128), BF16))],
        [(VM, mine2), (VM, got2)],
        [pltpu.VMEM((16, 240, 128), BF16), DMA((1,))],
    )
    sums2, plane = lax.optimization_barrier((sums2, plane))
    d1, mine1, theirs1 = call(
        third_kernel,
        [(HB, sds((10 * LINE, C), BF16)), (VM, half), (VM, half)],
        [(HB, v) for v in (stats2, sums2, e2, h1, taps1, order)],
        [
            pltpu.VMEM((10 * LINE, C), F32), pltpu.VMEM((10 * LINE, C), F32),
            pltpu.VMEM((10 * LINE, 3 * C), BF16), pltpu.VMEM((C, C), BF16),
            pltpu.VMEM((10 * LINE, C), BF16), *[pltpu.VMEM((DEVICES, 128), F32)] * 2, DMA((7,)),
        ],
        8 * conv_flops,
    )
    got1 = swap(theirs1)
    part, e1 = call(
        fourth_kernel,
        [(VM, row), (HB, sds((ROWS * LINE, C)))],
        [(HB, v) for v in (stats1, norm1_gain, norm1_shift, d1, fx, kernel1)],
        [
            pltpu.VMEM((10 * LINE, 1152), BF16), pltpu.VMEM((ROWS * LINE, C), BF16),
            pltpu.VMEM(full.shape, BF16), pltpu.VMEM((10 * LINE, C), BF16),
            pltpu.VMEM((ROWS * LINE, C), F32), pltpu.VMEM((DEVICES, 128), F32),
            *[pltpu.VMEM((C,), F32)] * 2, DMA((7,)),
        ],
        8 * conv_flops,
    )
    tails = lax.all_gather(jnp.concatenate([part, errs], axis=0), "c")
    plane = call(
        late_kernel,
        [(HB, sds((16, 496, 128), BF16))],
        [(VM, mine1), (VM, got1), (VM, tails), (HB, plane)],
        [pltpu.VMEM((16, 256, 128), BF16), DMA((1,))],
        0,
        {3: 0},
    )
    plane = lax.all_to_all(plane, ("x", "y"), 0, 0, tiled=True)
    depth = call(plane_kernel, [(VM, sds((8, 80, 128), BF16))], [(VM, plane), (VM, move)])
    depth = lax.all_to_all(depth, ("z",), 0, 0, tiled=True)
    copies, sums1, errs = call(
        depth_kernel, [(VM, sds((8, 64, 128), BF16)), (VM, row), (VM, row)], [(VM, depth)]
    )
    whole = lax.all_to_all(copies, ("x", "c"), 0, 0, tiled=True)
    grad, info = call(
        last_kernel,
        [(VM, lines), (VM, row)],
        [
            (VM, sums1), (VM, errs), (VM, stats1), (VM, sign), (VM, ref_error), (VM, e1), (VM, fx), (VM, u),
        ],
    )
    weight, loss = info[0, 0], jax.nn.softplus(info[0, 1])
    feature_grad = center(grad)
    scale = weight / jnp.sqrt(F32(2 * BAND_ROWS * BAND_COLS))
    whole = whole[:, :60].reshape(4, 2, 2, 3, 10, 128).transpose(2, 1, 0, 3, 5, 4).reshape(2, LANES, 10)
    whole = (whole[:, :TAPS].astype(F32) * scale).reshape(2, 3, 3, C, 10)
    return (block_out, feature_grad, whole[1], whole[0], loss)


def solution(mesh):
    fine = Mesh(mesh.devices.reshape(4, 2, 8, 4), AXES)
    cells = P(None, ("x", "c"), ("z", "y"), None)
    kernels = P(None, None, None, ("z", "y"))
    return jax.shard_map(
        body,
        mesh=fine,
        in_specs=(cells, cells) + (P(),) * 13,
        out_specs=(cells, cells, kernels, kernels, P()),
        check_vma=False,
    )
```

```python
import functools

import jax
import jax.numpy as jnp
import numpy as np
from jax import lax
from jax.experimental import pallas as pl
from jax.experimental.pallas import tpu as pltpu
from jax.sharding import Mesh
from jax.sharding import PartitionSpec as P

GROUPS = 32
TEMB = 1280
C = 320
WIDTH = C // GROUPS
ROWS, COLS = 8, 16
BAND_ROWS, BAND_COLS = 64, 512
RIM = 4
GH, GW = ROWS + 2 * RIM, COLS + 2 * RIM
LINE = 2 * GW
DEVICES = 256
LOCAL = ROWS * COLS * WIDTH
TOTAL = LOCAL * DEVICES
TAPS = 9 * C
LANES = 3072
EPS = 1e-05
F32, BF16 = jnp.float32, jnp.bfloat16
HIGH = lax.Precision.HIGHEST
VMEM_LIMIT = 63 * 2**20


def dot(a, b):
    return jnp.dot(a, b, preferred_element_type=F32)


def pieces(row):
    high = row.astype(BF16).astype(F32)
    rest = row - high
    mid = rest.astype(BF16).astype(F32)
    return high, mid, rest - mid


def hot():
    blocks = []
    for slot in range(4):
        low = (lax.broadcasted_iota(jnp.int32, (128, 384), 0) - slot * GROUPS) * WIDTH
        chan = lax.broadcasted_iota(jnp.int32, (128, 384), 1)
        blocks.append(((chan >= low) & (chan < low + WIDTH) & (chan < C)).astype(F32).astype(BF16))
    return jnp.concatenate(blocks, axis=1)


def stacked(row):
    index = lax.broadcasted_iota(jnp.int32, (16, row.shape[1]), 0)
    out = jnp.zeros((16, row.shape[1]), F32)
    for i, piece in enumerate(pieces(row)):
        out = jnp.where(index == i, piece, out)
    return out.astype(BF16)


def expand(row, table):
    wide = jnp.sum(dot(stacked(row), table), axis=0, keepdims=True)
    return [wide[:, i * 384 : i * 384 + C] for i in range(4)]


def collapse(rows, table):
    gap, empty = jnp.zeros((1, 384 - C), F32), jnp.zeros((1, C), F32)
    wide = jnp.concatenate([v for row in rows for v in (empty if row is None else row, gap)], axis=1)
    small = lax.dot_general(stacked(wide), table, (((1,), (1,)), ((), ())), preferred_element_type=F32)
    return jnp.sum(small, axis=0, keepdims=True)


def per_line(first, second):
    return jnp.concatenate(
        [jnp.broadcast_to(first, (GW, C)), jnp.broadcast_to(second, (GW, C))], axis=0
    )


def tile_lines(line, count):
    return jnp.broadcast_to(line[None], (count, LINE, C)).reshape(count * LINE, C)


def masked(values, top, count):
    high = lax.axis_index("x") * 2 + lax.axis_index("c")
    wide = lax.axis_index("z") * 4 + lax.axis_index("y")
    col = lax.broadcasted_iota(jnp.int32, (LINE, C), 0)
    gx = jnp.where(col >= GW, col - GW, col) + (wide * COLS - RIM)
    line = ((gx >= 0) & (gx < BAND_COLS)).astype(F32)
    upper = line * jnp.where(high > 0, 1.0, 0.0)
    lower = line * jnp.where(high < BAND_ROWS // ROWS - 1, 1.0, 0.0)
    parts = [(upper, RIM - top), (line, ROWS), (lower, top + count - RIM - ROWS)]
    mask = jnp.concatenate([jnp.broadcast_to(v[None], (n, LINE, C)) for v, n in parts], axis=0)
    return values * mask.reshape(count * LINE, C)


def center_line():
    col = lax.broadcasted_iota(jnp.int32, (LINE, C), 0)
    one = (col >= RIM) & (col < RIM + COLS)
    two = (col >= GW + RIM) & (col < GW + RIM + COLS)
    return one.astype(F32), two.astype(F32)


def line_sums(values):
    total = jnp.sum(values.reshape(ROWS, LINE, C), axis=0)
    return [jnp.sum(total * line, axis=0, keepdims=True) for line in center_line()]


def norm_lines(stats_ref, table):
    stats = stats_ref[...]
    sums = jnp.sum(stats, axis=0, keepdims=True)
    mean = sums * (1.0 / DEVICES)
    off = stats - mean
    spread = jnp.sum(off * off, axis=0, keepdims=True) * LOCAL
    var = (sums + pltpu.roll(spread, 64, 1)) * (1.0 / TOTAL)
    lane = lax.broadcasted_iota(jnp.int32, (1, 128), 1)
    row = jnp.where(lane < 64, mean, 1.0 / jnp.sqrt(jnp.maximum(var, 0.0) + EPS))
    one, two, three, four = expand(row, table)
    return per_line(one, two), per_line(three, four)


def moments(values, table):
    first, second = line_sums(values)
    means = collapse([first, second, None, None], table) * (1.0 / LOCAL)
    one, two, _, _ = expand(means, table)
    off = values - tile_lines(per_line(one, two), ROWS)
    first, second = line_sums(off * off)
    return means + collapse([None, None, first, second], table)


def pair_sums(scaled, normed, table):
    return collapse(line_sums(scaled) + line_sums(scaled * normed), table)


def sigmoid(v):
    return 0.5 + 0.5 * jnp.tanh(0.5 * v)


def silu_slope(v):
    sig = sigmoid(v)
    return sig * (1.0 + v * (1.0 - sig))


def spread_taps(ref, values):
    count = values.shape[0]
    ref[:, 0:C] = pltpu.roll(values, 1, 0).astype(BF16)
    ref[:, C : 2 * C] = values.astype(BF16)
    ref[:, 2 * C : 3 * C] = pltpu.roll(values, count - 1, 0).astype(BF16)


def spread_wide(ref, values):
    count = values.shape[0]
    ref[:, 0:C] = pltpu.roll(values, 1, 0).astype(BF16)
    ref[:, 384 : 384 + C] = values.astype(BF16)
    ref[:, 768 : 768 + C] = pltpu.roll(values, count - 1, 0).astype(BF16)


def conv_lines(ref, weights_ref, count):
    total = dot(ref[0 : count * LINE, :], weights_ref[0])
    for ky in range(1, 3):
        total = total + dot(ref[ky * LINE : (ky + count) * LINE, :], weights_ref[ky])
    return total


def conv_turned(ref, weights_ref, count):
    total = None
    for ky in range(3):
        for kx in range(3):
            part = lax.dot_general(
                ref[ky * LINE : (ky + count) * LINE, kx * 384 : kx * 384 + C],
                weights_ref[2 - ky, 2 - kx],
                (((1,), (1,)), ((), ())),
                preferred_element_type=F32,
            )
            total = part if total is None else total + part
    return total


def kernel_grad(mine_ref, theirs_ref, taps_ref, top, grads, order_ref):
    core = lax.axis_index("c")
    ordered = dot(grads.astype(BF16), order_ref[...])
    left = ordered.T.astype(BF16)
    parts = []
    for ky in range(3):
        lines = taps_ref[(top + ky) * LINE : (top + ky + ROWS) * LINE, :]
        parts.append(dot(left, lines).astype(BF16))
    parts.append(jnp.zeros((C, LANES - TAPS), BF16))
    whole = jnp.concatenate(parts, axis=1)
    low, high = whole[:, : LANES // 2], whole[:, LANES // 2 :]

    @pl.when(core == 0)
    def _():
        mine_ref[...] = low
        theirs_ref[...] = high

    @pl.when(core == 1)
    def _():
        mine_ref[...] = high
        theirs_ref[...] = low


def fetch(sems, index, src, dst):
    copy = pltpu.make_async_copy(src, dst, sems.at[index])
    copy.start()
    return copy


def fetch_all(sems, first, pairs):
    return [fetch(sems, first + i, src, dst) for i, (src, dst) in enumerate(pairs)]


def wait_all(copies):
    for copy in copies:
        copy.wait()


def flat(ref):
    return ref[...].reshape(1, C)


def moments_kernel(x_ref, t_ref, out_ref, low_ref, high_ref):
    half = ROWS * COLS
    for b in range(2):
        at, to = b * half, b * 6 * COLS
        low_ref[to : to + 4 * COLS] = x_ref[at + 4 * COLS : at + 8 * COLS, :]
        low_ref[to + 4 * COLS : to + 6 * COLS] = t_ref[at + 6 * COLS : at + 8 * COLS, :]
        high_ref[to : to + 4 * COLS] = x_ref[at : at + 4 * COLS, :]
        high_ref[to + 4 * COLS : to + 6 * COLS] = t_ref[at : at + 2 * COLS, :]
    table = hot()
    values = [x_ref[b * half : (b + 1) * half, :].astype(F32) for b in range(2)]
    sums = [jnp.sum(v, axis=0, keepdims=True) for v in values]
    means = collapse(sums + [None, None], table) * (1.0 / LOCAL)
    offs = [v - m for v, m in zip(values, expand(means, table))]
    sums = [jnp.sum(v * v, axis=0, keepdims=True) for v in offs]
    out = means + collapse([None, None] + sums, table)
    out_ref[...] = jnp.broadcast_to(out, (DEVICES, 128))


def strip_blocks():
    out = []
    for b in range(2):
        low, high = 512 + b * 6 * COLS, 704 + b * 6 * COLS
        for y in range(GH):
            start = low + y * COLS if y < 4 else b * 128 + (y - 4) * COLS if y < 12 else high + (y - 12) * COLS
            out.append((start, y * LINE + b * GW))
        for y in range(12):
            start = low + (4 + y) * COLS if y < 2 else 256 + b * 128 + (y - 2) * COLS if y < 10 else high + (y - 6) * COLS
            out.append((start, (GH + y) * LINE + b * GW))
    return out


def widened(scr, x_ref, t_ref, low_ref, high_ref):
    scr[0:256] = x_ref[...].astype(F32)
    scr[256:512] = t_ref[...].astype(F32)
    scr[512:704] = low_ref[...].astype(F32)
    scr[704:896] = high_ref[...].astype(F32)


def pack_kernel(x_ref, t_ref, low_ref, high_ref, right_ref, left_ref, scr, right, left):
    widened(scr, x_ref, t_ref, low_ref, high_ref)
    for i, (start, _) in enumerate(strip_blocks()):
        left[i * 4 : i * 4 + 4] = scr[start : start + 4]
        right[i * 4 : i * 4 + 4] = scr[start + COLS - 4 : start + COLS]
    right_ref[...] = right[...].astype(BF16)
    left_ref[...] = left[...].astype(BF16)


def grid_kernel(x_ref, t_ref, low_ref, high_ref, first_ref, last_ref, f_ref, g_ref, scr, first, last, grid):
    widened(scr, x_ref, t_ref, low_ref, high_ref)
    first[...] = first_ref[...].astype(F32)
    last[...] = last_ref[...].astype(F32)
    for i, (start, at) in enumerate(strip_blocks()):
        grid[at : at + RIM] = first[i * 4 : i * 4 + 4]
        grid[at + RIM : at + RIM + COLS] = scr[start : start + COLS]
        grid[at + RIM + COLS : at + GW] = last[i * 4 : i * 4 + 4]
    f_ref[...] = grid[0 : GH * LINE].astype(BF16)
    g_ref[...] = grid[GH * LINE : (GH + 12) * LINE].astype(BF16)


def first_kernel(
    stats_hbm, gain_hbm, shift_hbm, bias_hbm, temb_hbm, x_hbm, w_hbm,
    out_ref, h_hbm, taps_hbm, scr, w_ref, x_ref, h_ref, stats_ref, gain_ref, shift_ref, bias_ref, temb_ref, sems,
):
    small = fetch_all(
        sems, 4,
        [
            (stats_hbm, stats_ref), (gain_hbm, gain_ref), (shift_hbm, shift_ref),
            (bias_hbm, bias_ref), (temb_hbm, temb_ref),
        ],
    )
    xs = fetch(sems, 2, x_hbm, x_ref)
    weights = fetch(sems, 0, w_hbm, w_ref)
    table = hot()
    wait_all(small)
    mean, rstd = norm_lines(stats_ref, table)
    scale = tile_lines(rstd * flat(gain_ref), GH)
    xs.wait()
    n1 = (x_ref[...].astype(F32) - tile_lines(mean, GH)) * scale + flat(shift_ref)
    spread_taps(scr, masked(n1 * sigmoid(n1), 0, GH))
    taps = fetch(sems, 1, scr.at[3 * LINE : 13 * LINE, :], taps_hbm)
    weights.wait()
    h1 = conv_lines(scr, w_ref, GH - 2) + (flat(bias_ref) + flat(temb_ref))
    h_ref[...] = h1
    hs = fetch(sems, 3, h_ref, h_hbm)
    out_ref[...] = jnp.broadcast_to(moments(h1[3 * LINE : 11 * LINE], table), (DEVICES, 128))
    taps.wait()
    hs.wait()


def second_kernel(
    stats_hbm, gain_hbm, shift_hbm, bias_hbm, sign_hbm, h_hbm, w_hbm, wt_hbm, x_hbm, t_hbm, order_hbm,
    out_ref, err_ref, e_hbm, bout_hbm, u_hbm, mine_hbm, theirs_hbm,
    scr_a, scr_u, w_ref, wt_ref, x_ref, t_ref, order_ref, bout_ref, u_ref, mine_ref, theirs_ref, h_ref, e_ref,
    stats_ref, gain_ref, shift_ref, bias_ref, sign_ref, sems,
):
    small = fetch_all(
        sems, 11,
        [
            (stats_hbm, stats_ref), (gain_hbm, gain_ref), (shift_hbm, shift_ref),
            (bias_hbm, bias_ref), (sign_hbm, sign_ref),
        ],
    )
    hs = fetch(sems, 9, h_hbm, h_ref)
    weights = fetch(sems, 0, w_hbm, w_ref)
    xs = fetch(sems, 1, x_hbm.at[2 * LINE : 14 * LINE, :], x_ref)
    ts = fetch(sems, 2, t_hbm, t_ref)
    orders = fetch(sems, 4, order_hbm, order_ref)
    turned = fetch(sems, 3, wt_hbm, wt_ref)
    table = hot()
    wait_all(small)
    mean, rstd = norm_lines(stats_ref, table)
    hs.wait()
    nhat = (h_ref[...] - tile_lines(mean, GH - 2)) * tile_lines(rstd, GH - 2)
    n2 = nhat * flat(gain_ref) + flat(shift_ref)
    spread_taps(scr_a, masked(n2 * sigmoid(n2), 1, GH - 2))
    weights.wait()
    conv = conv_lines(scr_a, w_ref, 12) + flat(bias_ref)
    xs.wait()
    out = x_ref[...].astype(F32) + conv
    bout_ref[...] = out[2 * LINE : 10 * LINE].astype(BF16)
    bouts = fetch(sems, 5, bout_ref, bout_hbm)
    ts.wait()
    diff = out - t_ref[...].astype(F32)
    mid = diff[2 * LINE : 10 * LINE]
    lane = lax.broadcasted_iota(jnp.int32, (1, 128), 1)
    errs = jnp.zeros((1, 128), F32)
    for b, part in enumerate(line_sums(mid * mid)):
        errs = errs + jnp.where(lane == b, jnp.sum(part, axis=1, keepdims=True), 0.0)
    err_ref[...] = errs
    sign = tile_lines(per_line(flat(sign_ref), -flat(sign_ref)), 12)
    u = masked(diff * sign, 2, 12)
    spread_wide(scr_u, u)
    center = u[2 * LINE : 10 * LINE]
    u_ref[...] = center.astype(BF16)
    us = fetch(sems, 6, u_ref, u_hbm)
    one, two = center_line()
    orders.wait()
    kernel_grad(mine_ref, theirs_ref, scr_a, 2, center * tile_lines(one + two, ROWS), order_ref)
    mines = fetch(sems, 7, mine_ref, mine_hbm)
    others = fetch(sems, 8, theirs_ref, theirs_hbm)
    turned.wait()
    da2 = conv_turned(scr_u, wt_ref, 10)
    e = da2 * silu_slope(n2[2 * LINE : 12 * LINE]) * flat(gain_ref)
    e_ref[...] = e
    es = fetch(sems, 10, e_ref, e_hbm)
    sums = pair_sums(e[LINE : 9 * LINE], nhat[3 * LINE : 11 * LINE], table)
    out_ref[...] = jnp.broadcast_to(sums, (DEVICES, 128))
    for copy in (bouts, us, mines, others, es):
        copy.wait()


def back_line(sums_ref, table):
    sums = jnp.sum(sums_ref[...], axis=0, keepdims=True) * (1.0 / TOTAL)
    one, two, three, four = expand(sums, table)
    return per_line(one, two), per_line(three, four)


def third_kernel(
    stats_hbm, sums_hbm, e_hbm, h_hbm, taps_hbm, order_hbm,
    d_hbm, mine_ref, theirs_ref, e_ref, h_ref, taps_ref, order_ref, d_ref, stats_ref, sums_ref, sems,
):
    small = fetch_all(sems, 5, [(stats_hbm, stats_ref), (sums_hbm, sums_ref)])
    hs = fetch(sems, 0, h_hbm.at[2 * LINE : 12 * LINE, :], h_ref)
    es = fetch(sems, 3, e_hbm, e_ref)
    orders = fetch(sems, 1, order_hbm, order_ref)
    taps = fetch(sems, 2, taps_hbm, taps_ref)
    table = hot()
    wait_all(small)
    mean, rstd = norm_lines(stats_ref, table)
    first, second = back_line(sums_ref, table)
    scale = tile_lines(rstd, 10)
    hs.wait()
    es.wait()
    nhat = (h_ref[...] - tile_lines(mean, 10)) * scale
    dh = scale * (e_ref[...] - tile_lines(first, 10) - nhat * tile_lines(second, 10))
    dh = masked(dh, 3, 10)
    d_ref[...] = dh.astype(BF16)
    ds = fetch(sems, 4, d_ref, d_hbm)
    one, two = center_line()
    orders.wait()
    taps.wait()
    kernel_grad(mine_ref, theirs_ref, taps_ref, 0, dh[LINE : 9 * LINE] * tile_lines(one + two, ROWS), order_ref)
    ds.wait()


def fourth_kernel(
    stats_hbm, gain_hbm, shift_hbm, errs_hbm, d_hbm, x_hbm, wt_hbm,
    out_ref, e_hbm, scr, x_ref, wt_ref, d_ref, e_ref, stats_ref, gain_ref, shift_ref, errs_ref, sems,
):
    ds = fetch(sems, 2, d_hbm, d_ref)
    small = fetch_all(
        sems, 4,
        [(stats_hbm, stats_ref), (gain_hbm, gain_ref), (shift_hbm, shift_ref), (errs_hbm, errs_ref)],
    )
    xs = fetch(sems, 1, x_hbm.at[4 * LINE : 12 * LINE, :], x_ref)
    turned = fetch(sems, 0, wt_hbm, wt_ref)
    table = hot()
    wait_all(small)
    mean, rstd = norm_lines(stats_ref, table)
    ds.wait()
    spread_wide(scr, d_ref[...].astype(F32))
    xs.wait()
    nhat = (x_ref[...].astype(F32) - tile_lines(mean, ROWS)) * tile_lines(rstd, ROWS)
    n1 = nhat * flat(gain_ref) + flat(shift_ref)
    slope = silu_slope(n1) * flat(gain_ref)
    turned.wait()
    e1 = conv_turned(scr, wt_ref, ROWS) * slope
    e_ref[...] = e1
    es = fetch(sems, 3, e_ref, e_hbm)
    out_ref[0:1] = pair_sums(e1, nhat, table)
    out_ref[1:2] = errs_ref[...]
    es.wait()


def last_kernel(sums_ref, info_ref, stats_ref, e_ref, x_ref, u_ref, out_ref):
    weight = info_ref[0:1, 0:1]
    table = hot()
    mean, rstd = norm_lines(stats_ref, table)
    first, second = back_line(sums_ref, table)
    scale = tile_lines(rstd, ROWS)
    nhat = (x_ref[4 * LINE : 12 * LINE, :].astype(F32) - tile_lines(mean, ROWS)) * scale
    dx = scale * (e_ref[...] - tile_lines(first, ROWS) - nhat * tile_lines(second, ROWS))
    out_ref[...] = ((u_ref[...].astype(F32) + dx) * weight).astype(BF16)


def piece_rows(count, at, sums, errs):
    index = lax.broadcasted_iota(jnp.int32, (count, 128), 0)
    out = jnp.zeros((count, 128), F32)
    for i, piece in enumerate(pieces(sums) + pieces(errs)):
        out = out + jnp.where(index == at + i, piece, 0.0)
    return out


def chunks(out_ref, mine_ref, got_ref):
    for j in range(4):
        for i in range(4):
            for k in range(3):
                rows = slice(j * 80, (j + 1) * 80)
                lanes = slice(i * 384 + k * 128, i * 384 + (k + 1) * 128)
                both = mine_ref[rows, lanes].astype(F32) + got_ref[rows, lanes].astype(F32)
                out_ref[i * 4 + j, k * 80 : (k + 1) * 80, :] = both.astype(BF16)


def early_kernel(mine_ref, got_ref, out_hbm, scr, sems):
    chunks(scr, mine_ref, got_ref)
    fetch(sems, 0, scr, out_hbm.at[:, 0:240, :]).wait()


def late_kernel(mine_ref, got_ref, tails_ref, in_hbm, out_hbm, scr, sems):
    del in_hbm
    chunks(scr, mine_ref, got_ref)
    tails = jnp.sum(tails_ref[...], axis=0)
    rows = piece_rows(16, 0, tails[0:1], tails[1:2]).astype(BF16)
    for i in range(16):
        scr[i, 240:256, :] = rows
    fetch(sems, 0, scr, out_hbm.at[:, 240:496, :]).wait()


def plane_kernel(in_ref, move_ref, out_ref):
    total = in_ref[0].astype(F32)
    for i in range(1, 16):
        total = total + in_ref[i].astype(F32)
    tail = total[480:496]
    sums = tail[0:1] + tail[1:2] + tail[2:3]
    errs = tail[3:4] + tail[4:5] + tail[5:6]
    rows = piece_rows(80, 60, sums, errs)
    moved = dot(move_ref[...], total[0:480].astype(BF16))
    for z in range(8):
        out_ref[z] = (moved[z * 80 : (z + 1) * 80] + rows).astype(BF16)


def depth_kernel(in_ref, sign_ref, ref_ref, out_ref, sums_ref, info_ref):
    total = in_ref[0].astype(F32)
    for i in range(1, 8):
        total = total + in_ref[i].astype(F32)
    sums_ref[...] = total[60:61] + total[61:62] + total[62:63]
    errs = total[63:64] + total[64:65] + total[65:66]
    excess = errs[:, 0:2] * (1.0 / (BAND_ROWS * BAND_COLS * C)) - ref_ref[...]
    gap = 0.5 * flat(sign_ref)[:, 0:1] * (excess[:, 0:1] - excess[:, 1:2])
    weight = 1.0 / (1.0 + jnp.exp(-gap))
    loss = jnp.maximum(gap, 0.0) + jnp.log1p(jnp.exp(-jnp.abs(gap)))
    lane = lax.broadcasted_iota(jnp.int32, (1, 128), 1)
    info_ref[...] = jnp.where(lane == 0, weight, loss)
    grads = (total[0:64] * (weight * (2 * BAND_ROWS * BAND_COLS) ** -0.5)).astype(BF16)
    for i in range(8):
        out_ref[i] = grads


VM = pl.BlockSpec(memory_space=pltpu.VMEM)
HB = pl.BlockSpec(memory_space=pltpu.HBM)
DMA = pltpu.SemaphoreType.DMA


def call(kernel, outs, ins, scratch=(), flops=0, aliases=None):
    size = sum(int(np.prod(s.shape)) * s.dtype.itemsize for _, s in outs)
    size += sum(a.size * a.dtype.itemsize for _, a in ins)
    many = len(outs) > 1
    shapes, spaces = [s for _, s in outs], [p for p, _ in outs]
    return pl.pallas_call(
        kernel,
        out_shape=tuple(shapes) if many else shapes[0],
        in_specs=[p for p, _ in ins],
        out_specs=tuple(spaces) if many else spaces[0],
        scratch_shapes=list(scratch),
        input_output_aliases=aliases or {},
        compiler_params=pltpu.CompilerParams(vmem_limit_bytes=VMEM_LIMIT),
        cost_estimate=pl.CostEstimate(flops=flops, bytes_accessed=size, transcendentals=0),
    )(*[a for _, a in ins])


def sds(shape, dtype=F32):
    return jax.ShapeDtypeStruct(shape, dtype)


AXES = ("x", "c", "z", "y")


def share(rows):
    return lax.all_to_all(rows, AXES, 0, 0, tiled=True)


def widen(features, target, low, high, part):
    up = [(i, i + 1) for i in range(7)]
    down = [(i + 1, i) for i in range(7)]
    low = lax.ppermute(low, ("x", "c"), up)
    high = lax.ppermute(high, ("x", "c"), down)
    low, high, part = lax.optimization_barrier((low, high, part))
    strip, wide = sds((224, C), BF16), pltpu.VMEM((896, C), F32)
    edge = pltpu.VMEM((224, C), F32)
    ins = [(VM, features), (VM, target), (VM, low), (VM, high)]
    right, left = call(pack_kernel, [(VM, strip), (VM, strip)], ins, [wide, edge, edge])
    first = lax.ppermute(right, ("z", "y"), [(i, i + 1) for i in range(31)])
    last = lax.ppermute(left, ("z", "y"), [(i + 1, i) for i in range(31)])
    f, t = call(
        grid_kernel,
        [(VM, sds((GH * LINE, C), BF16)), (VM, sds((12 * LINE, C), BF16))],
        ins + [(VM, first), (VM, last)],
        [wide, edge, edge, pltpu.VMEM(((GH + 12) * LINE, C), F32)],
    )
    return f, t, part


def center(values):
    return values.reshape(ROWS, 2, GW, C)[:, :, RIM : RIM + COLS].transpose(1, 0, 2, 3)


def time_embed(timestep, time_weight, time_bias):
    half = TEMB // 2
    freqs = jnp.exp(-jnp.log(10000.0) * jnp.arange(half, dtype=F32) / half)
    angles = timestep.astype(F32)[:, None] * freqs[None, :]
    emb = jnp.concatenate([jnp.cos(angles), jnp.sin(angles)], axis=1)
    return jnp.dot(jax.nn.silu(emb), time_weight.astype(F32), precision=HIGH) + time_bias


def order_matrix():
    out = np.zeros((C, C), np.float32)
    for z in range(8):
        for y in range(4):
            for j in range(10):
                out[z * 40 + y * 10 + j, y * 80 + z * 10 + j] = 1.0
    return jnp.asarray(out, BF16)


def move_matrix():
    out = np.zeros((640, 480), np.float32)
    for grad in range(2):
        for k in range(3):
            for z in range(8):
                for j in range(10):
                    out[z * 80 + grad * 30 + k * 10 + j, grad * 240 + k * 80 + z * 10 + j] = 1.0
    return jnp.asarray(out, BF16)


def swap(theirs):
    return lax.ppermute(theirs, "c", [(0, 1), (1, 0)])


def body(
    features, target, norm1_gain, norm1_shift, kernel1, bias1, time_weight, time_bias,
    norm2_gain, norm2_shift, kernel2, bias2, ref_error, preference, timestep,
):
    sign = jnp.broadcast_to(jnp.where(preference == 0, 2.0, -2.0).astype(F32), (C,))
    strip, cells = sds((2 * 6 * COLS, C), BF16), 2 * ROWS * COLS
    part, low, high = call(
        moments_kernel,
        [(VM, sds((DEVICES, 128))), (VM, strip), (VM, strip)],
        [(VM, features.reshape(cells, C)), (VM, target.reshape(cells, C))],
    )
    fx, tx, part = widen(features.reshape(cells, C), target.reshape(cells, C), low, high, part)
    stats1 = share(part)
    temb = time_embed(timestep, time_weight, time_bias).reshape(C)
    order, move = order_matrix(), move_matrix()
    w1, w2 = kernel1.reshape(3, 3 * C, C), kernel2.reshape(3, 3 * C, C)
    conv_flops = 2 * 9 * C * C * LINE
    half = sds((C, LANES // 2), BF16)
    row, table, lines = sds((1, 128)), sds((DEVICES, 128)), sds((ROWS * LINE, C), BF16)
    full = sds((3, 3, C, C), BF16)
    part, h1, taps1 = call(
        first_kernel,
        [(VM, table), (HB, sds((14 * LINE, C))), (HB, sds((10 * LINE, 3 * C), BF16))],
        [(HB, v) for v in (stats1, norm1_gain, norm1_shift, bias1, temb, fx, w1)],
        [
            pltpu.VMEM((GH * LINE, 3 * C), BF16), pltpu.VMEM((3, 3 * C, C), BF16),
            pltpu.VMEM((GH * LINE, C), BF16), pltpu.VMEM((14 * LINE, C), F32),
            pltpu.VMEM((DEVICES, 128), F32), *[pltpu.VMEM((C,), F32)] * 4, DMA((9,)),
        ],
        14 * conv_flops,
    )
    stats2 = share(part)
    part, errs, e2, bout, u, mine2, theirs2 = call(
        second_kernel,
        [
            (VM, table), (VM, row), (HB, sds((10 * LINE, C))), (HB, lines), (HB, lines), (HB, half), (HB, half),
        ],
        [
            (HB, v)
            for v in (stats2, norm2_gain, norm2_shift, bias2, sign, h1, w2, kernel2, fx, tx, order)
        ],
        [
            pltpu.VMEM((14 * LINE, 3 * C), BF16), pltpu.VMEM((12 * LINE, 1152), BF16),
            pltpu.VMEM((3, 3 * C, C), BF16), pltpu.VMEM(full.shape, BF16),
            pltpu.VMEM((12 * LINE, C), BF16), pltpu.VMEM((12 * LINE, C), BF16), pltpu.VMEM((C, C), BF16),
            pltpu.VMEM((ROWS * LINE, C), BF16), pltpu.VMEM((ROWS * LINE, C), BF16),
            pltpu.VMEM((C, LANES // 2), BF16), pltpu.VMEM((C, LANES // 2), BF16),
            pltpu.VMEM((14 * LINE, C), F32), pltpu.VMEM((10 * LINE, C), F32),
            pltpu.VMEM((DEVICES, 128), F32), *[pltpu.VMEM((C,), F32)] * 4, DMA((16,)),
        ],
        30 * conv_flops,
    )
    sums2 = share(part)
    got2 = swap(theirs2)
    block_out = center(bout)
    plane = call(
        early_kernel,
        [(HB, sds((16, 496, 128), BF16))],
        [(VM, mine2), (VM, got2)],
        [pltpu.VMEM((16, 240, 128), BF16), DMA((1,))],
    )
    sums2, plane = lax.optimization_barrier((sums2, plane))
    d1, mine1, theirs1 = call(
        third_kernel,
        [(HB, sds((10 * LINE, C), BF16)), (VM, half), (VM, half)],
        [(HB, v) for v in (stats2, sums2, e2, h1, taps1, order)],
        [
            pltpu.VMEM((10 * LINE, C), F32), pltpu.VMEM((10 * LINE, C), F32),
            pltpu.VMEM((10 * LINE, 3 * C), BF16), pltpu.VMEM((C, C), BF16),
            pltpu.VMEM((10 * LINE, C), BF16), *[pltpu.VMEM((DEVICES, 128), F32)] * 2, DMA((7,)),
        ],
        8 * conv_flops,
    )
    got1 = swap(theirs1)
    part, e1 = call(
        fourth_kernel,
        [(VM, sds((2, 128))), (HB, sds((ROWS * LINE, C)))],
        [(HB, v) for v in (stats1, norm1_gain, norm1_shift, errs, d1, fx, kernel1)],
        [
            pltpu.VMEM((10 * LINE, 1152), BF16), pltpu.VMEM((ROWS * LINE, C), BF16),
            pltpu.VMEM(full.shape, BF16), pltpu.VMEM((10 * LINE, C), BF16),
            pltpu.VMEM((ROWS * LINE, C), F32), pltpu.VMEM((DEVICES, 128), F32),
            *[pltpu.VMEM((C,), F32)] * 2, pltpu.VMEM((1, 128), F32), DMA((8,)),
        ],
        8 * conv_flops,
    )
    tails = lax.all_gather(part, "c")
    plane = call(
        late_kernel,
        [(HB, sds((16, 496, 128), BF16))],
        [(VM, mine1), (VM, got1), (VM, tails), (HB, plane)],
        [pltpu.VMEM((16, 256, 128), BF16), DMA((1,))],
        0,
        {3: 0},
    )
    plane = lax.all_to_all(plane, ("x", "y"), 0, 0, tiled=True)
    depth = call(plane_kernel, [(VM, sds((8, 80, 128), BF16))], [(VM, plane), (VM, move)])
    depth = lax.all_to_all(depth, ("z",), 0, 0, tiled=True)
    copies, sums1, info = call(
        depth_kernel,
        [(VM, sds((8, 64, 128), BF16)), (VM, row), (VM, row)],
        [(VM, depth), (VM, sign), (VM, ref_error)],
    )
    whole = lax.all_to_all(copies, ("x", "c"), 0, 0, tiled=True)
    grad = call(
        last_kernel,
        [(VM, lines)],
        [(VM, sums1), (VM, info), (VM, stats1), (VM, e1), (VM, fx), (VM, u)],
    )
    feature_grad = center(grad)
    whole = whole[:, :60].reshape(4, 2, 2, 3, 10, 128).transpose(2, 1, 0, 3, 5, 4).reshape(2, LANES, 10)
    whole = whole[:, :TAPS].astype(F32).reshape(2, 3, 3, C, 10)
    loss = info[0, 1]
    return (block_out, feature_grad, whole[1], whole[0], loss)


def solution(mesh):
    fine = Mesh(mesh.devices.reshape(4, 2, 8, 4), AXES)
    cells = P(None, ("x", "c"), ("z", "y"), None)
    kernels = P(None, None, None, ("z", "y"))
    return jax.shard_map(
        body,
        mesh=fine,
        in_specs=(cells, cells) + (P(),) * 13,
        out_specs=(cells, cells, kernels, kernels, P()),
        check_vma=False,
    )
```

```python
import functools

import jax
import jax.numpy as jnp
import numpy as np
from jax import lax
from jax.experimental import pallas as pl
from jax.experimental.pallas import tpu as pltpu
from jax.sharding import Mesh
from jax.sharding import PartitionSpec as P

GROUPS = 32
TEMB = 1280
C = 320
WIDTH = C // GROUPS
ROWS, COLS = 8, 16
BAND_ROWS, BAND_COLS = 64, 512
RIM = 4
GH, GW = ROWS + 2 * RIM, COLS + 2 * RIM
LINE = 2 * GW
DEVICES = 256
LOCAL = ROWS * COLS * WIDTH
TOTAL = LOCAL * DEVICES
TAPS = 9 * C
LANES = 3072
EPS = 1e-05
F32, BF16 = jnp.float32, jnp.bfloat16
HIGH = lax.Precision.HIGHEST
VMEM_LIMIT = 63 * 2**20


def dot(a, b):
    return jnp.dot(a, b, preferred_element_type=F32)


def pieces(row):
    high = row.astype(BF16).astype(F32)
    rest = row - high
    mid = rest.astype(BF16).astype(F32)
    return high, mid, rest - mid


def hot():
    blocks = []
    for slot in range(4):
        low = (lax.broadcasted_iota(jnp.int32, (128, 384), 0) - slot * GROUPS) * WIDTH
        chan = lax.broadcasted_iota(jnp.int32, (128, 384), 1)
        blocks.append(((chan >= low) & (chan < low + WIDTH) & (chan < C)).astype(F32).astype(BF16))
    return jnp.concatenate(blocks, axis=1)


def stacked(row):
    index = lax.broadcasted_iota(jnp.int32, (16, row.shape[1]), 0)
    out = jnp.zeros((16, row.shape[1]), F32)
    for i, piece in enumerate(pieces(row)):
        out = jnp.where(index == i, piece, out)
    return out.astype(BF16)


def expand(row, table):
    wide = jnp.sum(dot(stacked(row), table), axis=0, keepdims=True)
    return [wide[:, i * 384 : i * 384 + C] for i in range(4)]


def collapse(rows, table):
    gap, empty = jnp.zeros((1, 384 - C), F32), jnp.zeros((1, C), F32)
    wide = jnp.concatenate([v for row in rows for v in (empty if row is None else row, gap)], axis=1)
    small = lax.dot_general(stacked(wide), table, (((1,), (1,)), ((), ())), preferred_element_type=F32)
    return jnp.sum(small, axis=0, keepdims=True)


def per_line(first, second):
    return jnp.concatenate(
        [jnp.broadcast_to(first, (GW, C)), jnp.broadcast_to(second, (GW, C))], axis=0
    )


def tile_lines(line, count):
    return jnp.broadcast_to(line[None], (count, LINE, C)).reshape(count * LINE, C)


def masked(values, top, count):
    high = lax.axis_index("x") * 2 + lax.axis_index("c")
    wide = lax.axis_index("z") * 4 + lax.axis_index("y")
    col = lax.broadcasted_iota(jnp.int32, (LINE, C), 0)
    gx = jnp.where(col >= GW, col - GW, col) + (wide * COLS - RIM)
    line = ((gx >= 0) & (gx < BAND_COLS)).astype(F32)
    upper = line * jnp.where(high > 0, 1.0, 0.0)
    lower = line * jnp.where(high < BAND_ROWS // ROWS - 1, 1.0, 0.0)
    parts = [(upper, RIM - top), (line, ROWS), (lower, top + count - RIM - ROWS)]
    mask = jnp.concatenate([jnp.broadcast_to(v[None], (n, LINE, C)) for v, n in parts], axis=0)
    return values * mask.reshape(count * LINE, C)


def center_line():
    col = lax.broadcasted_iota(jnp.int32, (LINE, C), 0)
    one = (col >= RIM) & (col < RIM + COLS)
    two = (col >= GW + RIM) & (col < GW + RIM + COLS)
    return one.astype(F32), two.astype(F32)


def line_sums(values):
    total = jnp.sum(values.reshape(ROWS, LINE, C), axis=0)
    return [jnp.sum(total * line, axis=0, keepdims=True) for line in center_line()]


def norm_lines(stats_ref, table):
    stats = stats_ref[...]
    sums = jnp.sum(stats, axis=0, keepdims=True)
    mean = sums * (1.0 / DEVICES)
    off = stats - mean
    spread = jnp.sum(off * off, axis=0, keepdims=True) * LOCAL
    var = (sums + pltpu.roll(spread, 64, 1)) * (1.0 / TOTAL)
    lane = lax.broadcasted_iota(jnp.int32, (1, 128), 1)
    row = jnp.where(lane < 64, mean, 1.0 / jnp.sqrt(jnp.maximum(var, 0.0) + EPS))
    one, two, three, four = expand(row, table)
    return per_line(one, two), per_line(three, four)


def moments(values, table):
    first, second = line_sums(values)
    means = collapse([first, second, None, None], table) * (1.0 / LOCAL)
    one, two, _, _ = expand(means, table)
    off = values - tile_lines(per_line(one, two), ROWS)
    first, second = line_sums(off * off)
    return means + collapse([None, None, first, second], table)


def pair_sums(scaled, normed, table):
    return collapse(line_sums(scaled) + line_sums(scaled * normed), table)


def sigmoid(v):
    return 0.5 + 0.5 * jnp.tanh(0.5 * v)


def silu_slope(v):
    sig = sigmoid(v)
    return sig * (1.0 + v * (1.0 - sig))


def spread_taps(ref, values):
    count = values.shape[0]
    ref[:, 0:C] = pltpu.roll(values, 1, 0).astype(BF16)
    ref[:, C : 2 * C] = values.astype(BF16)
    ref[:, 2 * C : 3 * C] = pltpu.roll(values, count - 1, 0).astype(BF16)


def spread_wide(ref, values):
    count = values.shape[0]
    ref[:, 0:C] = pltpu.roll(values, 1, 0).astype(BF16)
    ref[:, 384 : 384 + C] = values.astype(BF16)
    ref[:, 768 : 768 + C] = pltpu.roll(values, count - 1, 0).astype(BF16)


def conv_lines(ref, weights_ref, count):
    total = dot(ref[0 : count * LINE, :], weights_ref[0])
    for ky in range(1, 3):
        total = total + dot(ref[ky * LINE : (ky + count) * LINE, :], weights_ref[ky])
    return total


def conv_turned(ref, weights_ref, count):
    total = None
    for ky in range(3):
        for kx in range(3):
            part = lax.dot_general(
                ref[ky * LINE : (ky + count) * LINE, kx * 384 : kx * 384 + C],
                weights_ref[2 - ky, 2 - kx],
                (((1,), (1,)), ((), ())),
                preferred_element_type=F32,
            )
            total = part if total is None else total + part
    return total


def kernel_grad(mine_ref, theirs_ref, taps_ref, top, grads, order_ref):
    core = lax.axis_index("c")
    ordered = dot(grads.astype(BF16), order_ref[...])
    left = ordered.T.astype(BF16)
    parts = []
    for ky in range(3):
        lines = taps_ref[(top + ky) * LINE : (top + ky + ROWS) * LINE, :]
        parts.append(dot(left, lines).astype(BF16))
    parts.append(jnp.zeros((C, LANES - TAPS), BF16))
    whole = jnp.concatenate(parts, axis=1)
    low, high = whole[:, : LANES // 2], whole[:, LANES // 2 :]

    @pl.when(core == 0)
    def _():
        mine_ref[...] = low
        theirs_ref[...] = high

    @pl.when(core == 1)
    def _():
        mine_ref[...] = high
        theirs_ref[...] = low


def fetch(sems, index, src, dst):
    copy = pltpu.make_async_copy(src, dst, sems.at[index])
    copy.start()
    return copy


def fetch_all(sems, first, pairs):
    return [fetch(sems, first + i, src, dst) for i, (src, dst) in enumerate(pairs)]


def wait_all(copies):
    for copy in copies:
        copy.wait()


def flat(ref):
    return ref[...].reshape(1, C)


def moments_kernel(x_ref, t_ref, out_ref, low_ref, high_ref):
    half = ROWS * COLS
    for b in range(2):
        at, to = b * half, b * 6 * COLS
        low_ref[to : to + 4 * COLS] = x_ref[at + 4 * COLS : at + 8 * COLS, :]
        low_ref[to + 4 * COLS : to + 6 * COLS] = t_ref[at + 6 * COLS : at + 8 * COLS, :]
        high_ref[to : to + 4 * COLS] = x_ref[at : at + 4 * COLS, :]
        high_ref[to + 4 * COLS : to + 6 * COLS] = t_ref[at : at + 2 * COLS, :]
    table = hot()
    values = [x_ref[b * half : (b + 1) * half, :].astype(F32) for b in range(2)]
    sums = [jnp.sum(v, axis=0, keepdims=True) for v in values]
    means = collapse(sums + [None, None], table) * (1.0 / LOCAL)
    offs = [v - m for v, m in zip(values, expand(means, table))]
    sums = [jnp.sum(v * v, axis=0, keepdims=True) for v in offs]
    out = means + collapse([None, None] + sums, table)
    out_ref[...] = jnp.broadcast_to(out, (DEVICES, 128))


def strip_blocks():
    out = []
    for b in range(2):
        low, high = 512 + b * 6 * COLS, 704 + b * 6 * COLS
        for y in range(GH):
            start = low + y * COLS if y < 4 else b * 128 + (y - 4) * COLS if y < 12 else high + (y - 12) * COLS
            out.append((start, y * LINE + b * GW))
        for y in range(12):
            start = low + (4 + y) * COLS if y < 2 else 256 + b * 128 + (y - 2) * COLS if y < 10 else high + (y - 6) * COLS
            out.append((start, (GH + y) * LINE + b * GW))
    return out


def widened(scr, x_ref, t_ref, low_ref, high_ref):
    scr[0:256] = x_ref[...].astype(F32)
    scr[256:512] = t_ref[...].astype(F32)
    scr[512:704] = low_ref[...].astype(F32)
    scr[704:896] = high_ref[...].astype(F32)


def pack_kernel(x_ref, t_ref, low_ref, high_ref, right_ref, left_ref, scr, right, left):
    widened(scr, x_ref, t_ref, low_ref, high_ref)
    for i, (start, _) in enumerate(strip_blocks()):
        left[i * 4 : i * 4 + 4] = scr[start : start + 4]
        right[i * 4 : i * 4 + 4] = scr[start + COLS - 4 : start + COLS]
    right_ref[...] = right[...].astype(BF16)
    left_ref[...] = left[...].astype(BF16)


def grid_kernel(x_ref, t_ref, low_ref, high_ref, first_ref, last_ref, f_ref, g_ref, scr, first, last, grid):
    widened(scr, x_ref, t_ref, low_ref, high_ref)
    first[...] = first_ref[...].astype(F32)
    last[...] = last_ref[...].astype(F32)
    for i, (start, at) in enumerate(strip_blocks()):
        grid[at : at + RIM] = first[i * 4 : i * 4 + 4]
        grid[at + RIM : at + RIM + COLS] = scr[start : start + COLS]
        grid[at + RIM + COLS : at + GW] = last[i * 4 : i * 4 + 4]
    f_ref[...] = grid[0 : GH * LINE].astype(BF16)
    g_ref[...] = grid[GH * LINE : (GH + 12) * LINE].astype(BF16)


def first_kernel(
    stats_hbm, gain_hbm, shift_hbm, bias_hbm, temb_hbm, x_hbm, w_hbm,
    out_ref, h_hbm, taps_hbm, scr, w_ref, x_ref, h_ref, stats_ref, gain_ref, shift_ref, bias_ref, temb_ref, sems,
):
    small = fetch_all(
        sems, 4,
        [
            (stats_hbm, stats_ref), (gain_hbm, gain_ref), (shift_hbm, shift_ref),
            (bias_hbm, bias_ref), (temb_hbm, temb_ref),
        ],
    )
    xs = fetch(sems, 2, x_hbm, x_ref)
    weights = fetch(sems, 0, w_hbm, w_ref)
    table = hot()
    wait_all(small)
    mean, rstd = norm_lines(stats_ref, table)
    scale = tile_lines(rstd * flat(gain_ref), GH)
    xs.wait()
    n1 = (x_ref[...].astype(F32) - tile_lines(mean, GH)) * scale + flat(shift_ref)
    spread_taps(scr, masked(n1 * sigmoid(n1), 0, GH))
    taps = fetch(sems, 1, scr.at[3 * LINE : 13 * LINE, :], taps_hbm)
    weights.wait()
    h1 = conv_lines(scr, w_ref, GH - 2) + (flat(bias_ref) + flat(temb_ref))
    h_ref[...] = h1
    hs = fetch(sems, 3, h_ref, h_hbm)
    out_ref[...] = jnp.broadcast_to(moments(h1[3 * LINE : 11 * LINE], table), (DEVICES, 128))
    taps.wait()
    hs.wait()


def second_kernel(
    stats_hbm, gain_hbm, shift_hbm, bias_hbm, sign_hbm, h_hbm, w_hbm, wt_hbm, x_hbm, t_hbm, order_hbm,
    out_ref, err_ref, e_hbm, bout_hbm, u_hbm, mine_hbm, theirs_hbm,
    scr_a, scr_u, w_ref, wt_ref, x_ref, t_ref, order_ref, bout_ref, u_ref, mine_ref, theirs_ref, h_ref, e_ref,
    stats_ref, gain_ref, shift_ref, bias_ref, sign_ref, sems,
):
    small = fetch_all(
        sems, 11,
        [
            (stats_hbm, stats_ref), (gain_hbm, gain_ref), (shift_hbm, shift_ref),
            (bias_hbm, bias_ref), (sign_hbm, sign_ref),
        ],
    )
    hs = fetch(sems, 9, h_hbm, h_ref)
    weights = fetch(sems, 0, w_hbm, w_ref)
    xs = fetch(sems, 1, x_hbm.at[2 * LINE : 14 * LINE, :], x_ref)
    ts = fetch(sems, 2, t_hbm, t_ref)
    orders = fetch(sems, 4, order_hbm, order_ref)
    turned = fetch(sems, 3, wt_hbm, wt_ref)
    table = hot()
    wait_all(small)
    mean, rstd = norm_lines(stats_ref, table)
    hs.wait()
    nhat = (h_ref[...] - tile_lines(mean, GH - 2)) * tile_lines(rstd, GH - 2)
    n2 = nhat * flat(gain_ref) + flat(shift_ref)
    spread_taps(scr_a, masked(n2 * sigmoid(n2), 1, GH - 2))
    weights.wait()
    conv = conv_lines(scr_a, w_ref, 12) + flat(bias_ref)
    xs.wait()
    out = x_ref[...].astype(F32) + conv
    bout_ref[...] = out[2 * LINE : 10 * LINE].astype(BF16)
    bouts = fetch(sems, 5, bout_ref, bout_hbm)
    ts.wait()
    diff = out - t_ref[...].astype(F32)
    mid = diff[2 * LINE : 10 * LINE]
    lane = lax.broadcasted_iota(jnp.int32, (1, 128), 1)
    errs = jnp.zeros((1, 128), F32)
    for b, part in enumerate(line_sums(mid * mid)):
        errs = errs + jnp.where(lane == b, jnp.sum(part, axis=1, keepdims=True), 0.0)
    err_ref[...] = errs
    sign = tile_lines(per_line(flat(sign_ref), -flat(sign_ref)), 12)
    u = masked(diff * sign, 2, 12)
    spread_wide(scr_u, u)
    center = u[2 * LINE : 10 * LINE]
    u_ref[...] = center.astype(BF16)
    us = fetch(sems, 6, u_ref, u_hbm)
    one, two = center_line()
    orders.wait()
    kernel_grad(mine_ref, theirs_ref, scr_a, 2, center * tile_lines(one + two, ROWS), order_ref)
    mines = fetch(sems, 7, mine_ref, mine_hbm)
    others = fetch(sems, 8, theirs_ref, theirs_hbm)
    turned.wait()
    da2 = conv_turned(scr_u, wt_ref, 10)
    e = da2 * silu_slope(n2[2 * LINE : 12 * LINE]) * flat(gain_ref)
    e_ref[...] = e
    es = fetch(sems, 10, e_ref, e_hbm)
    sums = pair_sums(e[LINE : 9 * LINE], nhat[3 * LINE : 11 * LINE], table)
    out_ref[...] = jnp.broadcast_to(sums, (DEVICES, 128))
    for copy in (bouts, us, mines, others, es):
        copy.wait()


def back_line(sums_ref, table):
    sums = jnp.sum(sums_ref[...], axis=0, keepdims=True) * (1.0 / TOTAL)
    one, two, three, four = expand(sums, table)
    return per_line(one, two), per_line(three, four)


def third_kernel(
    stats_hbm, sums_hbm, first_hbm, gain_hbm, shift_hbm, errs_hbm, e_hbm, h_hbm, taps_hbm, order_hbm, x_hbm, wt_hbm,
    out_ref, mine_hbm, theirs_hbm, back_hbm,
    stats_ref, sums_ref, first_ref, gain_ref, shift_ref, errs_ref, e_ref, h_ref, taps_ref, order_ref, x_ref, wt_ref,
    mine_ref, theirs_ref, back_ref, scr, sems,
):
    small = fetch_all(sems, 0, [(stats_hbm, stats_ref), (sums_hbm, sums_ref)])
    main = fetch_all(sems, 2, [(h_hbm.at[2 * LINE : 12 * LINE, :], h_ref), (e_hbm, e_ref)])
    grads = fetch_all(sems, 4, [(order_hbm, order_ref), (taps_hbm, taps_ref)])
    rest = fetch_all(
        sems, 6,
        [
            (first_hbm, first_ref), (gain_hbm, gain_ref), (shift_hbm, shift_ref), (errs_hbm, errs_ref),
            (x_hbm.at[4 * LINE : 12 * LINE, :], x_ref), (wt_hbm, wt_ref),
        ],
    )
    table = hot()
    wait_all(small)
    mean, rstd = norm_lines(stats_ref, table)
    first, second = back_line(sums_ref, table)
    scale = tile_lines(rstd, 10)
    wait_all(main)
    nhat = (h_ref[...] - tile_lines(mean, 10)) * scale
    dh = scale * (e_ref[...] - tile_lines(first, 10) - nhat * tile_lines(second, 10))
    dh = masked(dh, 3, 10)
    spread_wide(scr, dh)
    one, two = center_line()
    wait_all(grads)
    kernel_grad(mine_ref, theirs_ref, taps_ref, 0, dh[LINE : 9 * LINE] * tile_lines(one + two, ROWS), order_ref)
    outs = fetch_all(sems, 12, [(theirs_ref, theirs_hbm), (mine_ref, mine_hbm)])
    wait_all(rest)
    mean, rstd = norm_lines(first_ref, table)
    nhat = (x_ref[...].astype(F32) - tile_lines(mean, ROWS)) * tile_lines(rstd, ROWS)
    n1 = nhat * flat(gain_ref) + flat(shift_ref)
    e1 = conv_turned(scr, wt_ref, ROWS) * (silu_slope(n1) * flat(gain_ref))
    back_ref[...] = e1
    outs = outs + [fetch(sems, 14, back_ref, back_hbm)]
    out_ref[0:1] = pair_sums(e1, nhat, table)
    out_ref[1:2] = errs_ref[...]
    wait_all(outs)


def last_kernel(sums_ref, info_ref, stats_ref, e_ref, x_ref, u_ref, out_ref, scr):
    weight = info_ref[0:1, 0:1]
    table = hot()
    mean, rstd = norm_lines(stats_ref, table)
    first, second = back_line(sums_ref, table)
    scale = tile_lines(rstd, ROWS)
    nhat = (x_ref[4 * LINE : 12 * LINE, :].astype(F32) - tile_lines(mean, ROWS)) * scale
    dx = scale * (e_ref[...] - tile_lines(first, ROWS) - nhat * tile_lines(second, ROWS))
    scr[...] = (u_ref[...].astype(F32) + dx) * weight
    centered(out_ref, scr)


def piece_rows(count, at, sums, errs):
    index = lax.broadcasted_iota(jnp.int32, (count, 128), 0)
    out = jnp.zeros((count, 128), F32)
    for i, piece in enumerate(pieces(sums) + pieces(errs)):
        out = out + jnp.where(index == at + i, piece, 0.0)
    return out


def centered(out_ref, scr):
    for b in range(2):
        for y in range(ROWS):
            at = y * LINE + b * GW + RIM
            out_ref[(b * ROWS + y) * COLS : (b * ROWS + y + 1) * COLS] = scr[at : at + COLS].astype(BF16)


def early_kernel(mine_ref, got_ref, lines_ref, block_ref, *outs):
    outs, scr = outs[:4], outs[4]
    scr[...] = lines_ref[...].astype(F32)
    centered(block_ref, scr)
    y = lax.axis_index("y")
    for k, out_ref in enumerate(outs):
        rows = pl.ds(pl.multiple_of(lax.rem(y + k, 4) * 80, 16), 80)
        out_ref[...] = (mine_ref[rows, :].astype(F32) + got_ref[rows, :].astype(F32)).astype(BF16)


def late_kernel(mine_ref, got_ref, part_ref, other_ref, a_ref, b_ref, c_ref, d_ref, out_ref, *outs):
    for j in range(4):
        for i in range(4):
            for k in range(3):
                rows = slice(j * 80, (j + 1) * 80)
                lanes = slice(i * 384 + k * 128, i * 384 + (k + 1) * 128)
                both = mine_ref[rows, lanes].astype(F32) + got_ref[rows, lanes].astype(F32)
                out_ref[i * 4 + j, k * 80 : (k + 1) * 80, :] = both.astype(BF16)
    tails = part_ref[...] + other_ref[...]
    rows = piece_rows(16, 0, tails[0:1], tails[1:2]).astype(BF16)
    for i in range(16):
        out_ref[i, 240:256, :] = rows
    outs, scr = outs[:4], outs[4]
    scr[...] = (
        (a_ref[...].astype(F32) + b_ref[...].astype(F32)) + (c_ref[...].astype(F32) + d_ref[...].astype(F32))
    )
    x = lax.axis_index("x")
    for i, out_ref in enumerate(outs):
        for k in range(3):
            lanes = pl.ds(pl.multiple_of(lax.rem(x + i, 4) * 384 + k * 128, 128), 128)
            out_ref[k * 80 : (k + 1) * 80] = scr[:, lanes].astype(BF16)


def plane_kernel(in_ref, a_ref, b_ref, c_ref, d_ref, move_ref, out_ref):
    total = in_ref[0].astype(F32)
    for i in range(1, 16):
        total = total + in_ref[i].astype(F32)
    tail = total[240:256]
    sums = tail[0:1] + tail[1:2] + tail[2:3]
    errs = tail[3:4] + tail[4:5] + tail[5:6]
    rows = piece_rows(80, 60, sums, errs)
    other = (a_ref[...].astype(F32) + b_ref[...].astype(F32)) + (c_ref[...].astype(F32) + d_ref[...].astype(F32))
    both = jnp.concatenate([other, total[0:240]], axis=0).astype(BF16)
    moved = dot(move_ref[...], both)
    for z in range(8):
        out_ref[z] = (moved[z * 80 : (z + 1) * 80] + rows).astype(BF16)


def depth_kernel(in_ref, sign_ref, ref_ref, out_ref, sums_ref, info_ref, loss_ref):
    total = in_ref[0].astype(F32)
    for i in range(1, 8):
        total = total + in_ref[i].astype(F32)
    sums_ref[...] = total[60:61] + total[61:62] + total[62:63]
    errs = total[63:64] + total[64:65] + total[65:66]
    excess = errs[:, 0:2] * (1.0 / (BAND_ROWS * BAND_COLS * C)) - ref_ref[...]
    gap = 0.5 * flat(sign_ref)[:, 0:1] * (excess[:, 0:1] - excess[:, 1:2])
    weight = 1.0 / (1.0 + jnp.exp(-gap))
    loss = jnp.maximum(gap, 0.0) + jnp.log1p(jnp.exp(-jnp.abs(gap)))
    info_ref[...] = jnp.broadcast_to(weight, (1, 128))
    loss_ref[...] = loss
    grads = (total[0:64] * (weight * (2 * BAND_ROWS * BAND_COLS) ** -0.5)).astype(BF16)
    for i in range(8):
        out_ref[i] = grads


VM = pl.BlockSpec(memory_space=pltpu.VMEM)
HB = pl.BlockSpec(memory_space=pltpu.HBM)
DMA = pltpu.SemaphoreType.DMA


def call(kernel, outs, ins, scratch=(), flops=0):
    size = sum(int(np.prod(s.shape)) * s.dtype.itemsize for _, s in outs)
    size += sum(a.size * a.dtype.itemsize for _, a in ins)
    many = len(outs) > 1
    shapes, spaces = [s for _, s in outs], [p for p, _ in outs]
    return pl.pallas_call(
        kernel,
        out_shape=tuple(shapes) if many else shapes[0],
        in_specs=[p for p, _ in ins],
        out_specs=tuple(spaces) if many else spaces[0],
        scratch_shapes=list(scratch),
        compiler_params=pltpu.CompilerParams(vmem_limit_bytes=VMEM_LIMIT),
        cost_estimate=pl.CostEstimate(flops=flops, bytes_accessed=size, transcendentals=0),
    )(*[a for _, a in ins])


def sds(shape, dtype=F32):
    return jax.ShapeDtypeStruct(shape, dtype)


AXES = ("x", "c", "z", "y")


def share(rows):
    return lax.all_to_all(rows, AXES, 0, 0, tiled=True)


def widen(features, target, low, high):
    up = [(i, i + 1) for i in range(7)]
    down = [(i + 1, i) for i in range(7)]
    low = lax.ppermute(low, ("x", "c"), up)
    high = lax.ppermute(high, ("x", "c"), down)
    strip, wide = sds((224, C), BF16), pltpu.VMEM((896, C), F32)
    edge = pltpu.VMEM((224, C), F32)
    ins = [(VM, features), (VM, target), (VM, low), (VM, high)]
    right, left = call(pack_kernel, [(VM, strip), (VM, strip)], ins, [wide, edge, edge])
    first = lax.ppermute(right, ("z", "y"), [(i, i + 1) for i in range(31)])
    last = lax.ppermute(left, ("z", "y"), [(i + 1, i) for i in range(31)])
    f, t = call(
        grid_kernel,
        [(VM, sds((GH * LINE, C), BF16)), (VM, sds((12 * LINE, C), BF16))],
        ins + [(VM, first), (VM, last)],
        [wide, edge, edge, pltpu.VMEM(((GH + 12) * LINE, C), F32)],
    )
    return f, t


def time_embed(timestep, time_weight, time_bias):
    half = TEMB // 2
    freqs = jnp.exp(-jnp.log(10000.0) * jnp.arange(half, dtype=F32) / half)
    angles = timestep.astype(F32)[:, None] * freqs[None, :]
    emb = jnp.concatenate([jnp.cos(angles), jnp.sin(angles)], axis=1)
    return jnp.dot(jax.nn.silu(emb), time_weight.astype(F32), precision=HIGH) + time_bias


def order_matrix():
    out = np.zeros((C, C), np.float32)
    for z in range(8):
        for y in range(4):
            for j in range(10):
                out[z * 40 + y * 10 + j, y * 80 + z * 10 + j] = 1.0
    return jnp.asarray(out, BF16)


def move_matrix():
    out = np.zeros((640, 480), np.float32)
    for grad in range(2):
        for k in range(3):
            for z in range(8):
                for j in range(10):
                    out[z * 80 + grad * 30 + k * 10 + j, grad * 240 + k * 80 + z * 10 + j] = 1.0
    return jnp.asarray(out, BF16)


def shift(block, axis, by):
    return lax.ppermute(block, axis, [(i, (i + by) % 4) for i in range(4)])


def swap(theirs):
    return lax.ppermute(theirs, "c", [(0, 1), (1, 0)])


def body(
    features, target, norm1_gain, norm1_shift, kernel1, bias1, time_weight, time_bias,
    norm2_gain, norm2_shift, kernel2, bias2, ref_error, preference, timestep,
):
    sign = jnp.broadcast_to(jnp.where(preference == 0, 2.0, -2.0).astype(F32), (C,))
    strip, cells = sds((2 * 6 * COLS, C), BF16), 2 * ROWS * COLS
    part, low, high = call(
        moments_kernel,
        [(VM, sds((DEVICES, 128))), (VM, strip), (VM, strip)],
        [(VM, features.reshape(cells, C)), (VM, target.reshape(cells, C))],
    )
    stats1 = share(part)
    fx, tx = widen(features.reshape(cells, C), target.reshape(cells, C), low, high)
    temb = time_embed(timestep, time_weight, time_bias).reshape(C)
    order, move = order_matrix(), move_matrix()
    w1, w2 = kernel1.reshape(3, 3 * C, C), kernel2.reshape(3, 3 * C, C)
    conv_flops = 2 * 9 * C * C * LINE
    half = sds((C, LANES // 2), BF16)
    row, table, lines = sds((1, 128)), sds((DEVICES, 128)), sds((ROWS * LINE, C), BF16)
    full = sds((3, 3, C, C), BF16)
    part, h1, taps1 = call(
        first_kernel,
        [(VM, table), (HB, sds((14 * LINE, C))), (HB, sds((10 * LINE, 3 * C), BF16))],
        [(HB, v) for v in (stats1, norm1_gain, norm1_shift, bias1, temb, fx, w1)],
        [
            pltpu.VMEM((GH * LINE, 3 * C), BF16), pltpu.VMEM((3, 3 * C, C), BF16),
            pltpu.VMEM((GH * LINE, C), BF16), pltpu.VMEM((14 * LINE, C), F32),
            pltpu.VMEM((DEVICES, 128), F32), *[pltpu.VMEM((C,), F32)] * 4, DMA((9,)),
        ],
        14 * conv_flops,
    )
    stats2 = share(part)
    part, errs, e2, bout, u, mine2, theirs2 = call(
        second_kernel,
        [
            (VM, table), (VM, row), (HB, sds((10 * LINE, C))), (HB, lines), (HB, lines), (HB, half), (HB, half),
        ],
        [
            (HB, v)
            for v in (stats2, norm2_gain, norm2_shift, bias2, sign, h1, w2, kernel2, fx, tx, order)
        ],
        [
            pltpu.VMEM((14 * LINE, 3 * C), BF16), pltpu.VMEM((12 * LINE, 1152), BF16),
            pltpu.VMEM((3, 3 * C, C), BF16), pltpu.VMEM(full.shape, BF16),
            pltpu.VMEM((12 * LINE, C), BF16), pltpu.VMEM((12 * LINE, C), BF16), pltpu.VMEM((C, C), BF16),
            pltpu.VMEM((ROWS * LINE, C), BF16), pltpu.VMEM((ROWS * LINE, C), BF16),
            pltpu.VMEM((C, LANES // 2), BF16), pltpu.VMEM((C, LANES // 2), BF16),
            pltpu.VMEM((14 * LINE, C), F32), pltpu.VMEM((10 * LINE, C), F32),
            pltpu.VMEM((DEVICES, 128), F32), *[pltpu.VMEM((C,), F32)] * 4, DMA((16,)),
        ],
        30 * conv_flops,
    )
    sums2 = share(part)
    got2 = swap(theirs2)
    block_out, *strips = call(
        early_kernel,
        [(VM, sds((cells, C), BF16))] + [(VM, sds((80, LANES // 2), BF16))] * 4,
        [(VM, mine2), (VM, got2), (VM, bout)],
        [pltpu.VMEM((ROWS * LINE, C), F32)],
    )
    block_out = block_out.reshape(2, ROWS, COLS, C)
    strips = [strips[0]] + [shift(strips[k], "y", k) for k in range(1, 4)]
    sums2, strips[0] = lax.optimization_barrier((sums2, strips[0]))
    part, mine1, theirs1, e1 = call(
        third_kernel,
        [(VM, sds((2, 128))), (HB, half), (HB, half), (HB, sds((ROWS * LINE, C)))],
        [
            (HB, v)
            for v in (
                stats2, sums2, stats1, norm1_gain, norm1_shift, errs, e2, h1, taps1, order, fx, kernel1,
            )
        ],
        [
            *[pltpu.VMEM((DEVICES, 128), F32)] * 3, *[pltpu.VMEM((C,), F32)] * 2, pltpu.VMEM((1, 128), F32),
            pltpu.VMEM((10 * LINE, C), F32), pltpu.VMEM((10 * LINE, C), F32),
            pltpu.VMEM((10 * LINE, 3 * C), BF16), pltpu.VMEM((C, C), BF16),
            pltpu.VMEM((ROWS * LINE, C), BF16), pltpu.VMEM(full.shape, BF16),
            pltpu.VMEM(half.shape, BF16), pltpu.VMEM(half.shape, BF16), pltpu.VMEM((ROWS * LINE, C), F32),
            pltpu.VMEM((10 * LINE, 1152), BF16), DMA((15,)),
        ],
        16 * conv_flops,
    )
    theirs1, *strips = lax.optimization_barrier((theirs1, *strips))
    got1, other = swap(theirs1), swap(part)
    plane, *parts = call(
        late_kernel,
        [(VM, sds((16, 256, 128), BF16))] + [(VM, sds((240, 128), BF16))] * 4,
        [(VM, mine1), (VM, got1), (VM, part), (VM, other)] + [(VM, v) for v in strips],
        [pltpu.VMEM((80, LANES // 2), F32)],
    )
    plane = lax.all_to_all(plane, ("x", "y"), 0, 0, tiled=True)
    parts = [parts[0]] + [shift(parts[k], "x", k) for k in range(1, 4)]
    depth = call(
        plane_kernel,
        [(VM, sds((8, 80, 128), BF16))],
        [(VM, plane)] + [(VM, v) for v in parts] + [(VM, move)],
    )
    depth = lax.all_to_all(depth, ("z",), 0, 0, tiled=True)
    copies, sums1, info, loss = call(
        depth_kernel,
        [(VM, sds((8, 64, 128), BF16)), (VM, row), (VM, row), (VM, sds((1, 1)))],
        [(VM, depth), (VM, sign), (VM, ref_error)],
    )
    whole = lax.all_to_all(copies, ("x", "c"), 0, 0, tiled=True)
    grad = call(
        last_kernel,
        [(VM, sds((cells, C), BF16))],
        [(VM, sums1), (VM, info), (VM, stats1), (VM, e1), (VM, fx), (VM, u)],
        [pltpu.VMEM((ROWS * LINE, C), F32)],
    )
    feature_grad = grad.reshape(2, ROWS, COLS, C)
    whole = whole[:, :60].reshape(4, 2, 2, 3, 10, 128).transpose(2, 1, 0, 3, 5, 4).reshape(2, LANES, 10)
    whole = whole[:, :TAPS].astype(F32).reshape(2, 3, 3, C, 10)
    loss = loss.reshape(())
    return (block_out, feature_grad, whole[1], whole[0], loss)


def solution(mesh):
    fine = Mesh(mesh.devices.reshape(4, 2, 8, 4), AXES)
    cells = P(None, ("x", "c"), ("z", "y"), None)
    kernels = P(None, None, None, ("z", "y"))
    return jax.shard_map(
        body,
        mesh=fine,
        in_specs=(cells, cells) + (P(),) * 13,
        out_specs=(cells, cells, kernels, kernels, P()),
        check_vma=False,
    )
```

```python
import functools

import jax
import jax.numpy as jnp
import numpy as np
from jax import lax
from jax.experimental import pallas as pl
from jax.experimental.pallas import tpu as pltpu
from jax.sharding import Mesh
from jax.sharding import PartitionSpec as P

GROUPS = 32
TEMB = 1280
C = 320
WIDTH = C // GROUPS
ROWS, COLS = 8, 16
BAND_ROWS, BAND_COLS = 64, 512
RIM = 4
GH, GW = ROWS + 2 * RIM, COLS + 2 * RIM
LINE = 2 * GW
DEVICES = 256
LOCAL = ROWS * COLS * WIDTH
TOTAL = LOCAL * DEVICES
TAPS = 9 * C
LANES = 3072
EPS = 1e-05
F32, BF16 = jnp.float32, jnp.bfloat16
HIGH = lax.Precision.HIGHEST
VMEM_LIMIT = 63 * 2**20


def dot(a, b):
    return jnp.dot(a, b, preferred_element_type=F32)


def pieces(row):
    high = row.astype(BF16).astype(F32)
    rest = row - high
    mid = rest.astype(BF16).astype(F32)
    return high, mid, rest - mid


def hot():
    blocks = []
    for slot in range(4):
        low = (lax.broadcasted_iota(jnp.int32, (128, 384), 0) - slot * GROUPS) * WIDTH
        chan = lax.broadcasted_iota(jnp.int32, (128, 384), 1)
        blocks.append(((chan >= low) & (chan < low + WIDTH) & (chan < C)).astype(F32).astype(BF16))
    return jnp.concatenate(blocks, axis=1)


def stacked(row):
    index = lax.broadcasted_iota(jnp.int32, (16, row.shape[1]), 0)
    out = jnp.zeros((16, row.shape[1]), F32)
    for i, piece in enumerate(pieces(row)):
        out = jnp.where(index == i, piece, out)
    return out.astype(BF16)


def expand(row, table):
    wide = jnp.sum(dot(stacked(row), table), axis=0, keepdims=True)
    return [wide[:, i * 384 : i * 384 + C] for i in range(4)]


def collapse(rows, table):
    gap, empty = jnp.zeros((1, 384 - C), F32), jnp.zeros((1, C), F32)
    wide = jnp.concatenate([v for row in rows for v in (empty if row is None else row, gap)], axis=1)
    small = lax.dot_general(stacked(wide), table, (((1,), (1,)), ((), ())), preferred_element_type=F32)
    return jnp.sum(small, axis=0, keepdims=True)


def per_line(first, second):
    return jnp.concatenate(
        [jnp.broadcast_to(first, (GW, C)), jnp.broadcast_to(second, (GW, C))], axis=0
    )


def tile_lines(line, count):
    return jnp.broadcast_to(line[None], (count, LINE, C)).reshape(count * LINE, C)


def masked(values, top, count):
    high = lax.axis_index("x") * 2 + lax.axis_index("c")
    wide = lax.axis_index("z") * 4 + lax.axis_index("y")
    col = lax.broadcasted_iota(jnp.int32, (LINE, C), 0)
    gx = jnp.where(col >= GW, col - GW, col) + (wide * COLS - RIM)
    line = ((gx >= 0) & (gx < BAND_COLS)).astype(F32)
    upper = line * jnp.where(high > 0, 1.0, 0.0)
    lower = line * jnp.where(high < BAND_ROWS // ROWS - 1, 1.0, 0.0)
    parts = [(upper, RIM - top), (line, ROWS), (lower, top + count - RIM - ROWS)]
    mask = jnp.concatenate([jnp.broadcast_to(v[None], (n, LINE, C)) for v, n in parts], axis=0)
    return values * mask.reshape(count * LINE, C)


def center_line():
    col = lax.broadcasted_iota(jnp.int32, (LINE, C), 0)
    one = (col >= RIM) & (col < RIM + COLS)
    two = (col >= GW + RIM) & (col < GW + RIM + COLS)
    return one.astype(F32), two.astype(F32)


def line_sums(values):
    total = jnp.sum(values.reshape(ROWS, LINE, C), axis=0)
    return [jnp.sum(total * line, axis=0, keepdims=True) for line in center_line()]


def norm_rows(stats_ref, table):
    stats = stats_ref[...]
    sums = jnp.sum(stats, axis=0, keepdims=True)
    mean = sums * (1.0 / DEVICES)
    off = stats - mean
    spread = jnp.sum(off * off, axis=0, keepdims=True) * LOCAL
    var = (sums + pltpu.roll(spread, 64, 1)) * (1.0 / TOTAL)
    lane = lax.broadcasted_iota(jnp.int32, (1, 128), 1)
    row = jnp.where(lane < 64, mean, 1.0 / jnp.sqrt(jnp.maximum(var, 0.0) + EPS))
    return expand(row, table)


def norm_lines(rows):
    return per_line(rows[0], rows[1]), per_line(rows[2], rows[3])


def kept_rows(ref):
    return [ref[i : i + 1, :] for i in range(4)]


def keep_rows(ref, rows):
    for i, row in enumerate(rows):
        ref[i : i + 1, :] = row


def moments(values, table):
    first, second = line_sums(values)
    means = collapse([first, second, None, None], table) * (1.0 / LOCAL)
    one, two, _, _ = expand(means, table)
    off = values - tile_lines(per_line(one, two), ROWS)
    first, second = line_sums(off * off)
    return means + collapse([None, None, first, second], table)


def pair_sums(scaled, normed, table):
    return collapse(line_sums(scaled) + line_sums(scaled * normed), table)


def sigmoid(v):
    return 0.5 + 0.5 * jnp.tanh(0.5 * v)


def silu_slope(v):
    sig = sigmoid(v)
    return sig * (1.0 + v * (1.0 - sig))


def spread_taps(ref, values):
    count = values.shape[0]
    ref[:, 0:C] = pltpu.roll(values, 1, 0).astype(BF16)
    ref[:, C : 2 * C] = values.astype(BF16)
    ref[:, 2 * C : 3 * C] = pltpu.roll(values, count - 1, 0).astype(BF16)


def spread_wide(ref, values):
    count = values.shape[0]
    ref[:, 0:C] = pltpu.roll(values, 1, 0).astype(BF16)
    ref[:, 384 : 384 + C] = values.astype(BF16)
    ref[:, 768 : 768 + C] = pltpu.roll(values, count - 1, 0).astype(BF16)


def conv_lines(ref, weights_ref, count):
    total = dot(ref[0 : count * LINE, :], weights_ref[0])
    for ky in range(1, 3):
        total = total + dot(ref[ky * LINE : (ky + count) * LINE, :], weights_ref[ky])
    return total


def conv_turned(ref, weights_ref, count):
    total = None
    for ky in range(3):
        for kx in range(3):
            part = lax.dot_general(
                ref[ky * LINE : (ky + count) * LINE, kx * 384 : kx * 384 + C],
                weights_ref[2 - ky, 2 - kx],
                (((1,), (1,)), ((), ())),
                preferred_element_type=F32,
            )
            total = part if total is None else total + part
    return total


def kernel_grad(mine_ref, theirs_ref, taps_ref, top, grads, order_ref):
    core = lax.axis_index("c")
    ordered = dot(grads.astype(BF16), order_ref[...])
    left = ordered.T.astype(BF16)
    parts = []
    for ky in range(3):
        lines = taps_ref[(top + ky) * LINE : (top + ky + ROWS) * LINE, :]
        parts.append(dot(left, lines).astype(BF16))
    parts.append(jnp.zeros((C, LANES - TAPS), BF16))
    whole = jnp.concatenate(parts, axis=1)
    low, high = whole[:, : LANES // 2], whole[:, LANES // 2 :]

    @pl.when(core == 0)
    def _():
        mine_ref[...] = low
        theirs_ref[...] = high

    @pl.when(core == 1)
    def _():
        mine_ref[...] = high
        theirs_ref[...] = low


def fetch(sems, index, src, dst):
    copy = pltpu.make_async_copy(src, dst, sems.at[index])
    copy.start()
    return copy


def fetch_all(sems, first, pairs):
    return [fetch(sems, first + i, src, dst) for i, (src, dst) in enumerate(pairs)]


def wait_all(copies):
    for copy in copies:
        copy.wait()


def flat(ref):
    return ref[...].reshape(1, C)


def moments_kernel(x_ref, t_ref, out_ref, near_ref, far_ref):
    half, core = ROWS * COLS, lax.axis_index("c")
    for b in range(2):
        at, to = b * half, b * 6 * COLS
        parts = [
            (x_ref[at + 4 * COLS : at + 8 * COLS, :], x_ref[at : at + 4 * COLS, :], to, 4 * COLS),
            (t_ref[at + 6 * COLS : at + 8 * COLS, :], t_ref[at : at + 2 * COLS, :], to + 4 * COLS, 2 * COLS),
        ]
        for bottom, top, first, count in parts:
            near_ref[first : first + count] = jnp.where(core == 0, bottom, top)
            far_ref[first : first + count] = jnp.where(core == 0, top, bottom)
    table = hot()
    values = [x_ref[b * half : (b + 1) * half, :].astype(F32) for b in range(2)]
    sums = [jnp.sum(v, axis=0, keepdims=True) for v in values]
    means = collapse(sums + [None, None], table) * (1.0 / LOCAL)
    offs = [v - m for v, m in zip(values, expand(means, table))]
    sums = [jnp.sum(v * v, axis=0, keepdims=True) for v in offs]
    out = means + collapse([None, None] + sums, table)
    out_ref[...] = jnp.broadcast_to(out, (DEVICES, 128))


def strip_blocks():
    out, row = [], 0
    for b in range(2):
        low, high = 512 + b * 6 * COLS, 704 + b * 6 * COLS
        for y in range(GH):
            start = low + y * COLS if y < 4 else b * 128 + (y - 4) * COLS if y < 12 else high + (y - 12) * COLS
            out.append((row, RIM, start, y * LINE + b * GW))
            row += RIM
        for y in range(12):
            start = low + (4 + y) * COLS if y < 2 else 256 + b * 128 + (y - 2) * COLS if y < 10 else high + (y - 6) * COLS
            out.append((row, 2, start, (GH + y) * LINE + b * GW))
            row += 2
    return out


def widened(scr, x_ref, t_ref, near_ref, far_ref):
    core = lax.axis_index("c")
    near, far = near_ref[...].astype(F32), far_ref[...].astype(F32)
    scr[0:256] = x_ref[...].astype(F32)
    scr[256:512] = t_ref[...].astype(F32)
    scr[512:704] = jnp.where(core == 0, far, near)
    scr[704:896] = jnp.where(core == 0, near, far)


def pack_kernel(x_ref, t_ref, near_ref, far_ref, right_ref, left_ref, scr, right, left):
    widened(scr, x_ref, t_ref, near_ref, far_ref)
    for row, width, start, _ in strip_blocks():
        left[row : row + width] = scr[start : start + width]
        right[row : row + width] = scr[start + COLS - width : start + COLS]
    right_ref[...] = right[...].astype(BF16)
    left_ref[...] = left[...].astype(BF16)


def grid_kernel(x_ref, t_ref, near_ref, far_ref, first_ref, last_ref, f_ref, g_ref, scr, first, last, grid):
    widened(scr, x_ref, t_ref, near_ref, far_ref)
    first[...] = first_ref[...].astype(F32)
    last[...] = last_ref[...].astype(F32)
    empty = jnp.zeros((2, C), F32)
    for row, width, start, at in strip_blocks():
        inner = at + RIM
        grid[inner - width : inner] = first[row : row + width]
        grid[inner : inner + COLS] = scr[start : start + COLS]
        grid[inner + COLS : inner + COLS + width] = last[row : row + width]
        if width == 2:
            grid[at : at + 2] = empty
            grid[at + GW - 2 : at + GW] = empty
    f_ref[...] = grid[0 : GH * LINE].astype(BF16)
    g_ref[...] = grid[GH * LINE : (GH + 12) * LINE].astype(BF16)


def first_kernel(
    stats_hbm, gain_hbm, shift_hbm, bias_hbm, temb_hbm, x_hbm, w_hbm,
    out_hbm, rows_hbm, h_hbm, taps_hbm, scr, w_ref, x_ref, h_ref, out_ref, rows_ref,
    stats_ref, gain_ref, shift_ref, bias_ref, temb_ref, sems,
):
    small = fetch_all(
        sems, 4,
        [
            (stats_hbm, stats_ref), (gain_hbm, gain_ref), (shift_hbm, shift_ref),
            (bias_hbm, bias_ref), (temb_hbm, temb_ref),
        ],
    )
    xs = fetch(sems, 2, x_hbm, x_ref)
    weights = fetch(sems, 0, w_hbm, w_ref)
    table = hot()
    wait_all(small)
    rows = norm_rows(stats_ref, table)
    keep_rows(rows_ref, rows)
    kept = fetch(sems, 9, rows_ref, rows_hbm)
    mean, rstd = norm_lines(rows)
    scale = tile_lines(rstd * flat(gain_ref), GH)
    xs.wait()
    n1 = (x_ref[...].astype(F32) - tile_lines(mean, GH)) * scale + flat(shift_ref)
    spread_taps(scr, masked(n1 * sigmoid(n1), 0, GH))
    taps = fetch(sems, 1, scr.at[3 * LINE : 13 * LINE, :], taps_hbm)
    weights.wait()
    h1 = conv_lines(scr, w_ref, GH - 2) + (flat(bias_ref) + flat(temb_ref))
    h_ref[...] = h1
    hs = fetch(sems, 3, h_ref, h_hbm)
    out_ref[...] = jnp.broadcast_to(moments(h1[3 * LINE : 11 * LINE], table), (DEVICES, 128))
    outs = fetch(sems, 10, out_ref, out_hbm)
    wait_all([taps, hs, kept, outs])


def second_kernel(
    stats_hbm, gain_hbm, shift_hbm, bias_hbm, sign_hbm, h_hbm, w_hbm, wt_hbm, x_hbm, t_hbm, order_hbm,
    out_hbm, err_hbm, rows_hbm, n_hbm, e_hbm, bout_hbm, u_hbm, mine_hbm, theirs_hbm,
    scr_a, scr_u, w_ref, wt_ref, x_ref, t_ref, order_ref, bout_ref, u_ref, mine_ref, theirs_ref, h_ref, e_ref,
    out_ref, err_ref, rows_ref, n_ref, stats_ref, gain_ref, shift_ref, bias_ref, sign_ref, sems,
):
    small = fetch_all(
        sems, 11,
        [
            (stats_hbm, stats_ref), (gain_hbm, gain_ref), (shift_hbm, shift_ref),
            (bias_hbm, bias_ref), (sign_hbm, sign_ref),
        ],
    )
    hs = fetch(sems, 9, h_hbm, h_ref)
    weights = fetch(sems, 0, w_hbm, w_ref)
    xs = fetch(sems, 1, x_hbm.at[2 * LINE : 14 * LINE, :], x_ref)
    ts = fetch(sems, 2, t_hbm, t_ref)
    orders = fetch(sems, 4, order_hbm, order_ref)
    turned = fetch(sems, 3, wt_hbm, wt_ref)
    table = hot()
    wait_all(small)
    rows = norm_rows(stats_ref, table)
    keep_rows(rows_ref, rows)
    mean, rstd = norm_lines(rows)
    hs.wait()
    nhat = (h_ref[...] - tile_lines(mean, GH - 2)) * tile_lines(rstd, GH - 2)
    n_ref[...] = nhat[2 * LINE : 12 * LINE]
    kept = fetch_all(sems, 16, [(rows_ref, rows_hbm), (n_ref, n_hbm)])
    n2 = nhat * flat(gain_ref) + flat(shift_ref)
    spread_taps(scr_a, masked(n2 * sigmoid(n2), 1, GH - 2))
    weights.wait()
    conv = conv_lines(scr_a, w_ref, 12) + flat(bias_ref)
    xs.wait()
    out = x_ref[...].astype(F32) + conv
    bout_ref[...] = out[2 * LINE : 10 * LINE].astype(BF16)
    bouts = fetch(sems, 5, bout_ref, bout_hbm)
    ts.wait()
    diff = out - t_ref[...].astype(F32)
    mid = diff[2 * LINE : 10 * LINE]
    lane = lax.broadcasted_iota(jnp.int32, (1, 128), 1)
    errs = jnp.zeros((1, 128), F32)
    for b, part in enumerate(line_sums(mid * mid)):
        errs = errs + jnp.where(lane == b, jnp.sum(part, axis=1, keepdims=True), 0.0)
    err_ref[...] = errs
    sign = tile_lines(per_line(flat(sign_ref), -flat(sign_ref)), 12)
    u = masked(diff * sign, 2, 12)
    spread_wide(scr_u, u)
    center = u[2 * LINE : 10 * LINE]
    u_ref[...] = center.astype(BF16)
    us = fetch(sems, 6, u_ref, u_hbm)
    one, two = center_line()
    orders.wait()
    kernel_grad(mine_ref, theirs_ref, scr_a, 2, center * tile_lines(one + two, ROWS), order_ref)
    mines = fetch(sems, 7, mine_ref, mine_hbm)
    others = fetch(sems, 8, theirs_ref, theirs_hbm)
    turned.wait()
    da2 = conv_turned(scr_u, wt_ref, 10)
    e = da2 * silu_slope(n2[2 * LINE : 12 * LINE]) * flat(gain_ref)
    e_ref[...] = e
    es = fetch(sems, 10, e_ref, e_hbm)
    sums = pair_sums(e[LINE : 9 * LINE], nhat[3 * LINE : 11 * LINE], table)
    out_ref[...] = jnp.broadcast_to(sums, (DEVICES, 128))
    outs = fetch_all(sems, 18, [(out_ref, out_hbm), (err_ref, err_hbm)])
    wait_all([bouts, us, mines, others, es] + kept + outs)


def back_line(sums_ref, table):
    sums = jnp.sum(sums_ref[...], axis=0, keepdims=True) * (1.0 / TOTAL)
    one, two, three, four = expand(sums, table)
    return per_line(one, two), per_line(three, four)


def third_kernel(
    second_hbm, sums_hbm, first_hbm, gain_hbm, shift_hbm, errs_hbm, e_hbm, n_hbm, taps_hbm, order_hbm, x_hbm, wt_hbm,
    out_hbm, mine_hbm, theirs_hbm, back_hbm,
    out_ref, second_ref, sums_ref, first_ref, gain_ref, shift_ref, errs_ref, e_ref, n_ref, taps_ref, order_ref, x_ref, wt_ref,
    mine_ref, theirs_ref, back_ref, scr, sems,
):
    small = fetch_all(sems, 0, [(second_hbm, second_ref), (sums_hbm, sums_ref)])
    main = fetch_all(sems, 2, [(n_hbm, n_ref), (e_hbm, e_ref)])
    grads = fetch_all(sems, 4, [(order_hbm, order_ref), (taps_hbm, taps_ref)])
    rest = fetch_all(
        sems, 6,
        [
            (first_hbm, first_ref), (gain_hbm, gain_ref), (shift_hbm, shift_ref), (errs_hbm, errs_ref),
            (x_hbm.at[4 * LINE : 12 * LINE, :], x_ref), (wt_hbm, wt_ref),
        ],
    )
    table = hot()
    wait_all(small)
    first, second = back_line(sums_ref, table)
    scale = tile_lines(norm_lines(kept_rows(second_ref))[1], 10)
    wait_all(main)
    dh = scale * (e_ref[...] - tile_lines(first, 10) - n_ref[...] * tile_lines(second, 10))
    dh = masked(dh, 3, 10)
    spread_wide(scr, dh)
    one, two = center_line()
    wait_all(grads)
    kernel_grad(mine_ref, theirs_ref, taps_ref, 0, dh[LINE : 9 * LINE] * tile_lines(one + two, ROWS), order_ref)
    outs = fetch_all(sems, 12, [(theirs_ref, theirs_hbm), (mine_ref, mine_hbm)])
    wait_all(rest)
    mean, rstd = norm_lines(kept_rows(first_ref))
    nhat = (x_ref[...].astype(F32) - tile_lines(mean, ROWS)) * tile_lines(rstd, ROWS)
    n1 = nhat * flat(gain_ref) + flat(shift_ref)
    e1 = conv_turned(scr, wt_ref, ROWS) * (silu_slope(n1) * flat(gain_ref))
    back_ref[...] = e1
    outs = outs + [fetch(sems, 14, back_ref, back_hbm)]
    out_ref[0:1] = pair_sums(e1, nhat, table)
    out_ref[1:2] = errs_ref[...]
    wait_all(outs + [fetch(sems, 15, out_ref, out_hbm)])


def last_kernel(sums_ref, info_ref, norm_ref, e_ref, x_ref, u_ref, out_ref, scr):
    weight = info_ref[0:1, 0:1]
    table = hot()
    mean, rstd = norm_lines(kept_rows(norm_ref))
    first, second = back_line(sums_ref, table)
    scale = tile_lines(rstd, ROWS)
    nhat = (x_ref[4 * LINE : 12 * LINE, :].astype(F32) - tile_lines(mean, ROWS)) * scale
    dx = scale * (e_ref[...] - tile_lines(first, ROWS) - nhat * tile_lines(second, ROWS))
    scr[...] = (u_ref[...].astype(F32) + dx) * weight
    centered(out_ref, scr)


def piece_rows(count, at, sums, errs):
    index = lax.broadcasted_iota(jnp.int32, (count, 128), 0)
    out = jnp.zeros((count, 128), F32)
    for i, piece in enumerate(pieces(sums) + pieces(errs)):
        out = out + jnp.where(index == at + i, piece, 0.0)
    return out


def centered(out_ref, scr):
    for b in range(2):
        for y in range(ROWS):
            at = y * LINE + b * GW + RIM
            out_ref[(b * ROWS + y) * COLS : (b * ROWS + y + 1) * COLS] = scr[at : at + COLS].astype(BF16)


def early_kernel(mine_ref, got_ref, lines_ref, block_ref, *outs):
    outs, scr = outs[:4], outs[4]
    scr[...] = lines_ref[...].astype(F32)
    centered(block_ref, scr)
    y = lax.axis_index("y")
    for k, out_ref in enumerate(outs):
        rows = pl.ds(pl.multiple_of(lax.rem(y + k, 4) * 80, 16), 80)
        out_ref[...] = (mine_ref[rows, :].astype(F32) + got_ref[rows, :].astype(F32)).astype(BF16)


def late_kernel(mine_ref, got_ref, part_ref, other_ref, a_ref, b_ref, c_ref, d_ref, out_ref, *outs):
    for j in range(4):
        for i in range(4):
            for k in range(3):
                rows = slice(j * 80, (j + 1) * 80)
                lanes = slice(i * 384 + k * 128, i * 384 + (k + 1) * 128)
                both = mine_ref[rows, lanes].astype(F32) + got_ref[rows, lanes].astype(F32)
                out_ref[i * 4 + j, k * 80 : (k + 1) * 80, :] = both.astype(BF16)
    tails = part_ref[...] + other_ref[...]
    rows = piece_rows(16, 0, tails[0:1], tails[1:2]).astype(BF16)
    for i in range(16):
        out_ref[i, 240:256, :] = rows
    outs, scr = outs[:4], outs[4]
    scr[...] = (
        (a_ref[...].astype(F32) + b_ref[...].astype(F32)) + (c_ref[...].astype(F32) + d_ref[...].astype(F32))
    )
    x = lax.axis_index("x")
    for i, out_ref in enumerate(outs):
        for k in range(3):
            lanes = pl.ds(pl.multiple_of(lax.rem(x + i, 4) * 384 + k * 128, 128), 128)
            out_ref[k * 80 : (k + 1) * 80] = scr[:, lanes].astype(BF16)


def plane_kernel(in_ref, a_ref, b_ref, c_ref, d_ref, move_ref, out_ref):
    total = in_ref[0].astype(F32)
    for i in range(1, 16):
        total = total + in_ref[i].astype(F32)
    tail = total[240:256]
    sums = tail[0:1] + tail[1:2] + tail[2:3]
    errs = tail[3:4] + tail[4:5] + tail[5:6]
    rows = piece_rows(80, 60, sums, errs)
    other = (a_ref[...].astype(F32) + b_ref[...].astype(F32)) + (c_ref[...].astype(F32) + d_ref[...].astype(F32))
    both = jnp.concatenate([other, total[0:240]], axis=0).astype(BF16)
    moved = dot(move_ref[...], both)
    for z in range(8):
        out_ref[z] = (moved[z * 80 : (z + 1) * 80] + rows).astype(BF16)


def depth_kernel(in_ref, sign_ref, ref_ref, out_ref, sums_ref, info_ref, loss_ref):
    total = in_ref[0].astype(F32)
    for i in range(1, 8):
        total = total + in_ref[i].astype(F32)
    sums_ref[...] = total[60:61] + total[61:62] + total[62:63]
    errs = total[63:64] + total[64:65] + total[65:66]
    excess = errs[:, 0:2] * (1.0 / (BAND_ROWS * BAND_COLS * C)) - ref_ref[...]
    gap = 0.5 * flat(sign_ref)[:, 0:1] * (excess[:, 0:1] - excess[:, 1:2])
    weight = 1.0 / (1.0 + jnp.exp(-gap))
    loss = jnp.maximum(gap, 0.0) + jnp.log1p(jnp.exp(-jnp.abs(gap)))
    info_ref[...] = jnp.broadcast_to(weight, (1, 128))
    loss_ref[...] = loss
    grads = (total[0:64] * (weight * (2 * BAND_ROWS * BAND_COLS) ** -0.5)).astype(BF16)
    for i in range(8):
        out_ref[i] = grads


VM = pl.BlockSpec(memory_space=pltpu.VMEM)
HB = pl.BlockSpec(memory_space=pltpu.HBM)
DMA = pltpu.SemaphoreType.DMA


def call(kernel, outs, ins, scratch=(), flops=0):
    size = sum(int(np.prod(s.shape)) * s.dtype.itemsize for _, s in outs)
    size += sum(a.size * a.dtype.itemsize for _, a in ins)
    many = len(outs) > 1
    shapes, spaces = [s for _, s in outs], [p for p, _ in outs]
    return pl.pallas_call(
        kernel,
        out_shape=tuple(shapes) if many else shapes[0],
        in_specs=[p for p, _ in ins],
        out_specs=tuple(spaces) if many else spaces[0],
        scratch_shapes=list(scratch),
        compiler_params=pltpu.CompilerParams(vmem_limit_bytes=VMEM_LIMIT),
        cost_estimate=pl.CostEstimate(flops=flops, bytes_accessed=size, transcendentals=0),
    )(*[a for _, a in ins])


def sds(shape, dtype=F32):
    return jax.ShapeDtypeStruct(shape, dtype)


AXES = ("x", "c", "z", "y")


def share(rows):
    return lax.all_to_all(rows, AXES, 0, 0, tiled=True)


def widen(features, target, near, far):
    strip, wide = sds((176, C), BF16), pltpu.VMEM((896, C), F32)
    edge = pltpu.VMEM((176, C), F32)
    ins = [(VM, features), (VM, target), (VM, near), (VM, far)]
    right, left = call(pack_kernel, [(VM, strip), (VM, strip)], ins, [wide, edge, edge])
    first = lax.ppermute(right, ("z", "y"), [(i, i + 1) for i in range(31)])
    last = lax.ppermute(left, ("z", "y"), [(i + 1, i) for i in range(31)])
    f, t = call(
        grid_kernel,
        [(VM, sds((GH * LINE, C), BF16)), (VM, sds((12 * LINE, C), BF16))],
        ins + [(VM, first), (VM, last)],
        [wide, edge, edge, pltpu.VMEM(((GH + 12) * LINE, C), F32)],
    )
    return f, t


def time_embed(timestep, time_weight, time_bias):
    half = TEMB // 2
    freqs = jnp.exp(-jnp.log(10000.0) * jnp.arange(half, dtype=F32) / half)
    angles = timestep.astype(F32)[:, None] * freqs[None, :]
    emb = jnp.concatenate([jnp.cos(angles), jnp.sin(angles)], axis=1)
    return jnp.dot(jax.nn.silu(emb), time_weight.astype(F32), precision=HIGH) + time_bias


def order_matrix():
    out = np.zeros((C, C), np.float32)
    for z in range(8):
        for y in range(4):
            for j in range(10):
                out[z * 40 + y * 10 + j, y * 80 + z * 10 + j] = 1.0
    return jnp.asarray(out, BF16)


def move_matrix():
    out = np.zeros((640, 480), np.float32)
    for grad in range(2):
        for k in range(3):
            for z in range(8):
                for j in range(10):
                    out[z * 80 + grad * 30 + k * 10 + j, grad * 240 + k * 80 + z * 10 + j] = 1.0
    return jnp.asarray(out, BF16)


def shift(block, axis, by):
    return lax.ppermute(block, axis, [(i, (i + by) % 4) for i in range(4)])


def swap(theirs):
    return lax.ppermute(theirs, "c", [(0, 1), (1, 0)])


def body(
    features, target, norm1_gain, norm1_shift, kernel1, bias1, time_weight, time_bias,
    norm2_gain, norm2_shift, kernel2, bias2, ref_error, preference, timestep,
):
    sign = jnp.broadcast_to(jnp.where(preference == 0, 2.0, -2.0).astype(F32), (C,))
    strip, cells = sds((2 * 6 * COLS, C), BF16), 2 * ROWS * COLS
    part, near, far = call(
        moments_kernel,
        [(VM, sds((DEVICES, 128))), (VM, strip), (VM, strip)],
        [(VM, features.reshape(cells, C)), (VM, target.reshape(cells, C))],
    )
    far = lax.ppermute(far, ("x", "c"), [(1, 2), (2, 1), (3, 4), (4, 3), (5, 6), (6, 5)])
    near = swap(near)
    part, far = lax.optimization_barrier((part, far))
    stats1 = share(part)
    fx, tx = widen(features.reshape(cells, C), target.reshape(cells, C), near, far)
    temb = time_embed(timestep, time_weight, time_bias).reshape(C)
    order, move = order_matrix(), move_matrix()
    w1, w2 = kernel1.reshape(3, 3 * C, C), kernel2.reshape(3, 3 * C, C)
    conv_flops = 2 * 9 * C * C * LINE
    half = sds((C, LANES // 2), BF16)
    row, table, lines = sds((1, 128)), sds((DEVICES, 128)), sds((ROWS * LINE, C), BF16)
    full = sds((3, 3, C, C), BF16)
    rows4, tbl = sds((4, C)), pltpu.VMEM((DEVICES, 128), F32)
    part, norm1, h1, taps1 = call(
        first_kernel,
        [(HB, table), (HB, rows4), (HB, sds((14 * LINE, C))), (HB, sds((10 * LINE, 3 * C), BF16))],
        [(HB, v) for v in (stats1, norm1_gain, norm1_shift, bias1, temb, fx, w1)],
        [
            pltpu.VMEM((GH * LINE, 3 * C), BF16), pltpu.VMEM((3, 3 * C, C), BF16),
            pltpu.VMEM((GH * LINE, C), BF16), pltpu.VMEM((14 * LINE, C), F32), tbl, pltpu.VMEM((4, C), F32),
            tbl, *[pltpu.VMEM((C,), F32)] * 4, DMA((11,)),
        ],
        14 * conv_flops,
    )
    stats2 = share(part)
    part, errs, norm2, nhat2, e2, bout, u, mine2, theirs2 = call(
        second_kernel,
        [
            (HB, table), (HB, row), (HB, rows4), (HB, sds((10 * LINE, C))), (HB, sds((10 * LINE, C))), (HB, lines), (HB, lines), (HB, half), (HB, half),
        ],
        [
            (HB, v)
            for v in (stats2, norm2_gain, norm2_shift, bias2, sign, h1, w2, kernel2, fx, tx, order)
        ],
        [
            pltpu.VMEM((14 * LINE, 3 * C), BF16), pltpu.VMEM((12 * LINE, 1152), BF16),
            pltpu.VMEM((3, 3 * C, C), BF16), pltpu.VMEM(full.shape, BF16),
            pltpu.VMEM((12 * LINE, C), BF16), pltpu.VMEM((12 * LINE, C), BF16), pltpu.VMEM((C, C), BF16),
            pltpu.VMEM((ROWS * LINE, C), BF16), pltpu.VMEM((ROWS * LINE, C), BF16),
            pltpu.VMEM((C, LANES // 2), BF16), pltpu.VMEM((C, LANES // 2), BF16),
            pltpu.VMEM((14 * LINE, C), F32), pltpu.VMEM((10 * LINE, C), F32),
            tbl, pltpu.VMEM((1, 128), F32), pltpu.VMEM((4, C), F32), pltpu.VMEM((10 * LINE, C), F32),
            tbl, *[pltpu.VMEM((C,), F32)] * 4, DMA((20,)),
        ],
        30 * conv_flops,
    )
    sums2 = share(part)
    got2 = swap(theirs2)
    block_out, *strips = call(
        early_kernel,
        [(VM, sds((cells, C), BF16))] + [(VM, sds((80, LANES // 2), BF16))] * 4,
        [(VM, mine2), (VM, got2), (VM, bout)],
        [pltpu.VMEM((ROWS * LINE, C), F32)],
    )
    block_out = block_out.reshape(2, ROWS, COLS, C)
    strips = [strips[0]] + [shift(strips[k], "y", k) for k in (2, 1, 3)]
    sums2, strips[0] = lax.optimization_barrier((sums2, strips[0]))
    part, mine1, theirs1, e1 = call(
        third_kernel,
        [(HB, sds((2, 128))), (HB, half), (HB, half), (HB, sds((ROWS * LINE, C)))],
        [
            (HB, v)
            for v in (
                norm2, sums2, norm1, norm1_gain, norm1_shift, errs, e2, nhat2, taps1, order, fx, kernel1,
            )
        ],
        [
            pltpu.VMEM((2, 128), F32), pltpu.VMEM((4, C), F32), tbl, pltpu.VMEM((4, C), F32),
            *[pltpu.VMEM((C,), F32)] * 2, pltpu.VMEM((1, 128), F32),
            pltpu.VMEM((10 * LINE, C), F32), pltpu.VMEM((10 * LINE, C), F32),
            pltpu.VMEM((10 * LINE, 3 * C), BF16), pltpu.VMEM((C, C), BF16),
            pltpu.VMEM((ROWS * LINE, C), BF16), pltpu.VMEM(full.shape, BF16),
            pltpu.VMEM(half.shape, BF16), pltpu.VMEM(half.shape, BF16), pltpu.VMEM((ROWS * LINE, C), F32),
            pltpu.VMEM((10 * LINE, 1152), BF16), DMA((16,)),
        ],
        16 * conv_flops,
    )
    theirs1, *strips = lax.optimization_barrier((theirs1, *strips))
    got1, other = swap(theirs1), swap(part)
    plane, *parts = call(
        late_kernel,
        [(VM, sds((16, 256, 128), BF16))] + [(VM, sds((240, 128), BF16))] * 4,
        [(VM, mine1), (VM, got1), (VM, part), (VM, other)] + [(VM, v) for v in strips],
        [pltpu.VMEM((80, LANES // 2), F32)],
    )
    plane = lax.all_to_all(plane, ("x", "y"), 0, 0, tiled=True)
    parts = [parts[0]] + [shift(parts[k], "x", k) for k in range(1, 4)]
    depth = call(
        plane_kernel,
        [(VM, sds((8, 80, 128), BF16))],
        [(VM, plane)] + [(VM, v) for v in parts] + [(VM, move)],
    )
    depth = lax.all_to_all(depth, ("z",), 0, 0, tiled=True)
    copies, sums1, info, loss = call(
        depth_kernel,
        [(VM, sds((8, 64, 128), BF16)), (VM, row), (VM, row), (VM, sds((1, 1)))],
        [(VM, depth), (VM, sign), (VM, ref_error)],
    )
    whole = lax.all_to_all(copies, ("x", "c"), 0, 0, tiled=True)
    grad = call(
        last_kernel,
        [(VM, sds((cells, C), BF16))],
        [(VM, sums1), (VM, info), (VM, norm1), (VM, e1), (VM, fx), (VM, u)],
        [pltpu.VMEM((ROWS * LINE, C), F32)],
    )
    feature_grad = grad.reshape(2, ROWS, COLS, C)
    whole = whole[:, :60].reshape(4, 2, 2, 3, 10, 128).transpose(2, 1, 0, 3, 5, 4).reshape(2, LANES, 10)
    whole = whole[:, :TAPS].astype(F32).reshape(2, 3, 3, C, 10)
    loss = loss.reshape(())
    return (block_out, feature_grad, whole[1], whole[0], loss)


def solution(mesh):
    fine = Mesh(mesh.devices.reshape(4, 2, 8, 4), AXES)
    cells = P(None, ("x", "c"), ("z", "y"), None)
    kernels = P(None, None, None, ("z", "y"))
    return jax.shard_map(
        body,
        mesh=fine,
        in_specs=(cells, cells) + (P(),) * 13,
        out_specs=(cells, cells, kernels, kernels, P()),
        check_vma=False,
    )
```

```python
import functools

import jax
import jax.numpy as jnp
import numpy as np
from jax import lax
from jax.experimental import pallas as pl
from jax.experimental.pallas import tpu as pltpu
from jax.sharding import Mesh
from jax.sharding import PartitionSpec as P

GROUPS = 32
TEMB = 1280
C = 320
WIDTH = C // GROUPS
ROWS, COLS = 8, 16
BAND_ROWS, BAND_COLS = 64, 512
RIM = 4
GH, GW = ROWS + 2 * RIM, COLS + 2 * RIM
LINE = 2 * GW
DEVICES = 256
LOCAL = ROWS * COLS * WIDTH
TOTAL = LOCAL * DEVICES
TAPS = 9 * C
LANES = 3072
EPS = 1e-05
F32, BF16 = jnp.float32, jnp.bfloat16
HIGH = lax.Precision.HIGHEST
VMEM_LIMIT = 63 * 2**20


def dot(a, b):
    return jnp.dot(a, b, preferred_element_type=F32)


def pieces(row):
    high = row.astype(BF16).astype(F32)
    rest = row - high
    mid = rest.astype(BF16).astype(F32)
    return high, mid, rest - mid


def hot():
    blocks = []
    for slot in range(4):
        low = (lax.broadcasted_iota(jnp.int32, (128, 384), 0) - slot * GROUPS) * WIDTH
        chan = lax.broadcasted_iota(jnp.int32, (128, 384), 1)
        blocks.append(((chan >= low) & (chan < low + WIDTH) & (chan < C)).astype(F32).astype(BF16))
    return jnp.concatenate(blocks, axis=1)


def stacked(row):
    index = lax.broadcasted_iota(jnp.int32, (16, row.shape[1]), 0)
    out = jnp.zeros((16, row.shape[1]), F32)
    for i, piece in enumerate(pieces(row)):
        out = jnp.where(index == i, piece, out)
    return out.astype(BF16)


def expand(row, table):
    wide = jnp.sum(dot(stacked(row), table), axis=0, keepdims=True)
    return [wide[:, i * 384 : i * 384 + C] for i in range(4)]


def collapse(rows, table):
    gap, empty = jnp.zeros((1, 384 - C), F32), jnp.zeros((1, C), F32)
    wide = jnp.concatenate([v for row in rows for v in (empty if row is None else row, gap)], axis=1)
    small = lax.dot_general(stacked(wide), table, (((1,), (1,)), ((), ())), preferred_element_type=F32)
    return jnp.sum(small, axis=0, keepdims=True)


def per_line(first, second):
    return jnp.concatenate(
        [jnp.broadcast_to(first, (GW, C)), jnp.broadcast_to(second, (GW, C))], axis=0
    )


def tile_lines(line, count):
    return jnp.broadcast_to(line[None], (count, LINE, C)).reshape(count * LINE, C)


def masked(values, top, count):
    high = lax.axis_index("x") * 2 + lax.axis_index("c")
    wide = lax.axis_index("z") * 4 + lax.axis_index("y")
    col = lax.broadcasted_iota(jnp.int32, (LINE, C), 0)
    gx = jnp.where(col >= GW, col - GW, col) + (wide * COLS - RIM)
    line = ((gx >= 0) & (gx < BAND_COLS)).astype(F32)
    upper = line * jnp.where(high > 0, 1.0, 0.0)
    lower = line * jnp.where(high < BAND_ROWS // ROWS - 1, 1.0, 0.0)
    parts = [(upper, RIM - top), (line, ROWS), (lower, top + count - RIM - ROWS)]
    mask = jnp.concatenate([jnp.broadcast_to(v[None], (n, LINE, C)) for v, n in parts], axis=0)
    return values * mask.reshape(count * LINE, C)


def center_line():
    col = lax.broadcasted_iota(jnp.int32, (LINE, C), 0)
    one = (col >= RIM) & (col < RIM + COLS)
    two = (col >= GW + RIM) & (col < GW + RIM + COLS)
    return one.astype(F32), two.astype(F32)


def line_sums(values):
    total = jnp.sum(values.reshape(ROWS, LINE, C), axis=0)
    return [jnp.sum(total * line, axis=0, keepdims=True) for line in center_line()]


def norm_rows(stats_ref, table):
    stats = stats_ref[...]
    sums = jnp.sum(stats, axis=0, keepdims=True)
    mean = sums * (1.0 / DEVICES)
    off = stats - mean
    spread = jnp.sum(off * off, axis=0, keepdims=True) * LOCAL
    var = (sums + pltpu.roll(spread, 64, 1)) * (1.0 / TOTAL)
    lane = lax.broadcasted_iota(jnp.int32, (1, 128), 1)
    row = jnp.where(lane < 64, mean, 1.0 / jnp.sqrt(jnp.maximum(var, 0.0) + EPS))
    return expand(row, table)


def norm_lines(rows):
    return per_line(rows[0], rows[1]), per_line(rows[2], rows[3])


def kept_rows(ref):
    return [ref[i : i + 1, :] for i in range(4)]


def keep_rows(ref, rows):
    for i, row in enumerate(rows):
        ref[i : i + 1, :] = row


def moments(values, table):
    first, second = line_sums(values)
    means = collapse([first, second, None, None], table) * (1.0 / LOCAL)
    one, two, _, _ = expand(means, table)
    off = values - tile_lines(per_line(one, two), ROWS)
    first, second = line_sums(off * off)
    return means + collapse([None, None, first, second], table)


def pair_sums(scaled, normed, table):
    return collapse(line_sums(scaled) + line_sums(scaled * normed), table)


def sigmoid(v):
    return 0.5 + 0.5 * jnp.tanh(0.5 * v)


def silu_slope(v):
    sig = sigmoid(v)
    return sig * (1.0 + v * (1.0 - sig))


def spread_taps(ref, values):
    count = values.shape[0]
    ref[:, 0:C] = pltpu.roll(values, 1, 0).astype(BF16)
    ref[:, C : 2 * C] = values.astype(BF16)
    ref[:, 2 * C : 3 * C] = pltpu.roll(values, count - 1, 0).astype(BF16)


def conv_lines(ref, weights_ref, count):
    total = dot(ref[0 : count * LINE, :], weights_ref[0])
    for ky in range(1, 3):
        total = total + dot(ref[ky * LINE : (ky + count) * LINE, :], weights_ref[ky])
    return total


def turn_taps(ref, weights_ref):
    for ky in range(3):
        for kx in range(3):
            ref[ky, :, kx * C : (kx + 1) * C] = weights_ref[2 - ky, 2 - kx]


def conv_turned(ref, weights_ref, count):
    total = None
    for ky in range(3):
        part = lax.dot_general(
            ref[ky * LINE : (ky + count) * LINE, :],
            weights_ref[ky],
            (((1,), (1,)), ((), ())),
            preferred_element_type=F32,
        )
        total = part if total is None else total + part
    return total


def kernel_grad(mine_ref, theirs_ref, taps_ref, top, grads, order_ref):
    core = lax.axis_index("c")
    left = lax.dot_general(
        order_ref[...], grads.astype(BF16), (((1,), (1,)), ((), ())), preferred_element_type=F32
    ).astype(BF16)
    parts = []
    for ky in range(3):
        lines = taps_ref[(top + ky) * LINE : (top + ky + ROWS) * LINE, :]
        parts.append(dot(left, lines).astype(BF16))
    parts.append(jnp.zeros((C, LANES - TAPS), BF16))
    whole = jnp.concatenate(parts, axis=1)
    low, high = whole[:, : LANES // 2], whole[:, LANES // 2 :]

    @pl.when(core == 0)
    def _():
        mine_ref[...] = low
        theirs_ref[...] = high

    @pl.when(core == 1)
    def _():
        mine_ref[...] = high
        theirs_ref[...] = low


def fetch(sems, index, src, dst):
    copy = pltpu.make_async_copy(src, dst, sems.at[index])
    copy.start()
    return copy


def fetch_all(sems, first, pairs):
    return [fetch(sems, first + i, src, dst) for i, (src, dst) in enumerate(pairs)]


def wait_all(copies):
    for copy in copies:
        copy.wait()


def flat(ref):
    return ref[...].reshape(1, C)


def moments_kernel(x_ref, t_ref, out_ref, near_ref, far_ref):
    half, core = ROWS * COLS, lax.axis_index("c")
    for b in range(2):
        at, to = b * half, b * 6 * COLS
        parts = [
            (x_ref[at + 4 * COLS : at + 8 * COLS, :], x_ref[at : at + 4 * COLS, :], to, 4 * COLS),
            (t_ref[at + 6 * COLS : at + 8 * COLS, :], t_ref[at : at + 2 * COLS, :], to + 4 * COLS, 2 * COLS),
        ]
        for bottom, top, first, count in parts:
            near_ref[first : first + count] = jnp.where(core == 0, bottom, top)
            far_ref[first : first + count] = jnp.where(core == 0, top, bottom)
    table = hot()
    values = [x_ref[b * half : (b + 1) * half, :].astype(F32) for b in range(2)]
    sums = [jnp.sum(v, axis=0, keepdims=True) for v in values]
    means = collapse(sums + [None, None], table) * (1.0 / LOCAL)
    offs = [v - m for v, m in zip(values, expand(means, table))]
    sums = [jnp.sum(v * v, axis=0, keepdims=True) for v in offs]
    out = means + collapse([None, None] + sums, table)
    out_ref[...] = jnp.broadcast_to(out, (DEVICES, 128))


def strip_blocks():
    out, row = [], 0
    for b in range(2):
        low, high = 512 + b * 6 * COLS, 704 + b * 6 * COLS
        for y in range(GH):
            start = low + y * COLS if y < 4 else b * 128 + (y - 4) * COLS if y < 12 else high + (y - 12) * COLS
            out.append((row, RIM, start, y * LINE + b * GW))
            row += RIM
        for y in range(12):
            start = low + (4 + y) * COLS if y < 2 else 256 + b * 128 + (y - 2) * COLS if y < 10 else high + (y - 6) * COLS
            out.append((row, 2, start, (GH + y) * LINE + b * GW))
            row += 2
    return out


def widened(scr, x_ref, t_ref, near_ref, far_ref):
    core = lax.axis_index("c")
    near, far = near_ref[...].astype(F32), far_ref[...].astype(F32)
    scr[0:256] = x_ref[...].astype(F32)
    scr[256:512] = t_ref[...].astype(F32)
    scr[512:704] = jnp.where(core == 0, far, near)
    scr[704:896] = jnp.where(core == 0, near, far)


def pack_kernel(x_ref, t_ref, near_ref, far_ref, right_ref, left_ref, scr, right, left):
    widened(scr, x_ref, t_ref, near_ref, far_ref)
    for row, width, start, _ in strip_blocks():
        left[row : row + width] = scr[start : start + width]
        right[row : row + width] = scr[start + COLS - width : start + COLS]
    even = lax.rem(lax.axis_index("y"), 2) == 0
    right_ref[...] = jnp.where(even, right[...], left[...]).astype(BF16)
    left_ref[...] = jnp.where(even, left[...], right[...]).astype(BF16)


def grid_kernel(x_ref, t_ref, near_ref, far_ref, first_ref, last_ref, f_ref, g_ref, scr, first, last, grid):
    widened(scr, x_ref, t_ref, near_ref, far_ref)
    even = lax.rem(lax.axis_index("y"), 2) == 0
    first[...] = jnp.where(even, first_ref[...].astype(F32), last_ref[...].astype(F32))
    last[...] = jnp.where(even, last_ref[...].astype(F32), first_ref[...].astype(F32))
    empty = jnp.zeros((2, C), F32)
    for row, width, start, at in strip_blocks():
        inner = at + RIM
        grid[inner - width : inner] = first[row : row + width]
        grid[inner : inner + COLS] = scr[start : start + COLS]
        grid[inner + COLS : inner + COLS + width] = last[row : row + width]
        if width == 2:
            grid[at : at + 2] = empty
            grid[at + GW - 2 : at + GW] = empty
    f_ref[...] = grid[0 : GH * LINE].astype(BF16)
    g_ref[...] = grid[GH * LINE : (GH + 12) * LINE].astype(BF16)


def first_kernel(
    stats_hbm, gain_hbm, shift_hbm, bias_hbm, temb_hbm, x_hbm, w_hbm,
    out_hbm, rows_hbm, h_hbm, taps_hbm, scr, w_ref, x_ref, h_ref, out_ref, rows_ref,
    stats_ref, gain_ref, shift_ref, bias_ref, temb_ref, sems,
):
    small = fetch_all(
        sems, 4,
        [
            (stats_hbm, stats_ref), (gain_hbm, gain_ref), (shift_hbm, shift_ref),
            (bias_hbm, bias_ref), (temb_hbm, temb_ref),
        ],
    )
    xs = fetch(sems, 2, x_hbm, x_ref)
    weights = fetch(sems, 0, w_hbm, w_ref)
    table = hot()
    wait_all(small)
    rows = norm_rows(stats_ref, table)
    keep_rows(rows_ref, rows)
    kept = fetch(sems, 9, rows_ref, rows_hbm)
    mean, rstd = norm_lines(rows)
    scale = tile_lines(rstd * flat(gain_ref), GH)
    xs.wait()
    n1 = (x_ref[...].astype(F32) - tile_lines(mean, GH)) * scale + flat(shift_ref)
    spread_taps(scr, masked(n1 * sigmoid(n1), 0, GH))
    taps = fetch(sems, 1, scr.at[3 * LINE : 13 * LINE, :], taps_hbm)
    weights.wait()
    h1 = conv_lines(scr, w_ref, GH - 2) + (flat(bias_ref) + flat(temb_ref))
    h_ref[...] = h1
    hs = fetch(sems, 3, h_ref, h_hbm)
    out_ref[...] = jnp.broadcast_to(moments(h1[3 * LINE : 11 * LINE], table), (DEVICES, 128))
    outs = fetch(sems, 10, out_ref, out_hbm)
    wait_all([taps, hs, kept, outs])


def second_kernel(
    stats_hbm, gain_hbm, shift_hbm, bias_hbm, sign_hbm, h_hbm, w_hbm, wt_hbm, x_hbm, t_hbm, order_hbm,
    out_hbm, err_hbm, rows_hbm, n_hbm, e_hbm, bout_hbm, u_hbm, mine_hbm, theirs_hbm,
    scr_a, scr_u, w_ref, wt_ref, x_ref, t_ref, order_ref, bout_ref, u_ref, mine_ref, theirs_ref, h_ref, e_ref, turn_ref,
    out_ref, err_ref, rows_ref, n_ref, stats_ref, gain_ref, shift_ref, bias_ref, sign_ref, sems,
):
    small = fetch_all(
        sems, 11,
        [
            (stats_hbm, stats_ref), (gain_hbm, gain_ref), (shift_hbm, shift_ref),
            (bias_hbm, bias_ref), (sign_hbm, sign_ref),
        ],
    )
    hs = fetch(sems, 9, h_hbm, h_ref)
    weights = fetch(sems, 0, w_hbm, w_ref)
    xs = fetch(sems, 1, x_hbm.at[2 * LINE : 14 * LINE, :], x_ref)
    ts = fetch(sems, 2, t_hbm, t_ref)
    orders = fetch(sems, 4, order_hbm, order_ref)
    turned = fetch(sems, 3, wt_hbm, wt_ref)
    table = hot()
    wait_all(small)
    rows = norm_rows(stats_ref, table)
    keep_rows(rows_ref, rows)
    mean, rstd = norm_lines(rows)
    hs.wait()
    nhat = (h_ref[...] - tile_lines(mean, GH - 2)) * tile_lines(rstd, GH - 2)
    n_ref[...] = nhat[2 * LINE : 12 * LINE]
    kept = fetch_all(sems, 16, [(rows_ref, rows_hbm), (n_ref, n_hbm)])
    n2 = nhat * flat(gain_ref) + flat(shift_ref)
    spread_taps(scr_a, masked(n2 * sigmoid(n2), 1, GH - 2))
    weights.wait()
    conv = conv_lines(scr_a, w_ref, 12) + flat(bias_ref)
    xs.wait()
    out = x_ref[...].astype(F32) + conv
    bout_ref[...] = out[2 * LINE : 10 * LINE].astype(BF16)
    bouts = fetch(sems, 5, bout_ref, bout_hbm)
    ts.wait()
    diff = out - t_ref[...].astype(F32)
    mid = diff[2 * LINE : 10 * LINE]
    lane = lax.broadcasted_iota(jnp.int32, (1, 128), 1)
    errs = jnp.zeros((1, 128), F32)
    for b, part in enumerate(line_sums(mid * mid)):
        errs = errs + jnp.where(lane == b, jnp.sum(part, axis=1, keepdims=True), 0.0)
    err_ref[...] = errs
    sign = tile_lines(per_line(flat(sign_ref), -flat(sign_ref)), 12)
    u = masked(diff * sign, 2, 12)
    spread_taps(scr_u, u)
    center = u[2 * LINE : 10 * LINE]
    u_ref[...] = center.astype(BF16)
    us = fetch(sems, 6, u_ref, u_hbm)
    one, two = center_line()
    orders.wait()
    kernel_grad(mine_ref, theirs_ref, scr_a, 2, center * tile_lines(one + two, ROWS), order_ref)
    mines = fetch(sems, 7, mine_ref, mine_hbm)
    others = fetch(sems, 8, theirs_ref, theirs_hbm)
    turned.wait()
    turn_taps(turn_ref, wt_ref)
    da2 = conv_turned(scr_u, turn_ref, 10)
    e = da2 * silu_slope(n2[2 * LINE : 12 * LINE]) * flat(gain_ref)
    e_ref[...] = e
    es = fetch(sems, 10, e_ref, e_hbm)
    sums = pair_sums(e[LINE : 9 * LINE], nhat[3 * LINE : 11 * LINE], table)
    out_ref[...] = jnp.broadcast_to(sums, (DEVICES, 128))
    outs = fetch_all(sems, 18, [(out_ref, out_hbm), (err_ref, err_hbm)])
    wait_all([bouts, us, mines, others, es] + kept + outs)


def back_line(sums_ref, table):
    sums = jnp.sum(sums_ref[...], axis=0, keepdims=True) * (1.0 / TOTAL)
    one, two, three, four = expand(sums, table)
    return per_line(one, two), per_line(three, four)


def third_kernel(
    second_hbm, sums_hbm, first_hbm, gain_hbm, shift_hbm, errs_hbm, e_hbm, n_hbm, taps_hbm, order_hbm, x_hbm, wt_hbm,
    out_hbm, mine_hbm, theirs_hbm, back_hbm,
    out_ref, second_ref, sums_ref, first_ref, gain_ref, shift_ref, errs_ref, e_ref, n_ref, taps_ref, order_ref, x_ref, wt_ref,
    mine_ref, theirs_ref, back_ref, turn_ref, scr, sems,
):
    small = fetch_all(sems, 0, [(second_hbm, second_ref), (sums_hbm, sums_ref)])
    main = fetch_all(sems, 2, [(n_hbm, n_ref), (e_hbm, e_ref)])
    grads = fetch_all(sems, 4, [(order_hbm, order_ref), (taps_hbm, taps_ref)])
    rest = fetch_all(
        sems, 6,
        [
            (first_hbm, first_ref), (gain_hbm, gain_ref), (shift_hbm, shift_ref), (errs_hbm, errs_ref),
            (x_hbm.at[4 * LINE : 12 * LINE, :], x_ref), (wt_hbm, wt_ref),
        ],
    )
    table = hot()
    wait_all(small)
    first, second = back_line(sums_ref, table)
    scale = tile_lines(norm_lines(kept_rows(second_ref))[1], 10)
    wait_all(main)
    dh = scale * (e_ref[...] - tile_lines(first, 10) - n_ref[...] * tile_lines(second, 10))
    dh = masked(dh, 3, 10)
    spread_taps(scr, dh)
    one, two = center_line()
    wait_all(grads)
    kernel_grad(mine_ref, theirs_ref, taps_ref, 0, dh[LINE : 9 * LINE] * tile_lines(one + two, ROWS), order_ref)
    outs = fetch_all(sems, 12, [(theirs_ref, theirs_hbm), (mine_ref, mine_hbm)])
    wait_all(rest)
    mean, rstd = norm_lines(kept_rows(first_ref))
    nhat = (x_ref[...].astype(F32) - tile_lines(mean, ROWS)) * tile_lines(rstd, ROWS)
    n1 = nhat * flat(gain_ref) + flat(shift_ref)
    turn_taps(turn_ref, wt_ref)
    e1 = conv_turned(scr, turn_ref, ROWS) * (silu_slope(n1) * flat(gain_ref))
    back_ref[...] = e1
    outs = outs + [fetch(sems, 14, back_ref, back_hbm)]
    out_ref[0:1] = pair_sums(e1, nhat, table)
    out_ref[1:2] = errs_ref[...]
    wait_all(outs + [fetch(sems, 15, out_ref, out_hbm)])


def last_kernel(sums_ref, info_ref, norm_ref, e_ref, x_ref, u_ref, out_ref, scr):
    weight = info_ref[0:1, 0:1]
    table = hot()
    mean, rstd = norm_lines(kept_rows(norm_ref))
    first, second = back_line(sums_ref, table)
    scale = tile_lines(rstd, ROWS)
    nhat = (x_ref[4 * LINE : 12 * LINE, :].astype(F32) - tile_lines(mean, ROWS)) * scale
    dx = scale * (e_ref[...] - tile_lines(first, ROWS) - nhat * tile_lines(second, ROWS))
    scr[...] = (u_ref[...].astype(F32) + dx) * weight
    centered(out_ref, scr)


def piece_rows(count, at, sums, errs):
    index = lax.broadcasted_iota(jnp.int32, (count, 128), 0)
    out = jnp.zeros((count, 128), F32)
    for i, piece in enumerate(pieces(sums) + pieces(errs)):
        out = out + jnp.where(index == at + i, piece, 0.0)
    return out


def centered(out_ref, scr):
    for b in range(2):
        for y in range(ROWS):
            at = y * LINE + b * GW + RIM
            out_ref[(b * ROWS + y) * COLS : (b * ROWS + y + 1) * COLS] = scr[at : at + COLS].astype(BF16)


def early_kernel(mine_ref, got_ref, lines_ref, block_ref, *outs):
    outs, scr = outs[:4], outs[4]
    scr[...] = lines_ref[...].astype(F32)
    centered(block_ref, scr)
    y = lax.axis_index("y")
    for k, out_ref in enumerate(outs):
        rows = pl.ds(pl.multiple_of(lax.rem(y + k, 4) * 80, 16), 80)
        out_ref[...] = (mine_ref[rows, :].astype(F32) + got_ref[rows, :].astype(F32)).astype(BF16)


def late_kernel(mine_ref, got_ref, part_ref, other_ref, a_ref, b_ref, c_ref, d_ref, out_ref, *outs):
    for j in range(4):
        for i in range(4):
            for k in range(3):
                rows = slice(j * 80, (j + 1) * 80)
                lanes = slice(i * 384 + k * 128, i * 384 + (k + 1) * 128)
                both = mine_ref[rows, lanes].astype(F32) + got_ref[rows, lanes].astype(F32)
                out_ref[j * 4 + i, k * 80 : (k + 1) * 80, :] = both.astype(BF16)
    tails = part_ref[...] + other_ref[...]
    rows = piece_rows(16, 0, tails[0:1], tails[1:2]).astype(BF16)
    for i in range(16):
        out_ref[i, 240:256, :] = rows
    outs, scr = outs[:4], outs[4]
    scr[...] = (
        (a_ref[...].astype(F32) + b_ref[...].astype(F32)) + (c_ref[...].astype(F32) + d_ref[...].astype(F32))
    )
    x = lax.axis_index("x")
    for i, out_ref in enumerate(outs):
        for k in range(3):
            lanes = pl.ds(pl.multiple_of(lax.rem(x + i, 4) * 384 + k * 128, 128), 128)
            out_ref[k * 80 : (k + 1) * 80] = scr[:, lanes].astype(BF16)


def plane_kernel(in_ref, a_ref, b_ref, c_ref, d_ref, move_ref, out_ref):
    total = in_ref[0].astype(F32)
    for i in range(1, 16):
        total = total + in_ref[i].astype(F32)
    tail = total[240:256]
    sums = tail[0:1] + tail[1:2] + tail[2:3]
    errs = tail[3:4] + tail[4:5] + tail[5:6]
    rows = piece_rows(80, 60, sums, errs)
    other = (a_ref[...].astype(F32) + b_ref[...].astype(F32)) + (c_ref[...].astype(F32) + d_ref[...].astype(F32))
    both = jnp.concatenate([other, total[0:240]], axis=0).astype(BF16)
    moved = dot(move_ref[...], both)
    for z in range(8):
        out_ref[z] = (moved[z * 80 : (z + 1) * 80] + rows).astype(BF16)


def depth_kernel(in_ref, sign_ref, ref_ref, out_ref, sums_ref, info_ref, loss_ref):
    total = in_ref[0].astype(F32)
    for i in range(1, 8):
        total = total + in_ref[i].astype(F32)
    sums_ref[...] = total[60:61] + total[61:62] + total[62:63]
    errs = total[63:64] + total[64:65] + total[65:66]
    excess = errs[:, 0:2] * (1.0 / (BAND_ROWS * BAND_COLS * C)) - ref_ref[...]
    gap = 0.5 * flat(sign_ref)[:, 0:1] * (excess[:, 0:1] - excess[:, 1:2])
    weight = 1.0 / (1.0 + jnp.exp(-gap))
    loss = jnp.maximum(gap, 0.0) + jnp.log1p(jnp.exp(-jnp.abs(gap)))
    info_ref[...] = jnp.broadcast_to(weight, (1, 128))
    loss_ref[...] = loss
    grads = (total[0:64] * (weight * (2 * BAND_ROWS * BAND_COLS) ** -0.5)).astype(BF16)
    for i in range(8):
        out_ref[i] = grads


VM = pl.BlockSpec(memory_space=pltpu.VMEM)
HB = pl.BlockSpec(memory_space=pltpu.HBM)
DMA = pltpu.SemaphoreType.DMA


def call(kernel, outs, ins, scratch=(), flops=0):
    size = sum(int(np.prod(s.shape)) * s.dtype.itemsize for _, s in outs)
    size += sum(a.size * a.dtype.itemsize for _, a in ins)
    many = len(outs) > 1
    shapes, spaces = [s for _, s in outs], [p for p, _ in outs]
    return pl.pallas_call(
        kernel,
        out_shape=tuple(shapes) if many else shapes[0],
        in_specs=[p for p, _ in ins],
        out_specs=tuple(spaces) if many else spaces[0],
        scratch_shapes=list(scratch),
        compiler_params=pltpu.CompilerParams(vmem_limit_bytes=VMEM_LIMIT),
        cost_estimate=pl.CostEstimate(flops=flops, bytes_accessed=size, transcendentals=0),
    )(*[a for _, a in ins])


def sds(shape, dtype=F32):
    return jax.ShapeDtypeStruct(shape, dtype)


AXES = ("x", "c", "z", "y")


def share(rows):
    return lax.all_to_all(rows, AXES, 0, 0, tiled=True)


def widen(features, target, near, far):
    strip, wide = sds((176, C), BF16), pltpu.VMEM((896, C), F32)
    edge = pltpu.VMEM((176, C), F32)
    ins = [(VM, features), (VM, target), (VM, near), (VM, far)]
    right, left = call(pack_kernel, [(VM, strip), (VM, strip)], ins, [wide, edge, edge])
    inner = [(i, i ^ 1) for i in range(32)]
    outer = [(i, ((i - 1) ^ 1) + 1) for i in range(1, 31)]
    first = lax.ppermute(left, ("z", "y"), outer)
    last = lax.ppermute(right, ("z", "y"), inner)
    f, t = call(
        grid_kernel,
        [(VM, sds((GH * LINE, C), BF16)), (VM, sds((12 * LINE, C), BF16))],
        ins + [(VM, first), (VM, last)],
        [wide, edge, edge, pltpu.VMEM(((GH + 12) * LINE, C), F32)],
    )
    return f, t


def time_embed(timestep, time_weight, time_bias):
    half = TEMB // 2
    freqs = jnp.exp(-jnp.log(10000.0) * jnp.arange(half, dtype=F32) / half)
    angles = timestep.astype(F32)[:, None] * freqs[None, :]
    emb = jnp.concatenate([jnp.cos(angles), jnp.sin(angles)], axis=1)
    return jnp.dot(jax.nn.silu(emb), time_weight.astype(F32), precision=HIGH) + time_bias


def order_matrix():
    out = np.zeros((C, C), np.float32)
    for z in range(8):
        for y in range(4):
            for j in range(10):
                out[y * 80 + z * 10 + j, z * 40 + y * 10 + j] = 1.0
    return jnp.asarray(out, BF16)


def move_matrix():
    out = np.zeros((640, 480), np.float32)
    for grad in range(2):
        for k in range(3):
            for z in range(8):
                for j in range(10):
                    out[z * 80 + grad * 30 + k * 10 + j, grad * 240 + k * 80 + z * 10 + j] = 1.0
    return jnp.asarray(out, BF16)


def shift(block, axis, by):
    return lax.ppermute(block, axis, [(i, (i + by) % 4) for i in range(4)])


def swap(theirs):
    return lax.ppermute(theirs, "c", [(0, 1), (1, 0)])


def body(
    features, target, norm1_gain, norm1_shift, kernel1, bias1, time_weight, time_bias,
    norm2_gain, norm2_shift, kernel2, bias2, ref_error, preference, timestep,
):
    sign = jnp.broadcast_to(jnp.where(preference == 0, 2.0, -2.0).astype(F32), (C,))
    strip, cells = sds((2 * 6 * COLS, C), BF16), 2 * ROWS * COLS
    part, near, far = call(
        moments_kernel,
        [(VM, sds((DEVICES, 128))), (VM, strip), (VM, strip)],
        [(VM, features.reshape(cells, C)), (VM, target.reshape(cells, C))],
    )
    far = lax.ppermute(far, ("x", "c"), [(1, 2), (2, 1), (3, 4), (4, 3), (5, 6), (6, 5)])
    near = swap(near)
    part, far = lax.optimization_barrier((part, far))
    stats1 = share(part)
    fx, tx = widen(features.reshape(cells, C), target.reshape(cells, C), near, far)
    temb = time_embed(timestep, time_weight, time_bias).reshape(C)
    order, move = order_matrix(), move_matrix()
    w1, w2 = kernel1.reshape(3, 3 * C, C), kernel2.reshape(3, 3 * C, C)
    conv_flops = 2 * 9 * C * C * LINE
    half = sds((C, LANES // 2), BF16)
    row, table, lines = sds((1, 128)), sds((DEVICES, 128)), sds((ROWS * LINE, C), BF16)
    full = sds((3, 3, C, C), BF16)
    rows4, tbl = sds((4, C)), pltpu.VMEM((DEVICES, 128), F32)
    part, norm1, h1, taps1 = call(
        first_kernel,
        [(HB, table), (HB, rows4), (HB, sds((14 * LINE, C))), (HB, sds((10 * LINE, 3 * C), BF16))],
        [(HB, v) for v in (stats1, norm1_gain, norm1_shift, bias1, temb, fx, w1)],
        [
            pltpu.VMEM((GH * LINE, 3 * C), BF16), pltpu.VMEM((3, 3 * C, C), BF16),
            pltpu.VMEM((GH * LINE, C), BF16), pltpu.VMEM((14 * LINE, C), F32), tbl, pltpu.VMEM((4, C), F32),
            tbl, *[pltpu.VMEM((C,), F32)] * 4, DMA((11,)),
        ],
        14 * conv_flops,
    )
    stats2 = share(part)
    part, errs, norm2, nhat2, e2, bout, u, mine2, theirs2 = call(
        second_kernel,
        [
            (HB, table), (HB, row), (HB, rows4), (HB, sds((10 * LINE, C))), (HB, sds((10 * LINE, C))), (HB, lines), (HB, lines), (HB, half), (HB, half),
        ],
        [
            (HB, v)
            for v in (stats2, norm2_gain, norm2_shift, bias2, sign, h1, w2, kernel2, fx, tx, order)
        ],
        [
            pltpu.VMEM((14 * LINE, 3 * C), BF16), pltpu.VMEM((12 * LINE, 3 * C), BF16),
            pltpu.VMEM((3, 3 * C, C), BF16), pltpu.VMEM(full.shape, BF16),
            pltpu.VMEM((12 * LINE, C), BF16), pltpu.VMEM((12 * LINE, C), BF16), pltpu.VMEM((C, C), BF16),
            pltpu.VMEM((ROWS * LINE, C), BF16), pltpu.VMEM((ROWS * LINE, C), BF16),
            pltpu.VMEM((C, LANES // 2), BF16), pltpu.VMEM((C, LANES // 2), BF16),
            pltpu.VMEM((14 * LINE, C), F32), pltpu.VMEM((10 * LINE, C), F32), pltpu.VMEM((3, C, 3 * C), BF16),
            tbl, pltpu.VMEM((1, 128), F32), pltpu.VMEM((4, C), F32), pltpu.VMEM((10 * LINE, C), F32),
            tbl, *[pltpu.VMEM((C,), F32)] * 4, DMA((20,)),
        ],
        30 * conv_flops,
    )
    sums2 = share(part)
    got2 = swap(theirs2)
    block_out, *strips = call(
        early_kernel,
        [(VM, sds((cells, C), BF16))] + [(VM, sds((80, LANES // 2), BF16))] * 4,
        [(VM, mine2), (VM, got2), (VM, bout)],
        [pltpu.VMEM((ROWS * LINE, C), F32)],
    )
    block_out = block_out.reshape(2, ROWS, COLS, C)
    strips = [strips[0]] + [shift(strips[k], "y", k) for k in (2, 1, 3)]
    sums2, strips[0] = lax.optimization_barrier((sums2, strips[0]))
    part, mine1, theirs1, e1 = call(
        third_kernel,
        [(HB, sds((2, 128))), (HB, half), (HB, half), (HB, sds((ROWS * LINE, C)))],
        [
            (HB, v)
            for v in (
                norm2, sums2, norm1, norm1_gain, norm1_shift, errs, e2, nhat2, taps1, order, fx, kernel1,
            )
        ],
        [
            pltpu.VMEM((2, 128), F32), pltpu.VMEM((4, C), F32), tbl, pltpu.VMEM((4, C), F32),
            *[pltpu.VMEM((C,), F32)] * 2, pltpu.VMEM((1, 128), F32),
            pltpu.VMEM((10 * LINE, C), F32), pltpu.VMEM((10 * LINE, C), F32),
            pltpu.VMEM((10 * LINE, 3 * C), BF16), pltpu.VMEM((C, C), BF16),
            pltpu.VMEM((ROWS * LINE, C), BF16), pltpu.VMEM(full.shape, BF16),
            pltpu.VMEM(half.shape, BF16), pltpu.VMEM(half.shape, BF16), pltpu.VMEM((ROWS * LINE, C), F32),
            pltpu.VMEM((3, C, 3 * C), BF16),
            pltpu.VMEM((10 * LINE, 3 * C), BF16), DMA((16,)),
        ],
        16 * conv_flops,
    )
    theirs1, *strips = lax.optimization_barrier((theirs1, *strips))
    got1, other = swap(theirs1), swap(part)
    plane, *parts = call(
        late_kernel,
        [(VM, sds((16, 256, 128), BF16))] + [(VM, sds((240, 128), BF16))] * 4,
        [(VM, mine1), (VM, got1), (VM, part), (VM, other)] + [(VM, v) for v in strips],
        [pltpu.VMEM((80, LANES // 2), F32)],
    )
    plane = lax.all_to_all(plane, ("y", "x"), 0, 0, tiled=True)
    parts = [parts[0]] + [shift(parts[k], "x", k) for k in range(1, 4)]
    depth = call(
        plane_kernel,
        [(VM, sds((8, 80, 128), BF16))],
        [(VM, plane)] + [(VM, v) for v in parts] + [(VM, move)],
    )
    depth = lax.all_to_all(depth, ("z",), 0, 0, tiled=True)
    copies, sums1, info, loss = call(
        depth_kernel,
        [(VM, sds((8, 64, 128), BF16)), (VM, row), (VM, row), (VM, sds((1, 1)))],
        [(VM, depth), (VM, sign), (VM, ref_error)],
    )
    whole = lax.all_to_all(copies, ("x", "c"), 0, 0, tiled=True)
    grad = call(
        last_kernel,
        [(VM, sds((cells, C), BF16))],
        [(VM, sums1), (VM, info), (VM, norm1), (VM, e1), (VM, fx), (VM, u)],
        [pltpu.VMEM((ROWS * LINE, C), F32)],
    )
    feature_grad = grad.reshape(2, ROWS, COLS, C)
    whole = whole[:, :60].reshape(4, 2, 2, 3, 10, 128).transpose(2, 1, 0, 3, 5, 4).reshape(2, LANES, 10)
    whole = whole[:, :TAPS].astype(F32).reshape(2, 3, 3, C, 10)
    loss = loss.reshape(())
    return (block_out, feature_grad, whole[1], whole[0], loss)


def solution(mesh):
    fine = Mesh(mesh.devices.reshape(4, 2, 8, 4), AXES)
    cells = P(None, ("x", "c"), ("z", "y"), None)
    kernels = P(None, None, None, ("z", "y"))
    return jax.shard_map(
        body,
        mesh=fine,
        in_specs=(cells, cells) + (P(),) * 13,
        out_specs=(cells, cells, kernels, kernels, P()),
        check_vma=False,
    )
```

```python
import functools

import jax
import jax.numpy as jnp
import numpy as np
from jax import lax
from jax.experimental import pallas as pl
from jax.experimental.pallas import tpu as pltpu
from jax.sharding import Mesh
from jax.sharding import PartitionSpec as P

GROUPS = 32
TEMB = 1280
C = 320
WIDTH = C // GROUPS
ROWS, COLS = 8, 16
BAND_ROWS, BAND_COLS = 64, 512
RIM = 4
GH, GW = ROWS + 2 * RIM, COLS + 2 * RIM
LINE = 2 * GW
DEVICES = 256
LOCAL = ROWS * COLS * WIDTH
TOTAL = LOCAL * DEVICES
TAPS = 9 * C
LANES = 3072
EPS = 1e-05
F32, BF16 = jnp.float32, jnp.bfloat16
HIGH = lax.Precision.HIGHEST
VMEM_LIMIT = 63 * 2**20


def dot(a, b):
    return jnp.dot(a, b, preferred_element_type=F32)


def pieces(row):
    high = row.astype(BF16).astype(F32)
    rest = row - high
    mid = rest.astype(BF16).astype(F32)
    return high, mid, rest - mid


def hot():
    blocks = []
    for slot in range(4):
        low = (lax.broadcasted_iota(jnp.int32, (128, 384), 0) - slot * GROUPS) * WIDTH
        chan = lax.broadcasted_iota(jnp.int32, (128, 384), 1)
        blocks.append(((chan >= low) & (chan < low + WIDTH) & (chan < C)).astype(F32).astype(BF16))
    return jnp.concatenate(blocks, axis=1)


def stacked(row):
    index = lax.broadcasted_iota(jnp.int32, (16, row.shape[1]), 0)
    out = jnp.zeros((16, row.shape[1]), F32)
    for i, piece in enumerate(pieces(row)):
        out = jnp.where(index == i, piece, out)
    return out.astype(BF16)


def expand(row, table):
    wide = jnp.sum(dot(stacked(row), table), axis=0, keepdims=True)
    return [wide[:, i * 384 : i * 384 + C] for i in range(4)]


def collapse(rows, table):
    gap, empty = jnp.zeros((1, 384 - C), F32), jnp.zeros((1, C), F32)
    wide = jnp.concatenate([v for row in rows for v in (empty if row is None else row, gap)], axis=1)
    small = lax.dot_general(stacked(wide), table, (((1,), (1,)), ((), ())), preferred_element_type=F32)
    return jnp.sum(small, axis=0, keepdims=True)


def per_line(first, second):
    return jnp.concatenate(
        [jnp.broadcast_to(first, (GW, C)), jnp.broadcast_to(second, (GW, C))], axis=0
    )


def tile_lines(line, count):
    return jnp.broadcast_to(line[None], (count, LINE, C)).reshape(count * LINE, C)


def masked(values, top, count):
    high = lax.axis_index("x") * 2 + lax.axis_index("c")
    wide = lax.axis_index("z") * 4 + lax.axis_index("y")
    col = lax.broadcasted_iota(jnp.int32, (LINE, C), 0)
    gx = jnp.where(col >= GW, col - GW, col) + (wide * COLS - RIM)
    line = ((gx >= 0) & (gx < BAND_COLS)).astype(F32)
    upper = line * jnp.where(high > 0, 1.0, 0.0)
    lower = line * jnp.where(high < BAND_ROWS // ROWS - 1, 1.0, 0.0)
    parts = [(upper, RIM - top), (line, ROWS), (lower, top + count - RIM - ROWS)]
    mask = jnp.concatenate([jnp.broadcast_to(v[None], (n, LINE, C)) for v, n in parts], axis=0)
    return values * mask.reshape(count * LINE, C)


def center_line():
    col = lax.broadcasted_iota(jnp.int32, (LINE, C), 0)
    one = (col >= RIM) & (col < RIM + COLS)
    two = (col >= GW + RIM) & (col < GW + RIM + COLS)
    return one.astype(F32), two.astype(F32)


def line_sums(values):
    total = jnp.sum(values.reshape(ROWS, LINE, C), axis=0)
    return [jnp.sum(total * line, axis=0, keepdims=True) for line in center_line()]


def norm_rows(stats_ref, table):
    stats = stats_ref[...]
    sums = jnp.sum(stats, axis=0, keepdims=True)
    mean = sums * (1.0 / DEVICES)
    off = stats - mean
    spread = jnp.sum(off * off, axis=0, keepdims=True) * LOCAL
    var = (sums + pltpu.roll(spread, 64, 1)) * (1.0 / TOTAL)
    lane = lax.broadcasted_iota(jnp.int32, (1, 128), 1)
    row = jnp.where(lane < 64, mean, 1.0 / jnp.sqrt(jnp.maximum(var, 0.0) + EPS))
    return expand(row, table)


def norm_lines(rows):
    return per_line(rows[0], rows[1]), per_line(rows[2], rows[3])


def kept_rows(ref):
    return [ref[i : i + 1, :] for i in range(4)]


def keep_rows(ref, rows):
    for i, row in enumerate(rows):
        ref[i : i + 1, :] = row


def moments(values, table):
    first, second = line_sums(values)
    means = collapse([first, second, None, None], table) * (1.0 / LOCAL)
    one, two, _, _ = expand(means, table)
    off = values - tile_lines(per_line(one, two), ROWS)
    first, second = line_sums(off * off)
    return means + collapse([None, None, first, second], table)


def pair_sums(scaled, normed, table):
    return collapse(line_sums(scaled) + line_sums(scaled * normed), table)


def sigmoid(v):
    return 0.5 + 0.5 * jnp.tanh(0.5 * v)


def silu_slope(v):
    sig = sigmoid(v)
    return sig * (1.0 + v * (1.0 - sig))


def spread_taps(ref, values):
    count = values.shape[0]
    ref[:, 0:C] = pltpu.roll(values, 1, 0).astype(BF16)
    ref[:, C : 2 * C] = values.astype(BF16)
    ref[:, 2 * C : 3 * C] = pltpu.roll(values, count - 1, 0).astype(BF16)


def conv_lines(ref, weights_ref, count):
    total = dot(ref[0 : count * LINE, :], weights_ref[0])
    for ky in range(1, 3):
        total = total + dot(ref[ky * LINE : (ky + count) * LINE, :], weights_ref[ky])
    return total


def turn_taps(ref, weights_ref):
    for ky in range(3):
        for kx in range(3):
            ref[ky, :, kx * C : (kx + 1) * C] = weights_ref[2 - ky, 2 - kx]


def conv_turned(ref, weights_ref, count):
    total = None
    for ky in range(3):
        part = lax.dot_general(
            ref[ky * LINE : (ky + count) * LINE, :],
            weights_ref[ky],
            (((1,), (1,)), ((), ())),
            preferred_element_type=F32,
        )
        total = part if total is None else total + part
    return total


def kernel_grad(mine_ref, theirs_ref, taps_ref, top, grads, order_ref):
    core = lax.axis_index("c")
    left = lax.dot_general(
        order_ref[...], grads.astype(BF16), (((1,), (1,)), ((), ())), preferred_element_type=F32
    ).astype(BF16)
    parts = []
    for ky in range(3):
        lines = taps_ref[(top + ky) * LINE : (top + ky + ROWS) * LINE, :]
        parts.append(dot(left, lines).astype(BF16))
    parts.append(jnp.zeros((C, LANES - TAPS), BF16))
    whole = jnp.concatenate(parts, axis=1)
    low, high = whole[:, : LANES // 2], whole[:, LANES // 2 :]

    @pl.when(core == 0)
    def _():
        mine_ref[...] = low
        theirs_ref[...] = high

    @pl.when(core == 1)
    def _():
        mine_ref[...] = high
        theirs_ref[...] = low


def fetch(sems, index, src, dst):
    copy = pltpu.make_async_copy(src, dst, sems.at[index])
    copy.start()
    return copy


def fetch_all(sems, first, pairs):
    return [fetch(sems, first + i, src, dst) for i, (src, dst) in enumerate(pairs)]


def wait_all(copies):
    for copy in copies:
        copy.wait()


def flat(ref):
    return ref[...].reshape(1, C)


def moments_kernel(x_ref, t_ref, out_ref, near_ref, far_ref):
    half, core = ROWS * COLS, lax.axis_index("c")
    for b in range(2):
        at, to = b * half, b * 6 * COLS
        parts = [
            (x_ref[at + 4 * COLS : at + 8 * COLS, :], x_ref[at : at + 4 * COLS, :], to, 4 * COLS),
            (t_ref[at + 6 * COLS : at + 8 * COLS, :], t_ref[at : at + 2 * COLS, :], to + 4 * COLS, 2 * COLS),
        ]
        for bottom, top, first, count in parts:
            near_ref[first : first + count] = jnp.where(core == 0, bottom, top)
            far_ref[first : first + count] = jnp.where(core == 0, top, bottom)
    table = hot()
    values = [x_ref[b * half : (b + 1) * half, :].astype(F32) for b in range(2)]
    sums = [jnp.sum(v, axis=0, keepdims=True) for v in values]
    means = collapse(sums + [None, None], table) * (1.0 / LOCAL)
    offs = [v - m for v, m in zip(values, expand(means, table))]
    sums = [jnp.sum(v * v, axis=0, keepdims=True) for v in offs]
    out = means + collapse([None, None] + sums, table)
    out_ref[...] = jnp.broadcast_to(out, (DEVICES, 128))


def strip_blocks():
    out, row = [], 0
    for b in range(2):
        low, high = 512 + b * 6 * COLS, 704 + b * 6 * COLS
        for y in range(GH):
            start = low + y * COLS if y < 4 else b * 128 + (y - 4) * COLS if y < 12 else high + (y - 12) * COLS
            out.append((row, RIM, start, y * LINE + b * GW))
            row += RIM
        for y in range(12):
            start = low + (4 + y) * COLS if y < 2 else 256 + b * 128 + (y - 2) * COLS if y < 10 else high + (y - 6) * COLS
            out.append((row, 2, start, (GH + y) * LINE + b * GW))
            row += 2
    return out


def widened(scr, x_ref, t_ref, near_ref, far_ref):
    core = lax.axis_index("c")
    near, far = near_ref[...].astype(F32), far_ref[...].astype(F32)
    scr[0:256] = x_ref[...].astype(F32)
    scr[256:512] = t_ref[...].astype(F32)
    scr[512:704] = jnp.where(core == 0, far, near)
    scr[704:896] = jnp.where(core == 0, near, far)


def pack_kernel(x_ref, t_ref, near_ref, far_ref, right_ref, left_ref, scr, right, left):
    widened(scr, x_ref, t_ref, near_ref, far_ref)
    for row, width, start, _ in strip_blocks():
        left[row : row + width] = scr[start : start + width]
        right[row : row + width] = scr[start + COLS - width : start + COLS]
    even = lax.rem(lax.axis_index("y"), 2) == 0
    right_ref[...] = jnp.where(even, right[...], left[...]).astype(BF16)
    left_ref[...] = jnp.where(even, left[...], right[...]).astype(BF16)


def grid_kernel(x_ref, t_ref, near_ref, far_ref, first_ref, last_ref, f_ref, g_ref, scr, first, last, grid):
    widened(scr, x_ref, t_ref, near_ref, far_ref)
    even = lax.rem(lax.axis_index("y"), 2) == 0
    first[...] = jnp.where(even, first_ref[...].astype(F32), last_ref[...].astype(F32))
    last[...] = jnp.where(even, last_ref[...].astype(F32), first_ref[...].astype(F32))
    empty = jnp.zeros((2, C), F32)
    for row, width, start, at in strip_blocks():
        inner = at + RIM
        grid[inner - width : inner] = first[row : row + width]
        grid[inner : inner + COLS] = scr[start : start + COLS]
        grid[inner + COLS : inner + COLS + width] = last[row : row + width]
        if width == 2:
            grid[at : at + 2] = empty
            grid[at + GW - 2 : at + GW] = empty
    f_ref[...] = grid[0 : GH * LINE].astype(BF16)
    g_ref[...] = grid[GH * LINE : (GH + 12) * LINE].astype(BF16)


def first_kernel(
    stats_hbm, gain_hbm, shift_hbm, bias_hbm, temb_hbm, x_hbm, w_hbm,
    out_hbm, rows_hbm, h_hbm, taps_hbm, scr, w_ref, x_ref, h_ref, out_ref, rows_ref,
    stats_ref, gain_ref, shift_ref, bias_ref, temb_ref, sems,
):
    small = fetch_all(
        sems, 4,
        [
            (stats_hbm, stats_ref), (gain_hbm, gain_ref), (shift_hbm, shift_ref),
            (bias_hbm, bias_ref), (temb_hbm, temb_ref),
        ],
    )
    xs = fetch(sems, 2, x_hbm, x_ref)
    weights = fetch(sems, 0, w_hbm, w_ref)
    table = hot()
    wait_all(small)
    rows = norm_rows(stats_ref, table)
    keep_rows(rows_ref, rows)
    kept = fetch(sems, 9, rows_ref, rows_hbm)
    mean, rstd = norm_lines(rows)
    scale = tile_lines(rstd * flat(gain_ref), GH)
    xs.wait()
    n1 = (x_ref[...].astype(F32) - tile_lines(mean, GH)) * scale + flat(shift_ref)
    spread_taps(scr, masked(n1 * sigmoid(n1), 0, GH))
    taps = fetch(sems, 1, scr.at[3 * LINE : 13 * LINE, :], taps_hbm)
    weights.wait()
    h1 = conv_lines(scr, w_ref, GH - 2) + (flat(bias_ref) + flat(temb_ref))
    h_ref[...] = h1
    hs = fetch(sems, 3, h_ref, h_hbm)
    out_ref[...] = jnp.broadcast_to(moments(h1[3 * LINE : 11 * LINE], table), (DEVICES, 128))
    outs = fetch(sems, 10, out_ref, out_hbm)
    wait_all([taps, hs, kept, outs])


def second_kernel(
    stats_hbm, gain_hbm, shift_hbm, bias_hbm, sign_hbm, h_hbm, w_hbm, wt_hbm, x_hbm, t_hbm, order_hbm,
    out_hbm, err_hbm, rows_hbm, n_hbm, e_hbm, bout_hbm, u_hbm, mine_hbm, theirs_hbm,
    scr_a, scr_u, w_ref, wt_ref, x_ref, t_ref, order_ref, bout_ref, u_ref, mine_ref, theirs_ref, h_ref, e_ref, turn_ref,
    out_ref, err_ref, rows_ref, n_ref, stats_ref, gain_ref, shift_ref, bias_ref, sign_ref, sems,
):
    small = fetch_all(
        sems, 11,
        [
            (stats_hbm, stats_ref), (gain_hbm, gain_ref), (shift_hbm, shift_ref),
            (bias_hbm, bias_ref), (sign_hbm, sign_ref),
        ],
    )
    hs = fetch(sems, 9, h_hbm, h_ref)
    weights = fetch(sems, 0, w_hbm, w_ref)
    xs = fetch(sems, 1, x_hbm.at[2 * LINE : 14 * LINE, :], x_ref)
    ts = fetch(sems, 2, t_hbm, t_ref)
    orders = fetch(sems, 4, order_hbm, order_ref)
    turned = fetch(sems, 3, wt_hbm, wt_ref)
    table = hot()
    wait_all(small)
    rows = norm_rows(stats_ref, table)
    keep_rows(rows_ref, rows)
    mean, rstd = norm_lines(rows)
    hs.wait()
    nhat = (h_ref[...] - tile_lines(mean, GH - 2)) * tile_lines(rstd, GH - 2)
    n_ref[...] = nhat[2 * LINE : 12 * LINE]
    kept = fetch_all(sems, 16, [(rows_ref, rows_hbm), (n_ref, n_hbm)])
    n2 = nhat * flat(gain_ref) + flat(shift_ref)
    spread_taps(scr_a, masked(n2 * sigmoid(n2), 1, GH - 2))
    weights.wait()
    conv = conv_lines(scr_a, w_ref, 12) + flat(bias_ref)
    xs.wait()
    out = x_ref[...].astype(F32) + conv
    bout_ref[...] = out[2 * LINE : 10 * LINE].astype(BF16)
    bouts = fetch(sems, 5, bout_ref, bout_hbm)
    ts.wait()
    diff = out - t_ref[...].astype(F32)
    mid = diff[2 * LINE : 10 * LINE]
    lane = lax.broadcasted_iota(jnp.int32, (1, 128), 1)
    errs = jnp.zeros((1, 128), F32)
    for b, part in enumerate(line_sums(mid * mid)):
        errs = errs + jnp.where(lane == b, jnp.sum(part, axis=1, keepdims=True), 0.0)
    err_ref[...] = errs
    sign = tile_lines(per_line(flat(sign_ref), -flat(sign_ref)), 12)
    u = masked(diff * sign, 2, 12)
    spread_taps(scr_u, u)
    center = u[2 * LINE : 10 * LINE]
    u_ref[...] = center.astype(BF16)
    us = fetch(sems, 6, u_ref, u_hbm)
    one, two = center_line()
    orders.wait()
    kernel_grad(mine_ref, theirs_ref, scr_a, 2, center * tile_lines(one + two, ROWS), order_ref)
    mines = fetch(sems, 7, mine_ref, mine_hbm)
    others = fetch(sems, 8, theirs_ref, theirs_hbm)
    turned.wait()
    turn_taps(turn_ref, wt_ref)
    da2 = conv_turned(scr_u, turn_ref, 10)
    e = da2 * silu_slope(n2[2 * LINE : 12 * LINE]) * flat(gain_ref)
    e_ref[...] = e
    es = fetch(sems, 10, e_ref, e_hbm)
    sums = pair_sums(e[LINE : 9 * LINE], nhat[3 * LINE : 11 * LINE], table)
    out_ref[...] = jnp.broadcast_to(sums, (DEVICES, 128))
    outs = fetch_all(sems, 18, [(out_ref, out_hbm), (err_ref, err_hbm)])
    wait_all([bouts, us, mines, others, es] + kept + outs)


def back_line(sums_ref, table):
    sums = jnp.sum(sums_ref[...], axis=0, keepdims=True) * (1.0 / TOTAL)
    one, two, three, four = expand(sums, table)
    return per_line(one, two), per_line(three, four)


def third_kernel(
    second_hbm, sums_hbm, first_hbm, gain_hbm, shift_hbm, errs_hbm, e_hbm, n_hbm, taps_hbm, order_hbm, x_hbm, wt_hbm,
    out_hbm, mine_hbm, theirs_hbm, back_hbm,
    out_ref, second_ref, sums_ref, first_ref, gain_ref, shift_ref, errs_ref, e_ref, n_ref, taps_ref, order_ref, x_ref, wt_ref,
    mine_ref, theirs_ref, back_ref, turn_ref, scr, sems,
):
    small = fetch_all(sems, 0, [(second_hbm, second_ref), (sums_hbm, sums_ref)])
    main = fetch_all(sems, 2, [(n_hbm, n_ref), (e_hbm, e_ref)])
    grads = fetch_all(sems, 4, [(order_hbm, order_ref), (taps_hbm, taps_ref)])
    rest = fetch_all(
        sems, 6,
        [
            (first_hbm, first_ref), (gain_hbm, gain_ref), (shift_hbm, shift_ref), (errs_hbm, errs_ref),
            (x_hbm.at[4 * LINE : 12 * LINE, :], x_ref), (wt_hbm, wt_ref),
        ],
    )
    table = hot()
    wait_all(small)
    first, second = back_line(sums_ref, table)
    scale = tile_lines(norm_lines(kept_rows(second_ref))[1], 10)
    wait_all(main)
    dh = scale * (e_ref[...] - tile_lines(first, 10) - n_ref[...] * tile_lines(second, 10))
    dh = masked(dh, 3, 10)
    spread_taps(scr, dh)
    one, two = center_line()
    wait_all(grads)
    kernel_grad(mine_ref, theirs_ref, taps_ref, 0, dh[LINE : 9 * LINE] * tile_lines(one + two, ROWS), order_ref)
    outs = fetch_all(sems, 12, [(theirs_ref, theirs_hbm), (mine_ref, mine_hbm)])
    wait_all(rest)
    mean, rstd = norm_lines(kept_rows(first_ref))
    nhat = (x_ref[...].astype(F32) - tile_lines(mean, ROWS)) * tile_lines(rstd, ROWS)
    n1 = nhat * flat(gain_ref) + flat(shift_ref)
    turn_taps(turn_ref, wt_ref)
    e1 = conv_turned(scr, turn_ref, ROWS) * (silu_slope(n1) * flat(gain_ref))
    back_ref[...] = e1
    outs = outs + [fetch(sems, 14, back_ref, back_hbm)]
    out_ref[0:1] = pair_sums(e1, nhat, table)
    out_ref[1:2] = errs_ref[...]
    wait_all(outs + [fetch(sems, 15, out_ref, out_hbm)])


def last_kernel(sums_ref, info_ref, norm_ref, e_ref, x_ref, u_ref, out_ref, scr):
    weight = info_ref[0:1, 0:1]
    table = hot()
    mean, rstd = norm_lines(kept_rows(norm_ref))
    first, second = back_line(sums_ref, table)
    scale = tile_lines(rstd, ROWS)
    nhat = (x_ref[4 * LINE : 12 * LINE, :].astype(F32) - tile_lines(mean, ROWS)) * scale
    dx = scale * (e_ref[...] - tile_lines(first, ROWS) - nhat * tile_lines(second, ROWS))
    scr[...] = (u_ref[...].astype(F32) + dx) * weight
    centered(out_ref, scr)


def piece_rows(count, at, sums, errs):
    index = lax.broadcasted_iota(jnp.int32, (count, 128), 0)
    out = jnp.zeros((count, 128), F32)
    for i, piece in enumerate(pieces(sums) + pieces(errs)):
        out = out + jnp.where(index == at + i, piece, 0.0)
    return out


def centered(out_ref, scr):
    for b in range(2):
        for y in range(ROWS):
            at = y * LINE + b * GW + RIM
            out_ref[(b * ROWS + y) * COLS : (b * ROWS + y + 1) * COLS] = scr[at : at + COLS].astype(BF16)


def early_kernel(mine_ref, got_ref, lines_ref, block_ref, *outs):
    outs, scr = outs[:4], outs[4]
    scr[...] = lines_ref[...].astype(F32)
    centered(block_ref, scr)
    y = lax.axis_index("y")
    for k, out_ref in enumerate(outs):
        rows = pl.ds(pl.multiple_of(lax.rem(y + k, 4) * 80, 16), 80)
        out_ref[...] = (mine_ref[rows, :].astype(F32) + got_ref[rows, :].astype(F32)).astype(BF16)


def late_kernel(mine_ref, got_ref, part_ref, other_ref, a_ref, b_ref, c_ref, d_ref, out_ref, *outs):
    for j in range(4):
        for i in range(4):
            for k in range(3):
                rows = slice(j * 80, (j + 1) * 80)
                lanes = slice(i * 384 + k * 128, i * 384 + (k + 1) * 128)
                both = mine_ref[rows, lanes].astype(F32) + got_ref[rows, lanes].astype(F32)
                out_ref[j * 4 + i, k * 80 : (k + 1) * 80, :] = both.astype(BF16)
    tails = part_ref[...] + other_ref[...]
    rows = piece_rows(16, 0, tails[0:1], tails[1:2]).astype(BF16)
    for i in range(16):
        out_ref[i, 240:256, :] = rows
    outs, scr = outs[:4], outs[4]
    scr[...] = (
        (a_ref[...].astype(F32) + b_ref[...].astype(F32)) + (c_ref[...].astype(F32) + d_ref[...].astype(F32))
    )
    x = lax.axis_index("x")
    for i, out_ref in enumerate(outs):
        for k in range(3):
            lanes = pl.ds(pl.multiple_of(lax.rem(x + i, 4) * 384 + k * 128, 128), 128)
            out_ref[k * 80 : (k + 1) * 80] = scr[:, lanes].astype(BF16)


def plane_kernel(in_ref, a_ref, b_ref, c_ref, d_ref, move_ref, out_ref):
    total = in_ref[0].astype(F32)
    for i in range(1, 16):
        total = total + in_ref[i].astype(F32)
    tail = total[240:256]
    sums = tail[0:1] + tail[1:2] + tail[2:3]
    errs = tail[3:4] + tail[4:5] + tail[5:6]
    rows = piece_rows(80, 60, sums, errs)
    other = (a_ref[...].astype(F32) + b_ref[...].astype(F32)) + (c_ref[...].astype(F32) + d_ref[...].astype(F32))
    both = jnp.concatenate([other, total[0:240]], axis=0).astype(BF16)
    moved = dot(move_ref[...], both)
    for z in range(8):
        out_ref[z] = (moved[z * 80 : (z + 1) * 80] + rows).astype(BF16)


def depth_kernel(in_ref, sign_ref, ref_ref, out_ref, sums_ref, info_ref, loss_ref):
    total = in_ref[0].astype(F32)
    for i in range(1, 8):
        total = total + in_ref[i].astype(F32)
    sums_ref[...] = total[60:61] + total[61:62] + total[62:63]
    errs = total[63:64] + total[64:65] + total[65:66]
    excess = errs[:, 0:2] * (1.0 / (BAND_ROWS * BAND_COLS * C)) - ref_ref[...]
    gap = 0.5 * flat(sign_ref)[:, 0:1] * (excess[:, 0:1] - excess[:, 1:2])
    weight = 1.0 / (1.0 + jnp.exp(-gap))
    loss = jnp.maximum(gap, 0.0) + jnp.log1p(jnp.exp(-jnp.abs(gap)))
    info_ref[...] = jnp.broadcast_to(weight, (1, 128))
    loss_ref[...] = loss
    grads = (total[0:64] * (weight * (2 * BAND_ROWS * BAND_COLS) ** -0.5)).astype(BF16)
    for i in range(8):
        out_ref[i] = grads


VM = pl.BlockSpec(memory_space=pltpu.VMEM)
HB = pl.BlockSpec(memory_space=pltpu.HBM)
DMA = pltpu.SemaphoreType.DMA


def call(kernel, outs, ins, scratch=(), flops=0):
    size = sum(int(np.prod(s.shape)) * s.dtype.itemsize for _, s in outs)
    size += sum(a.size * a.dtype.itemsize for _, a in ins)
    many = len(outs) > 1
    shapes, spaces = [s for _, s in outs], [p for p, _ in outs]
    return pl.pallas_call(
        kernel,
        out_shape=tuple(shapes) if many else shapes[0],
        in_specs=[p for p, _ in ins],
        out_specs=tuple(spaces) if many else spaces[0],
        scratch_shapes=list(scratch),
        compiler_params=pltpu.CompilerParams(vmem_limit_bytes=VMEM_LIMIT),
        cost_estimate=pl.CostEstimate(flops=flops, bytes_accessed=size, transcendentals=0),
    )(*[a for _, a in ins])


def sds(shape, dtype=F32):
    return jax.ShapeDtypeStruct(shape, dtype)


AXES = ("x", "c", "z", "y")


def share(rows):
    return lax.all_to_all(rows, AXES, 0, 0, tiled=True)


def widen(features, target, near, far, part):
    strip, wide = sds((176, C), BF16), pltpu.VMEM((896, C), F32)
    edge = pltpu.VMEM((176, C), F32)
    ins = [(VM, features), (VM, target), (VM, near), (VM, far)]
    right, left = call(pack_kernel, [(VM, strip), (VM, strip)], ins, [wide, edge, edge])
    right, left, part = lax.optimization_barrier((right, left, part))
    inner = [(i, i ^ 1) for i in range(32)]
    outer = [(i, ((i - 1) ^ 1) + 1) for i in range(1, 31)]
    first = lax.ppermute(left, ("z", "y"), outer)
    last = lax.ppermute(right, ("z", "y"), inner)
    f, t = call(
        grid_kernel,
        [(VM, sds((GH * LINE, C), BF16)), (VM, sds((12 * LINE, C), BF16))],
        ins + [(VM, first), (VM, last)],
        [wide, edge, edge, pltpu.VMEM(((GH + 12) * LINE, C), F32)],
        10**10,
    )
    return f, t, part


def time_embed(timestep, time_weight, time_bias):
    half = TEMB // 2
    freqs = jnp.exp(-jnp.log(10000.0) * jnp.arange(half, dtype=F32) / half)
    angles = timestep.astype(F32)[:, None] * freqs[None, :]
    emb = jnp.concatenate([jnp.cos(angles), jnp.sin(angles)], axis=1)
    return jnp.dot(jax.nn.silu(emb), time_weight.astype(F32), precision=HIGH) + time_bias


def order_matrix():
    out = np.zeros((C, C), np.float32)
    for z in range(8):
        for y in range(4):
            for j in range(10):
                out[y * 80 + z * 10 + j, z * 40 + y * 10 + j] = 1.0
    return jnp.asarray(out, BF16)


def move_matrix():
    out = np.zeros((640, 480), np.float32)
    for grad in range(2):
        for k in range(3):
            for z in range(8):
                for j in range(10):
                    out[z * 80 + grad * 30 + k * 10 + j, grad * 240 + k * 80 + z * 10 + j] = 1.0
    return jnp.asarray(out, BF16)


def shift(block, axis, by):
    return lax.ppermute(block, axis, [(i, (i + by) % 4) for i in range(4)])


def swap(theirs):
    return lax.ppermute(theirs, "c", [(0, 1), (1, 0)])


def body(
    features, target, norm1_gain, norm1_shift, kernel1, bias1, time_weight, time_bias,
    norm2_gain, norm2_shift, kernel2, bias2, ref_error, preference, timestep,
):
    sign = jnp.broadcast_to(jnp.where(preference == 0, 2.0, -2.0).astype(F32), (C,))
    strip, cells = sds((2 * 6 * COLS, C), BF16), 2 * ROWS * COLS
    part, near, far = call(
        moments_kernel,
        [(VM, sds((DEVICES, 128))), (VM, strip), (VM, strip)],
        [(VM, features.reshape(cells, C)), (VM, target.reshape(cells, C))],
    )
    far = lax.ppermute(far, ("x", "c"), [(1, 2), (2, 1), (3, 4), (4, 3), (5, 6), (6, 5)])
    near = swap(near)
    fx, tx, part = widen(features.reshape(cells, C), target.reshape(cells, C), near, far, part)
    stats1 = share(part)
    temb = time_embed(timestep, time_weight, time_bias).reshape(C)
    order, move = order_matrix(), move_matrix()
    w1, w2 = kernel1.reshape(3, 3 * C, C), kernel2.reshape(3, 3 * C, C)
    conv_flops = 2 * 9 * C * C * LINE
    half = sds((C, LANES // 2), BF16)
    row, table, lines = sds((1, 128)), sds((DEVICES, 128)), sds((ROWS * LINE, C), BF16)
    full = sds((3, 3, C, C), BF16)
    rows4, tbl = sds((4, C)), pltpu.VMEM((DEVICES, 128), F32)
    part, norm1, h1, taps1 = call(
        first_kernel,
        [(HB, table), (HB, rows4), (HB, sds((14 * LINE, C))), (HB, sds((10 * LINE, 3 * C), BF16))],
        [(HB, v) for v in (stats1, norm1_gain, norm1_shift, bias1, temb, fx, w1)],
        [
            pltpu.VMEM((GH * LINE, 3 * C), BF16), pltpu.VMEM((3, 3 * C, C), BF16),
            pltpu.VMEM((GH * LINE, C), BF16), pltpu.VMEM((14 * LINE, C), F32), tbl, pltpu.VMEM((4, C), F32),
            tbl, *[pltpu.VMEM((C,), F32)] * 4, DMA((11,)),
        ],
        14 * conv_flops,
    )
    stats2 = share(part)
    part, errs, norm2, nhat2, e2, bout, u, mine2, theirs2 = call(
        second_kernel,
        [
            (HB, table), (HB, row), (HB, rows4), (HB, sds((10 * LINE, C))), (HB, sds((10 * LINE, C))), (HB, lines), (HB, lines), (HB, half), (HB, half),
        ],
        [
            (HB, v)
            for v in (stats2, norm2_gain, norm2_shift, bias2, sign, h1, w2, kernel2, fx, tx, order)
        ],
        [
            pltpu.VMEM((14 * LINE, 3 * C), BF16), pltpu.VMEM((12 * LINE, 3 * C), BF16),
            pltpu.VMEM((3, 3 * C, C), BF16), pltpu.VMEM(full.shape, BF16),
            pltpu.VMEM((12 * LINE, C), BF16), pltpu.VMEM((12 * LINE, C), BF16), pltpu.VMEM((C, C), BF16),
            pltpu.VMEM((ROWS * LINE, C), BF16), pltpu.VMEM((ROWS * LINE, C), BF16),
            pltpu.VMEM((C, LANES // 2), BF16), pltpu.VMEM((C, LANES // 2), BF16),
            pltpu.VMEM((14 * LINE, C), F32), pltpu.VMEM((10 * LINE, C), F32), pltpu.VMEM((3, C, 3 * C), BF16),
            tbl, pltpu.VMEM((1, 128), F32), pltpu.VMEM((4, C), F32), pltpu.VMEM((10 * LINE, C), F32),
            tbl, *[pltpu.VMEM((C,), F32)] * 4, DMA((20,)),
        ],
        30 * conv_flops,
    )
    sums2 = share(part)
    got2 = swap(theirs2)
    block_out, *strips = call(
        early_kernel,
        [(VM, sds((cells, C), BF16))] + [(VM, sds((80, LANES // 2), BF16))] * 4,
        [(VM, mine2), (VM, got2), (VM, bout)],
        [pltpu.VMEM((ROWS * LINE, C), F32)],
    )
    block_out = block_out.reshape(2, ROWS, COLS, C)
    strips = [strips[0]] + [shift(strips[k], "y", k) for k in (2, 1, 3)]
    sums2, strips[0] = lax.optimization_barrier((sums2, strips[0]))
    part, mine1, theirs1, e1 = call(
        third_kernel,
        [(HB, sds((2, 128))), (HB, half), (HB, half), (HB, sds((ROWS * LINE, C)))],
        [
            (HB, v)
            for v in (
                norm2, sums2, norm1, norm1_gain, norm1_shift, errs, e2, nhat2, taps1, order, fx, kernel1,
            )
        ],
        [
            pltpu.VMEM((2, 128), F32), pltpu.VMEM((4, C), F32), tbl, pltpu.VMEM((4, C), F32),
            *[pltpu.VMEM((C,), F32)] * 2, pltpu.VMEM((1, 128), F32),
            pltpu.VMEM((10 * LINE, C), F32), pltpu.VMEM((10 * LINE, C), F32),
            pltpu.VMEM((10 * LINE, 3 * C), BF16), pltpu.VMEM((C, C), BF16),
            pltpu.VMEM((ROWS * LINE, C), BF16), pltpu.VMEM(full.shape, BF16),
            pltpu.VMEM(half.shape, BF16), pltpu.VMEM(half.shape, BF16), pltpu.VMEM((ROWS * LINE, C), F32),
            pltpu.VMEM((3, C, 3 * C), BF16),
            pltpu.VMEM((10 * LINE, 3 * C), BF16), DMA((16,)),
        ],
        16 * conv_flops,
    )
    theirs1, *strips = lax.optimization_barrier((theirs1, *strips))
    got1, other = swap(theirs1), swap(part)
    plane, *parts = call(
        late_kernel,
        [(VM, sds((16, 256, 128), BF16))] + [(VM, sds((240, 128), BF16))] * 4,
        [(VM, mine1), (VM, got1), (VM, part), (VM, other)] + [(VM, v) for v in strips],
        [pltpu.VMEM((80, LANES // 2), F32)],
    )
    plane = lax.all_to_all(plane, ("y", "x"), 0, 0, tiled=True)
    parts = [parts[0]] + [shift(parts[k], "x", k) for k in range(1, 4)]
    depth = call(
        plane_kernel,
        [(VM, sds((8, 80, 128), BF16))],
        [(VM, plane)] + [(VM, v) for v in parts] + [(VM, move)],
    )
    depth = lax.all_to_all(depth, ("z",), 0, 0, tiled=True)
    copies, sums1, info, loss = call(
        depth_kernel,
        [(VM, sds((8, 64, 128), BF16)), (VM, row), (VM, row), (VM, sds((1, 1)))],
        [(VM, depth), (VM, sign), (VM, ref_error)],
    )
    whole = lax.all_to_all(copies, ("c", "x"), 0, 0, tiled=True)
    grad = call(
        last_kernel,
        [(VM, sds((cells, C), BF16))],
        [(VM, sums1), (VM, info), (VM, norm1), (VM, e1), (VM, fx), (VM, u)],
        [pltpu.VMEM((ROWS * LINE, C), F32)],
    )
    feature_grad = grad.reshape(2, ROWS, COLS, C)
    whole = whole[:, :60].reshape(2, 4, 2, 3, 10, 128).transpose(2, 0, 1, 3, 5, 4).reshape(2, LANES, 10)
    whole = whole[:, :TAPS].astype(F32).reshape(2, 3, 3, C, 10)
    loss = loss.reshape(())
    return (block_out, feature_grad, whole[1], whole[0], loss)


def solution(mesh):
    fine = Mesh(mesh.devices.reshape(4, 2, 8, 4), AXES)
    cells = P(None, ("x", "c"), ("z", "y"), None)
    kernels = P(None, None, None, ("z", "y"))
    return jax.shard_map(
        body,
        mesh=fine,
        in_specs=(cells, cells) + (P(),) * 13,
        out_specs=(cells, cells, kernels, kernels, P()),
        check_vma=False,
    )
```

```python
import functools

import jax
import jax.numpy as jnp
import numpy as np
from jax import lax
from jax.experimental import pallas as pl
from jax.experimental.pallas import tpu as pltpu
from jax.sharding import Mesh
from jax.sharding import PartitionSpec as P

GROUPS = 32
TEMB = 1280
C = 320
WIDTH = C // GROUPS
ROWS, COLS = 8, 16
BAND_ROWS, BAND_COLS = 64, 512
RIM = 4
GH, GW = ROWS + 2 * RIM, COLS + 2 * RIM
LINE = 2 * GW
DEVICES = 256
LOCAL = ROWS * COLS * WIDTH
TOTAL = LOCAL * DEVICES
TAPS = 9 * C
LANES = 3072
EPS = 1e-05
F32, BF16 = jnp.float32, jnp.bfloat16
HIGH = lax.Precision.HIGHEST
VMEM_LIMIT = 63 * 2**20


def dot(a, b):
    return jnp.dot(a, b, preferred_element_type=F32)


def pieces(row):
    high = row.astype(BF16).astype(F32)
    rest = row - high
    mid = rest.astype(BF16).astype(F32)
    return high, mid, rest - mid


def hot():
    blocks = []
    for slot in range(4):
        low = (lax.broadcasted_iota(jnp.int32, (128, 384), 0) - slot * GROUPS) * WIDTH
        chan = lax.broadcasted_iota(jnp.int32, (128, 384), 1)
        blocks.append(((chan >= low) & (chan < low + WIDTH) & (chan < C)).astype(F32).astype(BF16))
    return jnp.concatenate(blocks, axis=1)


def stacked(row):
    index = lax.broadcasted_iota(jnp.int32, (16, row.shape[1]), 0)
    out = jnp.zeros((16, row.shape[1]), F32)
    for i, piece in enumerate(pieces(row)):
        out = jnp.where(index == i, piece, out)
    return out.astype(BF16)


def expand(row, table):
    wide = jnp.sum(dot(stacked(row), table), axis=0, keepdims=True)
    return [wide[:, i * 384 : i * 384 + C] for i in range(4)]


def collapse(rows, table):
    gap, empty = jnp.zeros((1, 384 - C), F32), jnp.zeros((1, C), F32)
    wide = jnp.concatenate([v for row in rows for v in (empty if row is None else row, gap)], axis=1)
    small = lax.dot_general(stacked(wide), table, (((1,), (1,)), ((), ())), preferred_element_type=F32)
    return jnp.sum(small, axis=0, keepdims=True)


def per_line(first, second):
    return jnp.concatenate(
        [jnp.broadcast_to(first, (GW, C)), jnp.broadcast_to(second, (GW, C))], axis=0
    )


def tile_lines(line, count):
    return jnp.broadcast_to(line[None], (count, LINE, C)).reshape(count * LINE, C)


def masked(values, top, count):
    high = lax.axis_index("x") * 2 + lax.axis_index("c")
    wide = lax.axis_index("z") * 4 + lax.axis_index("y")
    col = lax.broadcasted_iota(jnp.int32, (LINE, C), 0)
    gx = jnp.where(col >= GW, col - GW, col) + (wide * COLS - RIM)
    line = ((gx >= 0) & (gx < BAND_COLS)).astype(F32)
    upper = line * jnp.where(high > 0, 1.0, 0.0)
    lower = line * jnp.where(high < BAND_ROWS // ROWS - 1, 1.0, 0.0)
    parts = [(upper, RIM - top), (line, ROWS), (lower, top + count - RIM - ROWS)]
    mask = jnp.concatenate([jnp.broadcast_to(v[None], (n, LINE, C)) for v, n in parts], axis=0)
    return values * mask.reshape(count * LINE, C)


def center_line():
    col = lax.broadcasted_iota(jnp.int32, (LINE, C), 0)
    one = (col >= RIM) & (col < RIM + COLS)
    two = (col >= GW + RIM) & (col < GW + RIM + COLS)
    return one.astype(F32), two.astype(F32)


def line_sums(values):
    total = jnp.sum(values.reshape(ROWS, LINE, C), axis=0)
    return [jnp.sum(total * line, axis=0, keepdims=True) for line in center_line()]


def norm_rows(stats_ref, table):
    stats = stats_ref[...]
    sums = jnp.sum(stats, axis=0, keepdims=True)
    mean = sums * (1.0 / DEVICES)
    off = stats - mean
    spread = jnp.sum(off * off, axis=0, keepdims=True) * LOCAL
    var = (sums + pltpu.roll(spread, 64, 1)) * (1.0 / TOTAL)
    lane = lax.broadcasted_iota(jnp.int32, (1, 128), 1)
    row = jnp.where(lane < 64, mean, 1.0 / jnp.sqrt(jnp.maximum(var, 0.0) + EPS))
    return expand(row, table)


def norm_lines(rows):
    return per_line(rows[0], rows[1]), per_line(rows[2], rows[3])


def kept_rows(ref):
    return [ref[i : i + 1, :] for i in range(4)]


def keep_rows(ref, rows):
    for i, row in enumerate(rows):
        ref[i : i + 1, :] = row


def moments(values, table):
    first, second = line_sums(values)
    means = collapse([first, second, None, None], table) * (1.0 / LOCAL)
    one, two, _, _ = expand(means, table)
    off = values - tile_lines(per_line(one, two), ROWS)
    first, second = line_sums(off * off)
    return means + collapse([None, None, first, second], table)


def pair_sums(scaled, normed, table):
    return collapse(line_sums(scaled) + line_sums(scaled * normed), table)


def sigmoid(v):
    return 0.5 + 0.5 * jnp.tanh(0.5 * v)


def silu_slope(v):
    sig = sigmoid(v)
    return sig * (1.0 + v * (1.0 - sig))


def spread_taps(ref, values):
    count = values.shape[0]
    ref[:, 0:C] = pltpu.roll(values, 1, 0).astype(BF16)
    ref[:, C : 2 * C] = values.astype(BF16)
    ref[:, 2 * C : 3 * C] = pltpu.roll(values, count - 1, 0).astype(BF16)


def conv_lines(ref, weights_ref, count):
    total = dot(ref[0 : count * LINE, :], weights_ref[0])
    for ky in range(1, 3):
        total = total + dot(ref[ky * LINE : (ky + count) * LINE, :], weights_ref[ky])
    return total


def turn_taps(ref, weights_ref):
    for ky in range(3):
        for kx in range(3):
            ref[ky, :, kx * C : (kx + 1) * C] = weights_ref[2 - ky, 2 - kx]


def conv_turned(ref, weights_ref, count):
    total = None
    for ky in range(3):
        part = lax.dot_general(
            ref[ky * LINE : (ky + count) * LINE, :],
            weights_ref[ky],
            (((1,), (1,)), ((), ())),
            preferred_element_type=F32,
        )
        total = part if total is None else total + part
    return total


def kernel_grad(mine_ref, theirs_ref, taps_ref, top, grads, order_ref):
    core = lax.axis_index("c")
    left = lax.dot_general(
        order_ref[...], grads.astype(BF16), (((1,), (1,)), ((), ())), preferred_element_type=F32
    ).astype(BF16)
    parts = []
    for ky in range(3):
        lines = taps_ref[(top + ky) * LINE : (top + ky + ROWS) * LINE, :]
        parts.append(dot(left, lines).astype(BF16))
    parts.append(jnp.zeros((C, LANES - TAPS), BF16))
    whole = jnp.concatenate(parts, axis=1)
    low, high = whole[:, : LANES // 2], whole[:, LANES // 2 :]

    @pl.when(core == 0)
    def _():
        mine_ref[...] = low
        theirs_ref[...] = high

    @pl.when(core == 1)
    def _():
        mine_ref[...] = high
        theirs_ref[...] = low


def fetch(sems, index, src, dst):
    copy = pltpu.make_async_copy(src, dst, sems.at[index])
    copy.start()
    return copy


def fetch_all(sems, first, pairs):
    return [fetch(sems, first + i, src, dst) for i, (src, dst) in enumerate(pairs)]


def wait_all(copies):
    for copy in copies:
        copy.wait()


def flat(ref):
    return ref[...].reshape(1, C)


def moments_kernel(x_ref, t_ref, out_ref, near_ref, far_ref):
    half, core = ROWS * COLS, lax.axis_index("c")
    for b in range(2):
        at, to = b * half, b * 6 * COLS
        parts = [
            (x_ref[at + 4 * COLS : at + 8 * COLS, :], x_ref[at : at + 4 * COLS, :], to, 4 * COLS),
            (t_ref[at + 6 * COLS : at + 8 * COLS, :], t_ref[at : at + 2 * COLS, :], to + 4 * COLS, 2 * COLS),
        ]
        for bottom, top, first, count in parts:
            near_ref[first : first + count] = jnp.where(core == 0, bottom, top)
            far_ref[first : first + count] = jnp.where(core == 0, top, bottom)
    table = hot()
    values = [x_ref[b * half : (b + 1) * half, :].astype(F32) for b in range(2)]
    sums = [jnp.sum(v, axis=0, keepdims=True) for v in values]
    means = collapse(sums + [None, None], table) * (1.0 / LOCAL)
    offs = [v - m for v, m in zip(values, expand(means, table))]
    sums = [jnp.sum(v * v, axis=0, keepdims=True) for v in offs]
    out = means + collapse([None, None] + sums, table)
    out_ref[...] = jnp.broadcast_to(out, (DEVICES, 128))


def strip_blocks():
    out, row = [], 0
    for b in range(2):
        low, high = 512 + b * 6 * COLS, 704 + b * 6 * COLS
        for y in range(GH):
            start = low + y * COLS if y < 4 else b * 128 + (y - 4) * COLS if y < 12 else high + (y - 12) * COLS
            out.append((row, RIM, start, y * LINE + b * GW))
            row += RIM
        for y in range(12):
            start = low + (4 + y) * COLS if y < 2 else 256 + b * 128 + (y - 2) * COLS if y < 10 else high + (y - 6) * COLS
            out.append((row, 2, start, (GH + y) * LINE + b * GW))
            row += 2
    return out


def widened(scr, x_ref, t_ref, near_ref, far_ref):
    core = lax.axis_index("c")
    near, far = near_ref[...].astype(F32), far_ref[...].astype(F32)
    scr[0:256] = x_ref[...].astype(F32)
    scr[256:512] = t_ref[...].astype(F32)
    scr[512:704] = jnp.where(core == 0, far, near)
    scr[704:896] = jnp.where(core == 0, near, far)


def pack_kernel(x_ref, t_ref, near_ref, far_ref, right_ref, left_ref, scr, right, left):
    widened(scr, x_ref, t_ref, near_ref, far_ref)
    for row, width, start, _ in strip_blocks():
        left[row : row + width] = scr[start : start + width]
        right[row : row + width] = scr[start + COLS - width : start + COLS]
    even = lax.rem(lax.axis_index("y"), 2) == 0
    right_ref[...] = jnp.where(even, right[...], left[...]).astype(BF16)
    left_ref[...] = jnp.where(even, left[...], right[...]).astype(BF16)


def grid_kernel(x_ref, t_ref, near_ref, far_ref, first_ref, last_ref, f_ref, g_ref, scr, first, last, grid):
    widened(scr, x_ref, t_ref, near_ref, far_ref)
    even = lax.rem(lax.axis_index("y"), 2) == 0
    first[...] = jnp.where(even, first_ref[...].astype(F32), last_ref[...].astype(F32))
    last[...] = jnp.where(even, last_ref[...].astype(F32), first_ref[...].astype(F32))
    empty = jnp.zeros((2, C), F32)
    for row, width, start, at in strip_blocks():
        inner = at + RIM
        grid[inner - width : inner] = first[row : row + width]
        grid[inner : inner + COLS] = scr[start : start + COLS]
        grid[inner + COLS : inner + COLS + width] = last[row : row + width]
        if width == 2:
            grid[at : at + 2] = empty
            grid[at + GW - 2 : at + GW] = empty
    f_ref[...] = grid[0 : GH * LINE].astype(BF16)
    g_ref[...] = grid[GH * LINE : (GH + 12) * LINE].astype(BF16)


def first_kernel(
    stats_hbm, gain_hbm, shift_hbm, bias_hbm, temb_hbm, time_hbm, x_hbm, w_hbm,
    out_hbm, rows_hbm, h_hbm, taps_hbm, scr, w_ref, x_ref, h_ref, out_ref, rows_ref,
    stats_ref, gain_ref, shift_ref, bias_ref, temb_ref, time_ref, sems,
):
    small = fetch_all(
        sems, 4,
        [
            (stats_hbm, stats_ref), (gain_hbm, gain_ref), (shift_hbm, shift_ref),
            (bias_hbm, bias_ref), (temb_hbm, temb_ref), (time_hbm, time_ref),
        ],
    )
    xs = fetch(sems, 2, x_hbm, x_ref)
    weights = fetch(sems, 0, w_hbm, w_ref)
    table = hot()
    wait_all(small)
    rows = norm_rows(stats_ref, table)
    keep_rows(rows_ref, rows)
    kept = fetch(sems, 11, rows_ref, rows_hbm)
    mean, rstd = norm_lines(rows)
    scale = tile_lines(rstd * flat(gain_ref), GH)
    xs.wait()
    n1 = (x_ref[...].astype(F32) - tile_lines(mean, GH)) * scale + flat(shift_ref)
    spread_taps(scr, masked(n1 * sigmoid(n1), 0, GH))
    taps = fetch(sems, 1, scr.at[3 * LINE : 13 * LINE, :], taps_hbm)
    weights.wait()
    h1 = conv_lines(scr, w_ref, GH - 2) + (flat(bias_ref) + (flat(temb_ref) + flat(time_ref)))
    h_ref[...] = h1
    hs = fetch(sems, 3, h_ref, h_hbm)
    out_ref[...] = jnp.broadcast_to(moments(h1[3 * LINE : 11 * LINE], table), (DEVICES, 128))
    outs = fetch(sems, 10, out_ref, out_hbm)
    wait_all([taps, hs, kept, outs])


def second_kernel(
    stats_hbm, gain_hbm, shift_hbm, bias_hbm, sign_hbm, h_hbm, w_hbm, wt_hbm, x_hbm, t_hbm, order_hbm,
    out_hbm, err_hbm, rows_hbm, n_hbm, e_hbm, bout_hbm, u_hbm, mine_hbm, theirs_hbm,
    scr_a, scr_u, w_ref, wt_ref, x_ref, t_ref, order_ref, bout_ref, u_ref, mine_ref, theirs_ref, h_ref, e_ref, turn_ref,
    out_ref, err_ref, rows_ref, n_ref, stats_ref, gain_ref, shift_ref, bias_ref, sign_ref, sems,
):
    small = fetch_all(
        sems, 11,
        [
            (stats_hbm, stats_ref), (gain_hbm, gain_ref), (shift_hbm, shift_ref),
            (bias_hbm, bias_ref), (sign_hbm, sign_ref),
        ],
    )
    hs = fetch(sems, 9, h_hbm, h_ref)
    weights = fetch(sems, 0, w_hbm, w_ref)
    xs = fetch(sems, 1, x_hbm.at[2 * LINE : 14 * LINE, :], x_ref)
    ts = fetch(sems, 2, t_hbm, t_ref)
    orders = fetch(sems, 4, order_hbm, order_ref)
    turned = fetch(sems, 3, wt_hbm, wt_ref)
    table = hot()
    wait_all(small)
    rows = norm_rows(stats_ref, table)
    keep_rows(rows_ref, rows)
    mean, rstd = norm_lines(rows)
    hs.wait()
    nhat = (h_ref[...] - tile_lines(mean, GH - 2)) * tile_lines(rstd, GH - 2)
    n_ref[...] = nhat[2 * LINE : 12 * LINE]
    kept = fetch_all(sems, 16, [(rows_ref, rows_hbm), (n_ref, n_hbm)])
    n2 = nhat * flat(gain_ref) + flat(shift_ref)
    spread_taps(scr_a, masked(n2 * sigmoid(n2), 1, GH - 2))
    weights.wait()
    conv = conv_lines(scr_a, w_ref, 12) + flat(bias_ref)
    xs.wait()
    out = x_ref[...].astype(F32) + conv
    bout_ref[...] = out[2 * LINE : 10 * LINE].astype(BF16)
    bouts = fetch(sems, 5, bout_ref, bout_hbm)
    ts.wait()
    diff = out - t_ref[...].astype(F32)
    mid = diff[2 * LINE : 10 * LINE]
    lane = lax.broadcasted_iota(jnp.int32, (1, 128), 1)
    errs = jnp.zeros((1, 128), F32)
    for b, part in enumerate(line_sums(mid * mid)):
        errs = errs + jnp.where(lane == b, jnp.sum(part, axis=1, keepdims=True), 0.0)
    err_ref[...] = errs
    sign = tile_lines(per_line(flat(sign_ref), -flat(sign_ref)), 12)
    u = masked(diff * sign, 2, 12)
    spread_taps(scr_u, u)
    center = u[2 * LINE : 10 * LINE]
    u_ref[...] = center.astype(BF16)
    us = fetch(sems, 6, u_ref, u_hbm)
    one, two = center_line()
    orders.wait()
    kernel_grad(mine_ref, theirs_ref, scr_a, 2, center * tile_lines(one + two, ROWS), order_ref)
    mines = fetch(sems, 7, mine_ref, mine_hbm)
    others = fetch(sems, 8, theirs_ref, theirs_hbm)
    turned.wait()
    turn_taps(turn_ref, wt_ref)
    da2 = conv_turned(scr_u, turn_ref, 10)
    e = da2 * silu_slope(n2[2 * LINE : 12 * LINE]) * flat(gain_ref)
    e_ref[...] = e
    es = fetch(sems, 10, e_ref, e_hbm)
    sums = pair_sums(e[LINE : 9 * LINE], nhat[3 * LINE : 11 * LINE], table)
    out_ref[...] = jnp.broadcast_to(sums, (DEVICES, 128))
    outs = fetch_all(sems, 18, [(out_ref, out_hbm), (err_ref, err_hbm)])
    wait_all([bouts, us, mines, others, es] + kept + outs)


def back_line(sums_ref, table):
    sums = jnp.sum(sums_ref[...], axis=0, keepdims=True) * (1.0 / TOTAL)
    one, two, three, four = expand(sums, table)
    return per_line(one, two), per_line(three, four)


def third_kernel(
    second_hbm, sums_hbm, first_hbm, gain_hbm, shift_hbm, errs_hbm, e_hbm, n_hbm, taps_hbm, order_hbm, x_hbm, wt_hbm,
    out_hbm, mine_hbm, theirs_hbm, back_hbm,
    out_ref, second_ref, sums_ref, first_ref, gain_ref, shift_ref, errs_ref, e_ref, n_ref, taps_ref, order_ref, x_ref, wt_ref,
    mine_ref, theirs_ref, back_ref, turn_ref, scr, sems,
):
    small = fetch_all(sems, 0, [(second_hbm, second_ref), (sums_hbm, sums_ref)])
    main = fetch_all(sems, 2, [(n_hbm, n_ref), (e_hbm, e_ref)])
    grads = fetch_all(sems, 4, [(order_hbm, order_ref), (taps_hbm, taps_ref)])
    rest = fetch_all(
        sems, 6,
        [
            (first_hbm, first_ref), (gain_hbm, gain_ref), (shift_hbm, shift_ref), (errs_hbm, errs_ref),
            (x_hbm.at[4 * LINE : 12 * LINE, :], x_ref), (wt_hbm, wt_ref),
        ],
    )
    table = hot()
    wait_all(small)
    first, second = back_line(sums_ref, table)
    scale = tile_lines(norm_lines(kept_rows(second_ref))[1], 10)
    wait_all(main)
    dh = scale * (e_ref[...] - tile_lines(first, 10) - n_ref[...] * tile_lines(second, 10))
    dh = masked(dh, 3, 10)
    spread_taps(scr, dh)
    one, two = center_line()
    wait_all(grads)
    kernel_grad(mine_ref, theirs_ref, taps_ref, 0, dh[LINE : 9 * LINE] * tile_lines(one + two, ROWS), order_ref)
    outs = fetch_all(sems, 12, [(theirs_ref, theirs_hbm), (mine_ref, mine_hbm)])
    wait_all(rest)
    mean, rstd = norm_lines(kept_rows(first_ref))
    nhat = (x_ref[...].astype(F32) - tile_lines(mean, ROWS)) * tile_lines(rstd, ROWS)
    n1 = nhat * flat(gain_ref) + flat(shift_ref)
    turn_taps(turn_ref, wt_ref)
    e1 = conv_turned(scr, turn_ref, ROWS) * (silu_slope(n1) * flat(gain_ref))
    back_ref[...] = e1
    outs = outs + [fetch(sems, 14, back_ref, back_hbm)]
    out_ref[0:1] = pair_sums(e1, nhat, table)
    out_ref[1:2] = errs_ref[...]
    wait_all(outs + [fetch(sems, 15, out_ref, out_hbm)])


def last_kernel(sums_ref, info_ref, norm_ref, e_ref, x_ref, u_ref, out_ref, scr):
    weight = info_ref[0:1, 0:1]
    table = hot()
    mean, rstd = norm_lines(kept_rows(norm_ref))
    first, second = back_line(sums_ref, table)
    scale = tile_lines(rstd, ROWS)
    nhat = (x_ref[4 * LINE : 12 * LINE, :].astype(F32) - tile_lines(mean, ROWS)) * scale
    dx = scale * (e_ref[...] - tile_lines(first, ROWS) - nhat * tile_lines(second, ROWS))
    scr[...] = (u_ref[...].astype(F32) + dx) * weight
    centered(out_ref, scr)


def piece_rows(count, at, sums, errs):
    index = lax.broadcasted_iota(jnp.int32, (count, 128), 0)
    out = jnp.zeros((count, 128), F32)
    for i, piece in enumerate(pieces(sums) + pieces(errs)):
        out = out + jnp.where(index == at + i, piece, 0.0)
    return out


def centered(out_ref, scr):
    for b in range(2):
        for y in range(ROWS):
            at = y * LINE + b * GW + RIM
            out_ref[(b * ROWS + y) * COLS : (b * ROWS + y + 1) * COLS] = scr[at : at + COLS].astype(BF16)


def early_kernel(mine_ref, got_ref, lines_ref, block_ref, *outs):
    outs, scr = outs[:4], outs[4]
    scr[...] = lines_ref[...].astype(F32)
    centered(block_ref, scr)
    y = lax.axis_index("y")
    for k, out_ref in enumerate(outs):
        rows = pl.ds(pl.multiple_of(lax.rem(y + k, 4) * 80, 16), 80)
        out_ref[...] = (mine_ref[rows, :].astype(F32) + got_ref[rows, :].astype(F32)).astype(BF16)


def late_kernel(mine_ref, got_ref, part_ref, other_ref, out_ref):
    for j in range(4):
        for i in range(4):
            for k in range(3):
                rows = slice(j * 80, (j + 1) * 80)
                lanes = slice(i * 384 + k * 128, i * 384 + (k + 1) * 128)
                both = mine_ref[rows, lanes].astype(F32) + got_ref[rows, lanes].astype(F32)
                out_ref[j * 4 + i, k * 80 : (k + 1) * 80, :] = both.astype(BF16)
    tails = part_ref[...] + other_ref[...]
    rows = piece_rows(16, 0, tails[0:1], tails[1:2]).astype(BF16)
    for i in range(16):
        out_ref[i, 240:256, :] = rows


def middle_kernel(a_ref, b_ref, c_ref, d_ref, *outs):
    outs, scr = outs[:4], outs[4]
    scr[...] = (
        (a_ref[...].astype(F32) + b_ref[...].astype(F32)) + (c_ref[...].astype(F32) + d_ref[...].astype(F32))
    )
    x = lax.axis_index("x")
    for i, out_ref in enumerate(outs):
        for k in range(3):
            lanes = pl.ds(pl.multiple_of(lax.rem(x + i, 4) * 384 + k * 128, 128), 128)
            out_ref[k * 80 : (k + 1) * 80] = scr[:, lanes].astype(BF16)


def plane_kernel(in_ref, a_ref, b_ref, c_ref, d_ref, move_ref, out_ref):
    total = in_ref[0].astype(F32)
    for i in range(1, 16):
        total = total + in_ref[i].astype(F32)
    tail = total[240:256]
    sums = tail[0:1] + tail[1:2] + tail[2:3]
    errs = tail[3:4] + tail[4:5] + tail[5:6]
    rows = piece_rows(80, 60, sums, errs)
    other = (a_ref[...].astype(F32) + b_ref[...].astype(F32)) + (c_ref[...].astype(F32) + d_ref[...].astype(F32))
    both = jnp.concatenate([other, total[0:240]], axis=0).astype(BF16)
    moved = dot(move_ref[...], both)
    for z in range(8):
        out_ref[z] = (moved[z * 80 : (z + 1) * 80] + rows).astype(BF16)


def depth_kernel(in_ref, sign_ref, ref_ref, out_ref, sums_ref, info_ref, loss_ref):
    total = in_ref[0].astype(F32)
    for i in range(1, 8):
        total = total + in_ref[i].astype(F32)
    sums_ref[...] = total[60:61] + total[61:62] + total[62:63]
    errs = total[63:64] + total[64:65] + total[65:66]
    excess = errs[:, 0:2] * (1.0 / (BAND_ROWS * BAND_COLS * C)) - ref_ref[...]
    gap = 0.5 * flat(sign_ref)[:, 0:1] * (excess[:, 0:1] - excess[:, 1:2])
    weight = 1.0 / (1.0 + jnp.exp(-gap))
    loss = jnp.maximum(gap, 0.0) + jnp.log1p(jnp.exp(-jnp.abs(gap)))
    info_ref[...] = jnp.broadcast_to(weight, (1, 128))
    loss_ref[...] = loss
    grads = (total[0:64] * (weight * (2 * BAND_ROWS * BAND_COLS) ** -0.5)).astype(BF16)
    for i in range(8):
        out_ref[i] = grads


VM = pl.BlockSpec(memory_space=pltpu.VMEM)
HB = pl.BlockSpec(memory_space=pltpu.HBM)
DMA = pltpu.SemaphoreType.DMA


def call(kernel, outs, ins, scratch=(), flops=0):
    size = sum(int(np.prod(s.shape)) * s.dtype.itemsize for _, s in outs)
    size += sum(a.size * a.dtype.itemsize for _, a in ins)
    many = len(outs) > 1
    shapes, spaces = [s for _, s in outs], [p for p, _ in outs]
    return pl.pallas_call(
        kernel,
        out_shape=tuple(shapes) if many else shapes[0],
        in_specs=[p for p, _ in ins],
        out_specs=tuple(spaces) if many else spaces[0],
        scratch_shapes=list(scratch),
        compiler_params=pltpu.CompilerParams(vmem_limit_bytes=VMEM_LIMIT),
        cost_estimate=pl.CostEstimate(flops=flops, bytes_accessed=size, transcendentals=0),
    )(*[a for _, a in ins])


def sds(shape, dtype=F32):
    return jax.ShapeDtypeStruct(shape, dtype)


AXES = ("x", "c", "z", "y")


def share(rows):
    return lax.all_to_all(rows, AXES, 0, 0, tiled=True)


def widen(features, target, near, far, part):
    strip, wide = sds((176, C), BF16), pltpu.VMEM((896, C), F32)
    edge = pltpu.VMEM((176, C), F32)
    ins = [(VM, features), (VM, target), (VM, near), (VM, far)]
    right, left = call(pack_kernel, [(VM, strip), (VM, strip)], ins, [wide, edge, edge])
    right, left, part = lax.optimization_barrier((right, left, part))
    inner = [(i, i ^ 1) for i in range(32)]
    outer = [(i, ((i - 1) ^ 1) + 1) for i in range(1, 31)]
    first = lax.ppermute(left, ("z", "y"), outer)
    last = lax.ppermute(right, ("z", "y"), inner)
    f, t = call(
        grid_kernel,
        [(VM, sds((GH * LINE, C), BF16)), (VM, sds((12 * LINE, C), BF16))],
        ins + [(VM, first), (VM, last)],
        [wide, edge, edge, pltpu.VMEM(((GH + 12) * LINE, C), F32)],
        10**10,
    )
    return f, t, part


def time_embed(timestep, time_weight):
    half = TEMB // 2
    freqs = jnp.exp(-jnp.log(10000.0) * jnp.arange(half, dtype=F32) / half)
    angles = timestep.astype(F32)[:, None] * freqs[None, :]
    emb = jnp.concatenate([jnp.cos(angles), jnp.sin(angles)], axis=1)
    return jnp.dot(jax.nn.silu(emb), time_weight.astype(F32), precision=HIGH)


def order_matrix():
    out = np.zeros((C, C), np.float32)
    for z in range(8):
        for y in range(4):
            for j in range(10):
                out[y * 80 + z * 10 + j, z * 40 + y * 10 + j] = 1.0
    return jnp.asarray(out, BF16)


def move_matrix():
    out = np.zeros((640, 480), np.float32)
    for grad in range(2):
        for k in range(3):
            for z in range(8):
                for j in range(10):
                    out[z * 80 + grad * 30 + k * 10 + j, grad * 240 + k * 80 + z * 10 + j] = 1.0
    return jnp.asarray(out, BF16)


def shift(block, axis, by):
    return lax.ppermute(block, axis, [(i, (i + by) % 4) for i in range(4)])


def swap(theirs):
    return lax.ppermute(theirs, "c", [(0, 1), (1, 0)])


def body(
    features, target, norm1_gain, norm1_shift, kernel1, bias1, time_weight, time_bias,
    norm2_gain, norm2_shift, kernel2, bias2, ref_error, preference, timestep,
):
    sign = jnp.broadcast_to(jnp.where(preference == 0, 2.0, -2.0).astype(F32), (C,))
    strip, cells = sds((2 * 6 * COLS, C), BF16), 2 * ROWS * COLS
    part, near, far = call(
        moments_kernel,
        [(VM, sds((DEVICES, 128))), (VM, strip), (VM, strip)],
        [(VM, features.reshape(cells, C)), (VM, target.reshape(cells, C))],
    )
    far = lax.ppermute(far, ("x", "c"), [(1, 2), (2, 1), (3, 4), (4, 3), (5, 6), (6, 5)])
    near = swap(near)
    fx, tx, part = widen(features.reshape(cells, C), target.reshape(cells, C), near, far, part)
    stats1 = share(part)
    temb = time_embed(timestep, time_weight).reshape(C)
    order, move = order_matrix(), move_matrix()
    w1, w2 = kernel1.reshape(3, 3 * C, C), kernel2.reshape(3, 3 * C, C)
    conv_flops = 2 * 9 * C * C * LINE
    half = sds((C, LANES // 2), BF16)
    row, table, lines = sds((1, 128)), sds((DEVICES, 128)), sds((ROWS * LINE, C), BF16)
    full = sds((3, 3, C, C), BF16)
    rows4, tbl = sds((4, C)), pltpu.VMEM((DEVICES, 128), F32)
    part, norm1, h1, taps1 = call(
        first_kernel,
        [(HB, table), (HB, rows4), (HB, sds((14 * LINE, C))), (HB, sds((10 * LINE, 3 * C), BF16))],
        [(HB, v) for v in (stats1, norm1_gain, norm1_shift, bias1, temb, time_bias, fx, w1)],
        [
            pltpu.VMEM((GH * LINE, 3 * C), BF16), pltpu.VMEM((3, 3 * C, C), BF16),
            pltpu.VMEM((GH * LINE, C), BF16), pltpu.VMEM((14 * LINE, C), F32), tbl, pltpu.VMEM((4, C), F32),
            tbl, *[pltpu.VMEM((C,), F32)] * 5, DMA((12,)),
        ],
        14 * conv_flops,
    )
    stats2 = share(part)
    part, errs, norm2, nhat2, e2, bout, u, mine2, theirs2 = call(
        second_kernel,
        [
            (HB, table), (HB, row), (HB, rows4), (HB, sds((10 * LINE, C))), (HB, sds((10 * LINE, C))), (HB, lines), (HB, lines), (HB, half), (HB, half),
        ],
        [
            (HB, v)
            for v in (stats2, norm2_gain, norm2_shift, bias2, sign, h1, w2, kernel2, fx, tx, order)
        ],
        [
            pltpu.VMEM((14 * LINE, 3 * C), BF16), pltpu.VMEM((12 * LINE, 3 * C), BF16),
            pltpu.VMEM((3, 3 * C, C), BF16), pltpu.VMEM(full.shape, BF16),
            pltpu.VMEM((12 * LINE, C), BF16), pltpu.VMEM((12 * LINE, C), BF16), pltpu.VMEM((C, C), BF16),
            pltpu.VMEM((ROWS * LINE, C), BF16), pltpu.VMEM((ROWS * LINE, C), BF16),
            pltpu.VMEM((C, LANES // 2), BF16), pltpu.VMEM((C, LANES // 2), BF16),
            pltpu.VMEM((14 * LINE, C), F32), pltpu.VMEM((10 * LINE, C), F32), pltpu.VMEM((3, C, 3 * C), BF16),
            tbl, pltpu.VMEM((1, 128), F32), pltpu.VMEM((4, C), F32), pltpu.VMEM((10 * LINE, C), F32),
            tbl, *[pltpu.VMEM((C,), F32)] * 4, DMA((20,)),
        ],
        30 * conv_flops,
    )
    sums2 = share(part)
    got2 = swap(theirs2)
    block_out, *strips = call(
        early_kernel,
        [(VM, sds((cells, C), BF16))] + [(VM, sds((80, LANES // 2), BF16))] * 4,
        [(VM, mine2), (VM, got2), (VM, bout)],
        [pltpu.VMEM((ROWS * LINE, C), F32)],
    )
    block_out = block_out.reshape(2, ROWS, COLS, C)
    strips = [strips[0]] + [shift(strips[k], "y", k) for k in (2, 1, 3)]
    sums2, strips[0] = lax.optimization_barrier((sums2, strips[0]))
    part, mine1, theirs1, e1 = call(
        third_kernel,
        [(HB, sds((2, 128))), (HB, half), (HB, half), (HB, sds((ROWS * LINE, C)))],
        [
            (HB, v)
            for v in (
                norm2, sums2, norm1, norm1_gain, norm1_shift, errs, e2, nhat2, taps1, order, fx, kernel1,
            )
        ],
        [
            pltpu.VMEM((2, 128), F32), pltpu.VMEM((4, C), F32), tbl, pltpu.VMEM((4, C), F32),
            *[pltpu.VMEM((C,), F32)] * 2, pltpu.VMEM((1, 128), F32),
            pltpu.VMEM((10 * LINE, C), F32), pltpu.VMEM((10 * LINE, C), F32),
            pltpu.VMEM((10 * LINE, 3 * C), BF16), pltpu.VMEM((C, C), BF16),
            pltpu.VMEM((ROWS * LINE, C), BF16), pltpu.VMEM(full.shape, BF16),
            pltpu.VMEM(half.shape, BF16), pltpu.VMEM(half.shape, BF16), pltpu.VMEM((ROWS * LINE, C), F32),
            pltpu.VMEM((3, C, 3 * C), BF16),
            pltpu.VMEM((10 * LINE, 3 * C), BF16), DMA((16,)),
        ],
        16 * conv_flops,
    )
    theirs1, *strips = lax.optimization_barrier((theirs1, *strips))
    got1, other = swap(theirs1), swap(part)
    parts = call(
        middle_kernel,
        [(VM, sds((240, 128), BF16))] * 4,
        [(VM, v) for v in strips],
        [pltpu.VMEM((80, LANES // 2), F32)],
    )
    parts = list(parts)
    got1, parts[0] = lax.optimization_barrier((got1, parts[0]))
    plane = call(
        late_kernel,
        [(VM, sds((16, 256, 128), BF16))],
        [(VM, mine1), (VM, got1), (VM, part), (VM, other)],
    )
    plane, *parts = lax.optimization_barrier((plane, *parts))
    plane = lax.all_to_all(plane, ("y", "x"), 0, 0, tiled=True)
    parts = [parts[0]] + [shift(parts[k], "x", k) for k in range(1, 4)]
    depth = call(
        plane_kernel,
        [(VM, sds((8, 80, 128), BF16))],
        [(VM, plane)] + [(VM, v) for v in parts] + [(VM, move)],
    )
    depth = lax.all_to_all(depth, ("z",), 0, 0, tiled=True)
    copies, sums1, info, loss = call(
        depth_kernel,
        [(VM, sds((8, 64, 128), BF16)), (VM, row), (VM, row), (VM, sds((1, 1)))],
        [(VM, depth), (VM, sign), (VM, ref_error)],
    )
    whole = lax.all_to_all(copies, ("c", "x"), 0, 0, tiled=True)
    grad = call(
        last_kernel,
        [(VM, sds((cells, C), BF16))],
        [(VM, sums1), (VM, info), (VM, norm1), (VM, e1), (VM, fx), (VM, u)],
        [pltpu.VMEM((ROWS * LINE, C), F32)],
    )
    feature_grad = grad.reshape(2, ROWS, COLS, C)
    whole = whole[:, :60].reshape(2, 4, 2, 3, 10, 128).transpose(2, 0, 1, 3, 5, 4).reshape(2, LANES, 10)
    whole = whole[:, :TAPS].astype(F32).reshape(2, 3, 3, C, 10)
    loss = loss.reshape(())
    return (block_out, feature_grad, whole[1], whole[0], loss)


def solution(mesh):
    fine = Mesh(mesh.devices.reshape(4, 2, 8, 4), AXES)
    cells = P(None, ("x", "c"), ("z", "y"), None)
    kernels = P(None, None, None, ("z", "y"))
    return jax.shard_map(
        body,
        mesh=fine,
        in_specs=(cells, cells) + (P(),) * 13,
        out_specs=(cells, cells, kernels, kernels, P()),
        check_vma=False,
    )
```

```python
import functools

import jax
import jax.numpy as jnp
import numpy as np
from jax import lax
from jax.experimental import pallas as pl
from jax.experimental.pallas import tpu as pltpu
from jax.sharding import Mesh
from jax.sharding import PartitionSpec as P

GROUPS = 32
TEMB = 1280
C = 320
WIDTH = C // GROUPS
ROWS, COLS = 8, 16
BAND_ROWS, BAND_COLS = 64, 512
RIM = 4
GH, GW = ROWS + 2 * RIM, COLS + 2 * RIM
LINE = 2 * GW
DEVICES = 256
LOCAL = ROWS * COLS * WIDTH
TOTAL = LOCAL * DEVICES
TAPS = 9 * C
LANES = 3072
EPS = 1e-05
F32, BF16 = jnp.float32, jnp.bfloat16
HIGH = lax.Precision.HIGHEST
VMEM_LIMIT = 63 * 2**20


def dot(a, b):
    return jnp.dot(a, b, preferred_element_type=F32)


def pieces(row):
    high = row.astype(BF16).astype(F32)
    rest = row - high
    mid = rest.astype(BF16).astype(F32)
    return high, mid, rest - mid


def hot():
    blocks = []
    for slot in range(4):
        low = (lax.broadcasted_iota(jnp.int32, (128, 384), 0) - slot * GROUPS) * WIDTH
        chan = lax.broadcasted_iota(jnp.int32, (128, 384), 1)
        blocks.append(((chan >= low) & (chan < low + WIDTH) & (chan < C)).astype(F32).astype(BF16))
    return jnp.concatenate(blocks, axis=1)


def stacked(row):
    index = lax.broadcasted_iota(jnp.int32, (16, row.shape[1]), 0)
    out = jnp.zeros((16, row.shape[1]), F32)
    for i, piece in enumerate(pieces(row)):
        out = jnp.where(index == i, piece, out)
    return out.astype(BF16)


def expand(row, table):
    wide = jnp.sum(dot(stacked(row), table), axis=0, keepdims=True)
    return [wide[:, i * 384 : i * 384 + C] for i in range(4)]


def collapse(rows, table):
    gap, empty = jnp.zeros((1, 384 - C), F32), jnp.zeros((1, C), F32)
    wide = jnp.concatenate([v for row in rows for v in (empty if row is None else row, gap)], axis=1)
    small = lax.dot_general(stacked(wide), table, (((1,), (1,)), ((), ())), preferred_element_type=F32)
    return jnp.sum(small, axis=0, keepdims=True)


def per_line(first, second):
    return jnp.concatenate(
        [jnp.broadcast_to(first, (GW, C)), jnp.broadcast_to(second, (GW, C))], axis=0
    )


def tile_lines(line, count):
    return jnp.broadcast_to(line[None], (count, LINE, C)).reshape(count * LINE, C)


def masked(values, top, count):
    high = lax.axis_index("x") * 2 + lax.axis_index("c")
    wide = lax.axis_index("z") * 4 + lax.axis_index("y")
    col = lax.broadcasted_iota(jnp.int32, (LINE, C), 0)
    gx = jnp.where(col >= GW, col - GW, col) + (wide * COLS - RIM)
    line = ((gx >= 0) & (gx < BAND_COLS)).astype(F32)
    upper = line * jnp.where(high > 0, 1.0, 0.0)
    lower = line * jnp.where(high < BAND_ROWS // ROWS - 1, 1.0, 0.0)
    parts = [(upper, RIM - top), (line, ROWS), (lower, top + count - RIM - ROWS)]
    mask = jnp.concatenate([jnp.broadcast_to(v[None], (n, LINE, C)) for v, n in parts], axis=0)
    return values * mask.reshape(count * LINE, C)


def center_line():
    col = lax.broadcasted_iota(jnp.int32, (LINE, C), 0)
    one = (col >= RIM) & (col < RIM + COLS)
    two = (col >= GW + RIM) & (col < GW + RIM + COLS)
    return one.astype(F32), two.astype(F32)


def line_sums(values):
    total = jnp.sum(values.reshape(ROWS, LINE, C), axis=0)
    return [jnp.sum(total * line, axis=0, keepdims=True) for line in center_line()]


def norm_rows(stats_ref, table):
    stats = stats_ref[...]
    sums = jnp.sum(stats, axis=0, keepdims=True)
    mean = sums * (1.0 / DEVICES)
    off = stats - mean
    spread = jnp.sum(off * off, axis=0, keepdims=True) * LOCAL
    var = (sums + pltpu.roll(spread, 64, 1)) * (1.0 / TOTAL)
    lane = lax.broadcasted_iota(jnp.int32, (1, 128), 1)
    row = jnp.where(lane < 64, mean, 1.0 / jnp.sqrt(jnp.maximum(var, 0.0) + EPS))
    return expand(row, table)


def norm_lines(rows):
    return per_line(rows[0], rows[1]), per_line(rows[2], rows[3])


def kept_rows(ref):
    return [ref[i : i + 1, :] for i in range(4)]


def keep_rows(ref, rows):
    for i, row in enumerate(rows):
        ref[i : i + 1, :] = row


def moments(values, table):
    first, second = line_sums(values)
    means = collapse([first, second, None, None], table) * (1.0 / LOCAL)
    one, two, _, _ = expand(means, table)
    off = values - tile_lines(per_line(one, two), ROWS)
    first, second = line_sums(off * off)
    return means + collapse([None, None, first, second], table)


def pair_sums(scaled, normed, table):
    return collapse(line_sums(scaled) + line_sums(scaled * normed), table)


def sigmoid(v):
    return 0.5 + 0.5 * jnp.tanh(0.5 * v)


def silu_slope(v):
    sig = sigmoid(v)
    return sig * (1.0 + v * (1.0 - sig))


def spread_taps(ref, values):
    count = values.shape[0]
    ref[:, 0:C] = pltpu.roll(values, 1, 0).astype(BF16)
    ref[:, C : 2 * C] = values.astype(BF16)
    ref[:, 2 * C : 3 * C] = pltpu.roll(values, count - 1, 0).astype(BF16)


def conv_lines(ref, weights_ref, count):
    total = dot(ref[0 : count * LINE, :], weights_ref[0])
    for ky in range(1, 3):
        total = total + dot(ref[ky * LINE : (ky + count) * LINE, :], weights_ref[ky])
    return total


def turn_taps(ref, weights_ref):
    for ky in range(3):
        for kx in range(3):
            ref[ky, :, kx * C : (kx + 1) * C] = weights_ref[2 - ky, 2 - kx]


def conv_turned(ref, weights_ref, count):
    total = None
    for ky in range(3):
        part = lax.dot_general(
            ref[ky * LINE : (ky + count) * LINE, :],
            weights_ref[ky],
            (((1,), (1,)), ((), ())),
            preferred_element_type=F32,
        )
        total = part if total is None else total + part
    return total


def kernel_grad(mine_ref, theirs_ref, taps_ref, top, grads, order_ref):
    core = lax.axis_index("c")
    left = lax.dot_general(
        order_ref[...], grads.astype(BF16), (((1,), (1,)), ((), ())), preferred_element_type=F32
    ).astype(BF16)
    parts = []
    for ky in range(3):
        lines = taps_ref[(top + ky) * LINE : (top + ky + ROWS) * LINE, :]
        parts.append(dot(left, lines).astype(BF16))
    parts.append(jnp.zeros((C, LANES - TAPS), BF16))
    whole = jnp.concatenate(parts, axis=1)
    low, high = whole[:, : LANES // 2], whole[:, LANES // 2 :]

    @pl.when(core == 0)
    def _():
        mine_ref[...] = low
        theirs_ref[...] = high

    @pl.when(core == 1)
    def _():
        mine_ref[...] = high
        theirs_ref[...] = low


def fetch(sems, index, src, dst):
    copy = pltpu.make_async_copy(src, dst, sems.at[index])
    copy.start()
    return copy


def fetch_all(sems, first, pairs):
    return [fetch(sems, first + i, src, dst) for i, (src, dst) in enumerate(pairs)]


def wait_all(copies):
    for copy in copies:
        copy.wait()


def flat(ref):
    return ref[...].reshape(1, C)


def moments_kernel(x_ref, t_ref, out_ref, near_ref, far_ref):
    half, core = ROWS * COLS, lax.axis_index("c")
    for b in range(2):
        at, to = b * half, b * 6 * COLS
        parts = [
            (x_ref[at + 4 * COLS : at + 8 * COLS, :], x_ref[at : at + 4 * COLS, :], to, 4 * COLS),
            (t_ref[at + 6 * COLS : at + 8 * COLS, :], t_ref[at : at + 2 * COLS, :], to + 4 * COLS, 2 * COLS),
        ]
        for bottom, top, first, count in parts:
            near_ref[first : first + count] = jnp.where(core == 0, bottom, top)
            far_ref[first : first + count] = jnp.where(core == 0, top, bottom)
    table = hot()
    values = [x_ref[b * half : (b + 1) * half, :].astype(F32) for b in range(2)]
    sums = [jnp.sum(v, axis=0, keepdims=True) for v in values]
    means = collapse(sums + [None, None], table) * (1.0 / LOCAL)
    offs = [v - m for v, m in zip(values, expand(means, table))]
    sums = [jnp.sum(v * v, axis=0, keepdims=True) for v in offs]
    out = means + collapse([None, None] + sums, table)
    out_ref[...] = jnp.broadcast_to(out, (DEVICES, 128))


def strip_blocks():
    out, row = [], 0
    for b in range(2):
        low, high = 512 + b * 6 * COLS, 704 + b * 6 * COLS
        for y in range(GH):
            start = low + y * COLS if y < 4 else b * 128 + (y - 4) * COLS if y < 12 else high + (y - 12) * COLS
            out.append((row, RIM, start, y * LINE + b * GW))
            row += RIM
        for y in range(12):
            start = low + (4 + y) * COLS if y < 2 else 256 + b * 128 + (y - 2) * COLS if y < 10 else high + (y - 6) * COLS
            out.append((row, 2, start, (GH + y) * LINE + b * GW))
            row += 2
    return out


def widened(scr, x_ref, t_ref, near_ref, far_ref):
    core = lax.axis_index("c")
    near, far = near_ref[...].astype(F32), far_ref[...].astype(F32)
    scr[0:256] = x_ref[...].astype(F32)
    scr[256:512] = t_ref[...].astype(F32)
    scr[512:704] = jnp.where(core == 0, far, near)
    scr[704:896] = jnp.where(core == 0, near, far)


def pack_kernel(x_ref, t_ref, near_ref, far_ref, right_ref, left_ref, scr, right, left):
    widened(scr, x_ref, t_ref, near_ref, far_ref)
    for row, width, start, _ in strip_blocks():
        left[row : row + width] = scr[start : start + width]
        right[row : row + width] = scr[start + COLS - width : start + COLS]
    even = lax.rem(lax.axis_index("y"), 2) == 0
    right_ref[...] = jnp.where(even, right[...], left[...]).astype(BF16)
    left_ref[...] = jnp.where(even, left[...], right[...]).astype(BF16)


def grid_kernel(x_ref, t_ref, near_ref, far_ref, first_ref, last_ref, f_ref, g_ref, scr, first, last, grid):
    widened(scr, x_ref, t_ref, near_ref, far_ref)
    even = lax.rem(lax.axis_index("y"), 2) == 0
    first[...] = jnp.where(even, first_ref[...].astype(F32), last_ref[...].astype(F32))
    last[...] = jnp.where(even, last_ref[...].astype(F32), first_ref[...].astype(F32))
    empty = jnp.zeros((2, C), F32)
    for row, width, start, at in strip_blocks():
        inner = at + RIM
        grid[inner - width : inner] = first[row : row + width]
        grid[inner : inner + COLS] = scr[start : start + COLS]
        grid[inner + COLS : inner + COLS + width] = last[row : row + width]
        if width == 2:
            grid[at : at + 2] = empty
            grid[at + GW - 2 : at + GW] = empty
    f_ref[...] = grid[0 : GH * LINE].astype(BF16)
    g_ref[...] = grid[GH * LINE : (GH + 12) * LINE].astype(BF16)


def first_kernel(
    stats_hbm, gain_hbm, shift_hbm, bias_hbm, temb_hbm, time_hbm, x_hbm, w_hbm,
    out_hbm, rows_hbm, h_hbm, taps_hbm, scr, w_ref, x_ref, h_ref, out_ref, rows_ref,
    stats_ref, gain_ref, shift_ref, bias_ref, temb_ref, time_ref, sems,
):
    small = fetch_all(
        sems, 4,
        [
            (stats_hbm, stats_ref), (gain_hbm, gain_ref), (shift_hbm, shift_ref),
            (bias_hbm, bias_ref), (temb_hbm, temb_ref), (time_hbm, time_ref),
        ],
    )
    xs = fetch(sems, 2, x_hbm, x_ref)
    weights = fetch(sems, 0, w_hbm, w_ref)
    table = hot()
    wait_all(small)
    rows = norm_rows(stats_ref, table)
    keep_rows(rows_ref, rows)
    kept = fetch(sems, 11, rows_ref, rows_hbm)
    mean, rstd = norm_lines(rows)
    scale = tile_lines(rstd * flat(gain_ref), GH)
    xs.wait()
    n1 = (x_ref[...].astype(F32) - tile_lines(mean, GH)) * scale + flat(shift_ref)
    spread_taps(scr, masked(n1 * sigmoid(n1), 0, GH))
    taps = fetch(sems, 1, scr.at[3 * LINE : 13 * LINE, :], taps_hbm)
    weights.wait()
    h1 = conv_lines(scr, w_ref, GH - 2) + (flat(bias_ref) + (flat(temb_ref) + flat(time_ref)))
    h_ref[...] = h1
    hs = fetch(sems, 3, h_ref, h_hbm)
    out_ref[...] = jnp.broadcast_to(moments(h1[3 * LINE : 11 * LINE], table), (DEVICES, 128))
    outs = fetch(sems, 10, out_ref, out_hbm)
    wait_all([taps, hs, kept, outs])


def second_kernel(
    stats_hbm, gain_hbm, shift_hbm, bias_hbm, sign_hbm, h_hbm, w_hbm, wt_hbm, x_hbm, t_hbm, order_hbm,
    out_hbm, err_hbm, rows_hbm, n_hbm, e_hbm, bout_hbm, u_hbm, mine_hbm, theirs_hbm,
    scr_a, scr_u, w_ref, wt_ref, x_ref, t_ref, order_ref, bout_ref, u_ref, mine_ref, theirs_ref, h_ref, e_ref, turn_ref,
    out_ref, err_ref, rows_ref, n_ref, stats_ref, gain_ref, shift_ref, bias_ref, sign_ref, sems,
):
    small = fetch_all(
        sems, 11,
        [
            (stats_hbm, stats_ref), (gain_hbm, gain_ref), (shift_hbm, shift_ref),
            (bias_hbm, bias_ref), (sign_hbm, sign_ref),
        ],
    )
    hs = fetch(sems, 9, h_hbm, h_ref)
    weights = fetch(sems, 0, w_hbm, w_ref)
    xs = fetch(sems, 1, x_hbm.at[2 * LINE : 14 * LINE, :], x_ref)
    ts = fetch(sems, 2, t_hbm, t_ref)
    orders = fetch(sems, 4, order_hbm, order_ref)
    turned = fetch(sems, 3, wt_hbm, wt_ref)
    table = hot()
    wait_all(small)
    rows = norm_rows(stats_ref, table)
    keep_rows(rows_ref, rows)
    mean, rstd = norm_lines(rows)
    hs.wait()
    nhat = (h_ref[...] - tile_lines(mean, GH - 2)) * tile_lines(rstd, GH - 2)
    n_ref[...] = nhat[2 * LINE : 12 * LINE]
    kept = fetch_all(sems, 16, [(rows_ref, rows_hbm), (n_ref, n_hbm)])
    n2 = nhat * flat(gain_ref) + flat(shift_ref)
    spread_taps(scr_a, masked(n2 * sigmoid(n2), 1, GH - 2))
    weights.wait()
    conv = conv_lines(scr_a, w_ref, 12) + flat(bias_ref)
    xs.wait()
    out = x_ref[...].astype(F32) + conv
    bout_ref[...] = out[2 * LINE : 10 * LINE].astype(BF16)
    bouts = fetch(sems, 5, bout_ref, bout_hbm)
    ts.wait()
    diff = out - t_ref[...].astype(F32)
    mid = diff[2 * LINE : 10 * LINE]
    lane = lax.broadcasted_iota(jnp.int32, (1, 128), 1)
    errs = jnp.zeros((1, 128), F32)
    for b, part in enumerate(line_sums(mid * mid)):
        errs = errs + jnp.where(lane == b, jnp.sum(part, axis=1, keepdims=True), 0.0)
    err_ref[...] = errs
    sign = tile_lines(per_line(flat(sign_ref), -flat(sign_ref)), 12)
    u = masked(diff * sign, 2, 12)
    spread_taps(scr_u, u)
    center = u[2 * LINE : 10 * LINE]
    u_ref[...] = center.astype(BF16)
    us = fetch(sems, 6, u_ref, u_hbm)
    one, two = center_line()
    orders.wait()
    kernel_grad(mine_ref, theirs_ref, scr_a, 2, center * tile_lines(one + two, ROWS), order_ref)
    mines = fetch(sems, 7, mine_ref, mine_hbm)
    others = fetch(sems, 8, theirs_ref, theirs_hbm)
    turned.wait()
    turn_taps(turn_ref, wt_ref)
    da2 = conv_turned(scr_u, turn_ref, 10)
    e = da2 * silu_slope(n2[2 * LINE : 12 * LINE]) * flat(gain_ref)
    e_ref[...] = e
    es = fetch(sems, 10, e_ref, e_hbm)
    sums = pair_sums(e[LINE : 9 * LINE], nhat[3 * LINE : 11 * LINE], table)
    out_ref[...] = jnp.broadcast_to(sums, (DEVICES, 128))
    outs = fetch_all(sems, 18, [(out_ref, out_hbm), (err_ref, err_hbm)])
    wait_all([bouts, us, mines, others, es] + kept + outs)


def back_line(sums_ref, table):
    sums = jnp.sum(sums_ref[...], axis=0, keepdims=True) * (1.0 / TOTAL)
    one, two, three, four = expand(sums, table)
    return per_line(one, two), per_line(three, four)


def third_kernel(
    second_hbm, sums_hbm, first_hbm, gain_hbm, shift_hbm, errs_hbm, e_hbm, n_hbm, taps_hbm, order_hbm, x_hbm, wt_hbm,
    out_hbm, mine_hbm, theirs_hbm, back_hbm,
    out_ref, second_ref, sums_ref, first_ref, gain_ref, shift_ref, errs_ref, e_ref, n_ref, taps_ref, order_ref, x_ref, wt_ref,
    mine_ref, theirs_ref, back_ref, turn_ref, scr, sems,
):
    small = fetch_all(sems, 0, [(second_hbm, second_ref), (sums_hbm, sums_ref)])
    main = fetch_all(sems, 2, [(n_hbm, n_ref), (e_hbm, e_ref)])
    grads = fetch_all(sems, 4, [(order_hbm, order_ref), (taps_hbm, taps_ref)])
    rest = fetch_all(
        sems, 6,
        [
            (first_hbm, first_ref), (gain_hbm, gain_ref), (shift_hbm, shift_ref), (errs_hbm, errs_ref),
            (x_hbm.at[4 * LINE : 12 * LINE, :], x_ref), (wt_hbm, wt_ref),
        ],
    )
    table = hot()
    wait_all(small)
    first, second = back_line(sums_ref, table)
    scale = tile_lines(norm_lines(kept_rows(second_ref))[1], 10)
    wait_all(main)
    dh = scale * (e_ref[...] - tile_lines(first, 10) - n_ref[...] * tile_lines(second, 10))
    dh = masked(dh, 3, 10)
    spread_taps(scr, dh)
    one, two = center_line()
    wait_all(grads)
    kernel_grad(mine_ref, theirs_ref, taps_ref, 0, dh[LINE : 9 * LINE] * tile_lines(one + two, ROWS), order_ref)
    outs = fetch_all(sems, 12, [(theirs_ref, theirs_hbm), (mine_ref, mine_hbm)])
    wait_all(rest)
    mean, rstd = norm_lines(kept_rows(first_ref))
    nhat = (x_ref[...].astype(F32) - tile_lines(mean, ROWS)) * tile_lines(rstd, ROWS)
    n1 = nhat * flat(gain_ref) + flat(shift_ref)
    turn_taps(turn_ref, wt_ref)
    e1 = conv_turned(scr, turn_ref, ROWS) * (silu_slope(n1) * flat(gain_ref))
    back_ref[...] = e1
    outs = outs + [fetch(sems, 14, back_ref, back_hbm)]
    out_ref[0:1] = pair_sums(e1, nhat, table)
    out_ref[1:2] = errs_ref[...]
    wait_all(outs + [fetch(sems, 15, out_ref, out_hbm)])


def last_kernel(sums_ref, info_ref, norm_ref, e_ref, x_ref, u_ref, out_ref, scr):
    weight = info_ref[0:1, 0:1]
    table = hot()
    mean, rstd = norm_lines(kept_rows(norm_ref))
    first, second = back_line(sums_ref, table)
    scale = tile_lines(rstd, ROWS)
    nhat = (x_ref[4 * LINE : 12 * LINE, :].astype(F32) - tile_lines(mean, ROWS)) * scale
    dx = scale * (e_ref[...] - tile_lines(first, ROWS) - nhat * tile_lines(second, ROWS))
    scr[...] = (u_ref[...].astype(F32) + dx) * weight
    centered(out_ref, scr)


def piece_rows(count, at, sums, errs):
    index = lax.broadcasted_iota(jnp.int32, (count, 128), 0)
    out = jnp.zeros((count, 128), F32)
    for i, piece in enumerate(pieces(sums) + pieces(errs)):
        out = out + jnp.where(index == at + i, piece, 0.0)
    return out


def centered(out_ref, scr):
    for b in range(2):
        for y in range(ROWS):
            at = y * LINE + b * GW + RIM
            out_ref[(b * ROWS + y) * COLS : (b * ROWS + y + 1) * COLS] = scr[at : at + COLS].astype(BF16)


def early_kernel(mine_ref, got_ref, lines_ref, block_ref, *outs):
    outs, scr = outs[:4], outs[4]
    scr[...] = lines_ref[...].astype(F32)
    centered(block_ref, scr)
    y = lax.axis_index("y")
    for k, out_ref in enumerate(outs):
        rows = pl.ds(pl.multiple_of(lax.rem(y + k, 4) * 80, 16), 80)
        out_ref[...] = (mine_ref[rows, :].astype(F32) + got_ref[rows, :].astype(F32)).astype(BF16)


def late_kernel(mine_ref, got_ref, part_ref, other_ref, out_ref):
    for j in range(4):
        for i in range(4):
            for k in range(3):
                rows = slice(j * 80, (j + 1) * 80)
                lanes = slice(i * 384 + k * 128, i * 384 + (k + 1) * 128)
                both = mine_ref[rows, lanes].astype(F32) + got_ref[rows, lanes].astype(F32)
                out_ref[j * 4 + i, k * 80 : (k + 1) * 80, :] = both.astype(BF16)
    tails = part_ref[...] + other_ref[...]
    rows = piece_rows(16, 0, tails[0:1], tails[1:2]).astype(BF16)
    for i in range(16):
        out_ref[i, 240:256, :] = rows


def middle_kernel(a_ref, b_ref, c_ref, d_ref, *outs):
    outs, scr = outs[:4], outs[4]
    scr[...] = (
        (a_ref[...].astype(F32) + b_ref[...].astype(F32)) + (c_ref[...].astype(F32) + d_ref[...].astype(F32))
    )
    x = lax.axis_index("x")
    for i, out_ref in enumerate(outs):
        for k in range(3):
            lanes = pl.ds(pl.multiple_of(lax.rem(x + i, 4) * 384 + k * 128, 128), 128)
            out_ref[k * 80 : (k + 1) * 80] = scr[:, lanes].astype(BF16)


def plane_kernel(in_ref, a_ref, b_ref, c_ref, d_ref, move_ref, out_ref):
    total = in_ref[0].astype(F32)
    for i in range(1, 16):
        total = total + in_ref[i].astype(F32)
    tail = total[240:256]
    sums = tail[0:1] + tail[1:2] + tail[2:3]
    errs = tail[3:4] + tail[4:5] + tail[5:6]
    rows = piece_rows(80, 60, sums, errs)
    other = (a_ref[...].astype(F32) + b_ref[...].astype(F32)) + (c_ref[...].astype(F32) + d_ref[...].astype(F32))
    both = jnp.concatenate([other, total[0:240]], axis=0).astype(BF16)
    moved = dot(move_ref[...], both)
    for z in range(8):
        out_ref[z] = (moved[z * 80 : (z + 1) * 80] + rows).astype(BF16)


def depth_kernel(in_ref, sign_ref, ref_ref, out_ref, sums_ref, info_ref, loss_ref):
    total = in_ref[0].astype(F32)
    for i in range(1, 8):
        total = total + in_ref[i].astype(F32)
    sums_ref[...] = total[60:61] + total[61:62] + total[62:63]
    errs = total[63:64] + total[64:65] + total[65:66]
    excess = errs[:, 0:2] * (1.0 / (BAND_ROWS * BAND_COLS * C)) - ref_ref[...]
    gap = 0.5 * flat(sign_ref)[:, 0:1] * (excess[:, 0:1] - excess[:, 1:2])
    weight = 1.0 / (1.0 + jnp.exp(-gap))
    loss = jnp.maximum(gap, 0.0) + jnp.log1p(jnp.exp(-jnp.abs(gap)))
    info_ref[...] = jnp.broadcast_to(weight, (1, 128))
    loss_ref[...] = loss
    grads = (total[0:64] * (weight * (2 * BAND_ROWS * BAND_COLS) ** -0.5)).astype(BF16)
    for i in range(8):
        out_ref[i] = grads


VM = pl.BlockSpec(memory_space=pltpu.VMEM)
HB = pl.BlockSpec(memory_space=pltpu.HBM)
DMA = pltpu.SemaphoreType.DMA


def call(kernel, outs, ins, scratch=(), flops=0):
    size = sum(int(np.prod(s.shape)) * s.dtype.itemsize for _, s in outs)
    size += sum(a.size * a.dtype.itemsize for _, a in ins)
    many = len(outs) > 1
    shapes, spaces = [s for _, s in outs], [p for p, _ in outs]
    return pl.pallas_call(
        kernel,
        out_shape=tuple(shapes) if many else shapes[0],
        in_specs=[p for p, _ in ins],
        out_specs=tuple(spaces) if many else spaces[0],
        scratch_shapes=list(scratch),
        compiler_params=pltpu.CompilerParams(vmem_limit_bytes=VMEM_LIMIT),
        cost_estimate=pl.CostEstimate(flops=flops, bytes_accessed=size, transcendentals=0),
    )(*[a for _, a in ins])


def sds(shape, dtype=F32):
    return jax.ShapeDtypeStruct(shape, dtype)


AXES = ("x", "c", "z", "y")


def share(rows):
    return lax.all_to_all(rows, AXES, 0, 0, tiled=True)


def widen(features, target, near, far, part):
    strip, wide = sds((176, C), BF16), pltpu.VMEM((896, C), F32)
    edge = pltpu.VMEM((176, C), F32)
    ins = [(VM, features), (VM, target), (VM, near), (VM, far)]
    right, left = call(pack_kernel, [(VM, strip), (VM, strip)], ins, [wide, edge, edge])
    right, left, part = lax.optimization_barrier((right, left, part))
    inner = [(i, i ^ 1) for i in range(32)]
    outer = [(i, ((i - 1) ^ 1) + 1) for i in range(1, 31)]
    first = lax.ppermute(left, ("z", "y"), outer)
    last = lax.ppermute(right, ("z", "y"), inner)
    f, t = call(
        grid_kernel,
        [(VM, sds((GH * LINE, C), BF16)), (VM, sds((12 * LINE, C), BF16))],
        ins + [(VM, first), (VM, last)],
        [wide, edge, edge, pltpu.VMEM(((GH + 12) * LINE, C), F32)],
        10**10,
    )
    return f, t, part


def time_embed(timestep, time_weight):
    half = TEMB // 2
    freqs = jnp.exp(-jnp.log(10000.0) * jnp.arange(half, dtype=F32) / half)
    angles = timestep.astype(F32)[:, None] * freqs[None, :]
    emb = jnp.concatenate([jnp.cos(angles), jnp.sin(angles)], axis=1)
    return jnp.dot(jax.nn.silu(emb), time_weight.astype(F32), precision=HIGH)


def order_matrix():
    out = np.zeros((C, C), np.float32)
    for z in range(8):
        for y in range(4):
            for j in range(10):
                out[y * 80 + z * 10 + j, z * 40 + y * 10 + j] = 1.0
    return jnp.asarray(out, BF16)


def move_matrix():
    out = np.zeros((640, 480), np.float32)
    for grad in range(2):
        for k in range(3):
            for z in range(8):
                for j in range(10):
                    out[z * 80 + grad * 30 + k * 10 + j, grad * 240 + k * 80 + z * 10 + j] = 1.0
    return jnp.asarray(out, BF16)


def shift(block, axis, by):
    return lax.ppermute(block, axis, [(i, (i + by) % 4) for i in range(4)])


def swap(theirs):
    return lax.ppermute(theirs, "c", [(0, 1), (1, 0)])


def body(
    features, target, norm1_gain, norm1_shift, kernel1, bias1, time_weight, time_bias,
    norm2_gain, norm2_shift, kernel2, bias2, ref_error, preference, timestep,
):
    sign = jnp.broadcast_to(jnp.where(preference == 0, 2.0, -2.0).astype(F32), (C,))
    strip, cells = sds((2 * 6 * COLS, C), BF16), 2 * ROWS * COLS
    part, near, far = call(
        moments_kernel,
        [(VM, sds((DEVICES, 128))), (VM, strip), (VM, strip)],
        [(VM, features.reshape(cells, C)), (VM, target.reshape(cells, C))],
    )
    far = lax.ppermute(far, ("x", "c"), [(1, 2), (2, 1), (3, 4), (4, 3), (5, 6), (6, 5)])
    near = swap(near)
    fx, tx, part = widen(features.reshape(cells, C), target.reshape(cells, C), near, far, part)
    stats1 = share(part)
    temb = time_embed(timestep, time_weight).reshape(C)
    order, move = order_matrix(), move_matrix()
    w1, w2 = kernel1.reshape(3, 3 * C, C), kernel2.reshape(3, 3 * C, C)
    conv_flops = 2 * 9 * C * C * LINE
    half = sds((C, LANES // 2), BF16)
    row, table, lines = sds((1, 128)), sds((DEVICES, 128)), sds((ROWS * LINE, C), BF16)
    full = sds((3, 3, C, C), BF16)
    rows4, tbl = sds((4, C)), pltpu.VMEM((DEVICES, 128), F32)
    part, norm1, h1, taps1 = call(
        first_kernel,
        [(HB, table), (HB, rows4), (HB, sds((14 * LINE, C))), (HB, sds((10 * LINE, 3 * C), BF16))],
        [(HB, v) for v in (stats1, norm1_gain, norm1_shift, bias1, temb, time_bias, fx, w1)],
        [
            pltpu.VMEM((GH * LINE, 3 * C), BF16), pltpu.VMEM((3, 3 * C, C), BF16),
            pltpu.VMEM((GH * LINE, C), BF16), pltpu.VMEM((14 * LINE, C), F32), tbl, pltpu.VMEM((4, C), F32),
            tbl, *[pltpu.VMEM((C,), F32)] * 5, DMA((12,)),
        ],
        14 * conv_flops,
    )
    stats2 = share(part)
    part, errs, norm2, nhat2, e2, bout, u, mine2, theirs2 = call(
        second_kernel,
        [
            (HB, table), (HB, row), (HB, rows4), (HB, sds((10 * LINE, C))), (HB, sds((10 * LINE, C))), (HB, lines), (HB, lines), (HB, half), (HB, half),
        ],
        [
            (HB, v)
            for v in (stats2, norm2_gain, norm2_shift, bias2, sign, h1, w2, kernel2, fx, tx, order)
        ],
        [
            pltpu.VMEM((14 * LINE, 3 * C), BF16), pltpu.VMEM((12 * LINE, 3 * C), BF16),
            pltpu.VMEM((3, 3 * C, C), BF16), pltpu.VMEM(full.shape, BF16),
            pltpu.VMEM((12 * LINE, C), BF16), pltpu.VMEM((12 * LINE, C), BF16), pltpu.VMEM((C, C), BF16),
            pltpu.VMEM((ROWS * LINE, C), BF16), pltpu.VMEM((ROWS * LINE, C), BF16),
            pltpu.VMEM((C, LANES // 2), BF16), pltpu.VMEM((C, LANES // 2), BF16),
            pltpu.VMEM((14 * LINE, C), F32), pltpu.VMEM((10 * LINE, C), F32), pltpu.VMEM((3, C, 3 * C), BF16),
            tbl, pltpu.VMEM((1, 128), F32), pltpu.VMEM((4, C), F32), pltpu.VMEM((10 * LINE, C), F32),
            tbl, *[pltpu.VMEM((C,), F32)] * 4, DMA((20,)),
        ],
        30 * conv_flops,
    )
    sums2 = share(part)
    got2 = swap(theirs2)
    block_out, *strips = call(
        early_kernel,
        [(VM, sds((cells, C), BF16))] + [(VM, sds((80, LANES // 2), BF16))] * 4,
        [(VM, mine2), (VM, got2), (VM, bout)],
        [pltpu.VMEM((ROWS * LINE, C), F32)],
    )
    block_out = block_out.reshape(2, ROWS, COLS, C)
    strips = [strips[0]] + [shift(strips[k], "y", k) for k in (2, 1, 3)]
    sums2, strips[0] = lax.optimization_barrier((sums2, strips[0]))
    part, mine1, theirs1, e1 = call(
        third_kernel,
        [(HB, sds((2, 128))), (HB, half), (HB, half), (HB, sds((ROWS * LINE, C)))],
        [
            (HB, v)
            for v in (
                norm2, sums2, norm1, norm1_gain, norm1_shift, errs, e2, nhat2, taps1, order, fx, kernel1,
            )
        ],
        [
            pltpu.VMEM((2, 128), F32), pltpu.VMEM((4, C), F32), tbl, pltpu.VMEM((4, C), F32),
            *[pltpu.VMEM((C,), F32)] * 2, pltpu.VMEM((1, 128), F32),
            pltpu.VMEM((10 * LINE, C), F32), pltpu.VMEM((10 * LINE, C), F32),
            pltpu.VMEM((10 * LINE, 3 * C), BF16), pltpu.VMEM((C, C), BF16),
            pltpu.VMEM((ROWS * LINE, C), BF16), pltpu.VMEM(full.shape, BF16),
            pltpu.VMEM(half.shape, BF16), pltpu.VMEM(half.shape, BF16), pltpu.VMEM((ROWS * LINE, C), F32),
            pltpu.VMEM((3, C, 3 * C), BF16),
            pltpu.VMEM((10 * LINE, 3 * C), BF16), DMA((16,)),
        ],
        16 * conv_flops,
    )
    theirs1, *strips = lax.optimization_barrier((theirs1, *strips))
    got1, other = swap(theirs1), swap(part)
    parts = call(
        middle_kernel,
        [(VM, sds((240, 128), BF16))] * 4,
        [(VM, v) for v in strips],
        [pltpu.VMEM((80, LANES // 2), F32)],
    )
    parts = list(parts)
    got1, parts[0] = lax.optimization_barrier((got1, parts[0]))
    plane = call(
        late_kernel,
        [(VM, sds((16, 256, 128), BF16))],
        [(VM, mine1), (VM, got1), (VM, part), (VM, other)],
    )
    plane, *parts = lax.optimization_barrier((plane, *parts))
    plane = lax.all_to_all(plane, ("y", "x"), 0, 0, tiled=True)
    parts = [parts[0]] + [shift(parts[k], "x", k) for k in (2, 1, 3)]
    depth = call(
        plane_kernel,
        [(VM, sds((8, 80, 128), BF16))],
        [(VM, plane)] + [(VM, v) for v in parts] + [(VM, move)],
    )
    depth = lax.all_to_all(depth, ("z",), 0, 0, tiled=True)
    copies, sums1, info, loss = call(
        depth_kernel,
        [(VM, sds((8, 64, 128), BF16)), (VM, row), (VM, row), (VM, sds((1, 1)))],
        [(VM, depth), (VM, sign), (VM, ref_error)],
    )
    whole = lax.all_to_all(copies, ("c", "x"), 0, 0, tiled=True)
    grad = call(
        last_kernel,
        [(VM, sds((cells, C), BF16))],
        [(VM, sums1), (VM, info), (VM, norm1), (VM, e1), (VM, fx), (VM, u)],
        [pltpu.VMEM((ROWS * LINE, C), F32)],
    )
    feature_grad = grad.reshape(2, ROWS, COLS, C)
    whole = whole[:, :60].reshape(2, 4, 2, 3, 10, 128).transpose(2, 0, 1, 3, 5, 4).reshape(2, LANES, 10)
    whole = whole[:, :TAPS].astype(F32).reshape(2, 3, 3, C, 10)
    loss = loss.reshape(())
    return (block_out, feature_grad, whole[1], whole[0], loss)


def solution(mesh):
    fine = Mesh(mesh.devices.reshape(4, 2, 8, 4), AXES)
    cells = P(None, ("x", "c"), ("z", "y"), None)
    kernels = P(None, None, None, ("z", "y"))
    return jax.shard_map(
        body,
        mesh=fine,
        in_specs=(cells, cells) + (P(),) * 13,
        out_specs=(cells, cells, kernels, kernels, P()),
        check_vma=False,
    )
```
